128 devices in a mesh: dp: 16 (over z, x), seq: 8 (over y, core).
Axes of the slice: x: 4, y: 4, z: 4, core: 2. Of those that a mesh axis runs over, the one named last changes fastest.
Arguments:
- inputs: bfloat16 [16, 1024, 1536], P('dp', 'seq'), may hold values from -6 to 6
- cotangent: bfloat16 [16, 1024, 1536], P('dp', 'seq'), may hold values from -6 to 6
- resets: int32 [16], P('dp'), may hold values 0 or 1
- start_state: float32 [16, 2048], P('dp'), may hold values from -6 to 6
- conv_history: bfloat16 [16, 3, 2048], P('dp'), may hold values from -6 to 6
- norm_gain: bfloat16 [1536], P(('dp', 'seq')), may hold values from 0.5 to 1.5
- proj_x: bfloat16 [1536, 2048], P(('dp', 'seq')), may hold values from -0.15625 to 0.15625
- proj_y: bfloat16 [1536, 2048], P(('dp', 'seq')), may hold values from -0.15625 to 0.15625
- conv_taps: bfloat16 [2048, 4], P(('dp', 'seq')), may hold values from -3 to 3
- conv_bias: bfloat16 [2048], P(('dp', 'seq')), may hold values from -3 to 3
- gate_weight: bfloat16 [2048, 256], P(('dp', 'seq')), may hold values from -0.5 to 0.5
- gate_bias: bfloat16 [2048, 2], P(('dp', 'seq')), may hold values from -4 to 4
- decay_param: bfloat16 [2048], P(('dp', 'seq')), may hold values from -11 to -4
- proj_out: bfloat16 [2048, 1536], P(('dp', 'seq')), may hold values from -0.375 to 0.375
- mlp_gain: bfloat16 [1536], P(('dp', 'seq')), may hold values from 0.5 to 1.5
- mlp_gate: bfloat16 [1536, 4608], P(('dp', 'seq')), may hold values from -0.15625 to 0.15625
- mlp_up: bfloat16 [1536, 4608], P(('dp', 'seq')), may hold values from -0.15625 to 0.15625
- mlp_down: bfloat16 [4608, 1536], P(('dp', 'seq')), may hold values from -0.125 to 0.125
Outputs:
- layer_out: bfloat16 [16, 1024, 1536], P('dp', 'seq')
- input_grad: bfloat16 [16, 1024, 1536], P('dp', 'seq')
- grad_norm_gain: float32 [1536], P(('dp', 'seq'))
- grad_proj_x: float32 [1536, 2048], P(('dp', 'seq'))
- grad_proj_y: float32 [1536, 2048], P(('dp', 'seq'))
- grad_conv_taps: float32 [2048, 4], P(('dp', 'seq'))
- grad_conv_bias: float32 [2048], P(('dp', 'seq'))
- grad_gate_weight: float32 [2048, 256], P(('dp', 'seq'))
- grad_gate_bias: float32 [2048, 2], P(('dp', 'seq'))
- grad_decay_param: float32 [2048], P(('dp', 'seq'))
- grad_proj_out: float32 [2048, 1536], P(('dp', 'seq'))
- grad_mlp_gain: float32 [1536], P(('dp', 'seq'))
- grad_mlp_gate: float32 [1536, 4608], P(('dp', 'seq'))
- grad_mlp_up: float32 [1536, 4608], P(('dp', 'seq'))
- grad_mlp_down: float32 [4608, 1536], P(('dp', 'seq'))
The draws below stay inside these ranges and needn't reach their ends.
All inputs are finite; a program needn't handle non-finite values. No bound on the sum of `resets` on one device may be relied on, other than what follows from the above.
Results may differ from the reference program's by a relative error of at most 0.025.
Values may be sent and summed in bfloat16 or wider, within the bound.
No kernel may reach another device: no remote copies, remote signals or barrier semaphores. Data moves between devices by JAX's collectives and lax.ppermute only.
A program may use at most 320 MiB of HBM per device.

```python
import jax
import jax.numpy as jnp
from jax import lax

D = 1536
R = 2048
BLOCKS = 16
BW = 128
FF = 4608
CONV_W = 4
LENGTH = 1024
SEQS = 16


def draw_decay_param(key, part):
    key = jax.random.fold_in(key, 7)
    values = jax.random.uniform(key, (R,), jnp.float32, -10.0, -4.0)
    return values.astype(jnp.bfloat16)


def with_ends(values, own_key, smallest, top_value):
    index_at = [jax.random.randint(jax.random.fold_in(own_key, axis), (), 0, length) for axis, length in enumerate(values.shape)]
    widest = values.shape.index(max(values.shape))
    beside = index_at[:widest] + [(index_at[widest] + 1) % values.shape[widest]] + index_at[widest + 1:]
    return values.at[tuple(index_at)].set(smallest).at[tuple(beside)].set(top_value)


def shard_levels(key, dims, split, smallest, high):
    def one(axis_at, blocks):
        draws = jax.random.uniform(jax.random.fold_in(jax.random.fold_in(key, 6), axis_at), (blocks,), jnp.float32, smallest / len(split), high / len(split))
        return jnp.repeat(jnp.exp(draws), dims[axis_at] // blocks).reshape((-1,) + (1,) * (len(dims) - axis_at - 1))

    loudness = one(*split[0])
    for cut in split[1:]:
        loudness = loudness * one(*cut)
    return loudness


def centred(own_key, dims, scale, limit, cuts=(), held_as=jnp.bfloat16):
    entries = jax.random.normal(own_key, dims, jnp.float32) * scale
    if len(cuts) > 0:
        entries = shard_levels(own_key, dims, cuts, -0.22, 0.18) * entries
    return jnp.clip(entries, min=-limit, max=limit).astype(held_as)


def setup_inputs(seed: int = 0) -> dict:
    streams_of = jax.random.split(jax.random.key(seed), 19)
    return {
        "inputs": centred(streams_of[0], (SEQS, LENGTH, D), 1.0, 6.0, ((0, 16), (1, 8))),
        "cotangent": centred(streams_of[1], (SEQS, LENGTH, D), 1.0, 6.0, ((0, 16), (1, 8))),
        "resets": with_ends((jax.random.randint(streams_of[2], (SEQS,), 0, 2) < 1).astype(jnp.int32), jax.random.fold_in(streams_of[2], 1), 0, 1),
        "start_state": centred(streams_of[3], (SEQS, R), 1.0, 6.0, ((0, 16),), jnp.float32),
        "conv_history": centred(streams_of[4], (SEQS, CONV_W - 1, R), 1.0, 6.0, ((0, 16),)),
        "norm_gain": jnp.clip(1.0 + 0.1 * jax.random.normal(streams_of[5], (D,), jnp.float32), 0.5, 1.5).astype(jnp.bfloat16),
        "proj_x": centred(streams_of[6], (D, R), D ** -0.5, 0.15625, ((0, 128),)),
        "proj_y": centred(streams_of[7], (D, R), D ** -0.5, 0.15625, ((0, 128),)),
        "conv_taps": centred(streams_of[8], (R, CONV_W), CONV_W ** -0.5, 3.0, ((0, 128),)),
        "conv_bias": centred(streams_of[9], (R,), 0.5, 3.0, ((0, 128),)),
        "gate_weight": centred(streams_of[10], (R, 2 * BW), BW ** -0.5, 0.5, ((0, 128),)),
        "gate_bias": centred(streams_of[11], (R, 2), 1.0, 4.0, ((0, 128),)),
        "decay_param": draw_decay_param(jax.random.fold_in(streams_of[18], 71), 0),
        "proj_out": centred(streams_of[13], (R, D), (R // 8) ** -0.5, 0.375, ((0, 128),)),
        "mlp_gain": jnp.clip(1.0 + 0.1 * jax.random.normal(streams_of[14], (D,), jnp.float32), 0.5, 1.5).astype(jnp.bfloat16),
        "mlp_gate": centred(streams_of[15], (D, FF), D ** -0.5, 0.15625, ((0, 128),)),
        "mlp_up": centred(streams_of[16], (D, FF), D ** -0.5, 0.15625, ((0, 128),)),
        "mlp_down": centred(streams_of[17], (FF, D), (FF // 2) ** -0.5, 0.125, ((0, 128),)),
    }


epsilon = 1e-06
highest = lax.Precision.HIGHEST

@jax.custom_vjp
def low(v):
    return lax.optimization_barrier(v.astype(jnp.bfloat16)).astype(jnp.float32)

@jax.custom_vjp
def low_back(v):
    return v

def low_keep(v):
    return (low(v), None)

def low_pass(kept, grad):
    return (grad,)

def back_keep(v):
    return (v, None)

def back_low(kept, grad):
    return (low(grad),)
low.defvjp(low_keep, low_pass)
low_back.defvjp(back_keep, back_low)

def matmul(left_op, right_op):
    return jnp.dot(left_op, right_op, precision=highest)

def gelu_tanh(values):
    return jax.nn.gelu(values, approximate=True)

def rms_scale(values, gain_row):
    return values * lax.rsqrt(lax.optimization_barrier(jnp.mean(values * values, axis=-1, keepdims=True)) + epsilon) * gain_row

def causal_conv(padded, conv_taps, bias_row):
    taps_count = conv_taps.shape[1]
    length = padded.shape[1] - taps_count + 1
    summed = bias_row
    for offset in range(taps_count):
        start_at = taps_count - 1 - offset
        summed = summed + conv_taps[:, offset] * padded[:, start_at:start_at + length]
    return summed

def recurrence_terms(gate_raw, gate_bias, conv_out, decay_param):
    blocks = gate_raw.shape[-2]
    block_width = gate_raw.shape[-1] // 2
    bias_blocks = jnp.concatenate([gate_bias[:, 0].reshape(blocks, block_width), gate_bias[:, 1].reshape(blocks, block_width)], axis=-1)
    gated = gate_raw + bias_blocks
    flat_shape = conv_out.shape
    recur_gate = jax.nn.sigmoid(gated[..., :block_width].reshape(flat_shape))
    opening = jax.nn.sigmoid(gated[..., block_width:].reshape(flat_shape))
    log_decay = -8.0 * jax.nn.softplus(decay_param) * recur_gate
    return (jnp.exp(log_decay), jnp.sqrt(-jnp.expm1(2.0 * log_decay)) * opening * conv_out)

def linear_chain(mult_rows, add_rows, initial):

    def advance(carried, factors):
        carried = factors[0] * carried + factors[1]
        return (carried, carried)
    last_state, states = lax.scan(jax.checkpoint(advance), initial, (jnp.swapaxes(mult_rows, 0, 1), jnp.swapaxes(add_rows, 0, 1)))
    return jnp.swapaxes(states, 0, 1)

def layer_forward(inputs, weights, history, initial):
    norm_gain, proj_x, proj_y, conv_taps, conv_bias, gate_weight, gate_bias, decay_param, proj_out, mlp_gain, mlp_gate, mlp_up, mlp_down = weights
    normed = low(rms_scale(inputs, norm_gain))
    y_pre = low_back(matmul(normed, proj_y))
    y_act = gelu_tanh(y_pre)
    x_lin = low(low_back(matmul(normed, proj_x)))
    padded = jnp.concatenate([history, x_lin], axis=1)
    conv_out = low(causal_conv(padded, conv_taps, conv_bias))
    group_count, length, channels = conv_out.shape
    block_width = channels // BLOCKS
    gate_raw = low_back(jnp.einsum('gthi,hio->gtho', conv_out.reshape(group_count, length, BLOCKS, block_width), gate_weight.reshape(BLOCKS, block_width, 2 * block_width), precision=highest))
    decays, pushes = recurrence_terms(gate_raw, gate_bias, conv_out, decay_param)
    hidden = linear_chain(decays, pushes, initial)
    mixed_out = low(hidden * y_act)
    residual = inputs + low_back(matmul(mixed_out, proj_out))
    normed_two = low(rms_scale(residual, mlp_gain))
    gate_pre = low_back(matmul(normed_two, mlp_gate))
    up_pre = low_back(matmul(normed_two, mlp_up))
    product = low(gelu_tanh(gate_pre) * up_pre)
    return residual + matmul(product, mlp_down)

def reference(inputs, cotangent, resets, start_state, conv_history, norm_gain, proj_x, proj_y, conv_taps, conv_bias, gate_weight, gate_bias, decay_param, proj_out, mlp_gain, mlp_gate, mlp_up, mlp_down):
    weights = tuple((weight_arg.astype(jnp.float32) for weight_arg in (norm_gain, proj_x, proj_y, conv_taps, conv_bias, gate_weight, gate_bias, decay_param, proj_out, mlp_gain, mlp_gate, mlp_up, mlp_down)))
    keep_flag = (1 - resets).astype(jnp.float32)
    initial = start_state.astype(jnp.float32) * keep_flag[:, None]
    history = conv_history.astype(jnp.float32) * keep_flag[:, None, None]
    group_size = 4 if SEQS % 4 == 0 else 1

    def grouped(values):
        return values.reshape((SEQS // group_size, group_size) + values.shape[1:])

    def accumulate(totals, pieces):
        seq_inputs, seq_cot, seq_history, seq_initial = pieces

        def forward(layer_in, layer_weights):
            return layer_forward(layer_in, layer_weights, seq_history, seq_initial)
        result, pullback = jax.vjp(forward, seq_inputs, weights)
        in_grad, weight_grads = pullback(seq_cot)
        totals = jax.tree.map(lambda total_part, grad_part: total_part + grad_part, totals, weight_grads)
        return (totals, (result.astype(jnp.bfloat16), in_grad.astype(jnp.bfloat16)))
    zeros_start = tuple((jnp.zeros_like(weight_arg) for weight_arg in weights))
    totals, (outputs, in_grads) = lax.scan(accumulate, zeros_start, (grouped(inputs.astype(jnp.float32)), grouped(cotangent.astype(jnp.float32)), grouped(history), grouped(initial)))
    layer_out = outputs.reshape(SEQS, LENGTH, D)
    input_grad = in_grads.reshape(SEQS, LENGTH, D)
    return (layer_out, input_grad, totals[0], totals[1], totals[2], totals[3], totals[4], totals[5], totals[6], totals[7], totals[8], totals[9], totals[10], totals[11], totals[12])
```

```python
import jax
import jax.numpy as jnp
from jax import lax
from jax.experimental import pallas as pl
from jax.experimental.pallas import tpu as pltpu
from jax.sharding import Mesh
from jax.sharding import PartitionSpec as P

BF = jnp.bfloat16
F32 = jnp.float32
EPS = 1e-06
GELU_C = 0.7978845608028654
GELU_K = 0.044715

TOKENS = 1024
BLOCK = 128
HALF = 64
WIDTH = 1536
CHAN = 256
HID = 576
HID_PAD = 640
GATED = 2 * HID
STEP = 256
REC_ROWS = 320
C_WIDTH = 1920
MLP_ROWS = 480
MLP_LANES = 384

DP = ("z", "x")
SEQ = ("y", "c")
DP_SEQ = ("z", "x", "y", "c")

ANY = pl.BlockSpec(memory_space=pl.ANY)
VMEM = pl.BlockSpec(memory_space=pltpu.VMEM)
SMEM = pl.BlockSpec(memory_space=pltpu.SMEM)

PIECES = [
    (ry, rc, row)
    for rc in (0, 1)
    for ry, row in ((0, 0), (0, HALF), (1, 0), (1, HALF), (3, 0), (3, HALF), (2, 0), (2, HALF))
]


def hop(value, axis, distance):
    size = lax.axis_size(axis)
    return lax.ppermute(value, axis, [(i, (i - distance) % size) for i in range(size)])


def gather_rows(top, bottom):
    right_top, left_bottom = hop(top, "y", 1), hop(bottom, "y", 3)
    right_bottom, left_top = hop(bottom, "y", 1), hop(top, "y", 3)
    far_top, far_bottom = hop(right_top, "y", 1), hop(left_bottom, "y", 3)
    mine = [top, bottom, right_top, right_bottom, left_top, left_bottom, far_top, far_bottom]
    return mine + [hop(piece, "c", 1) for piece in mine]


def added(one, two):
    return (one.astype(F32) + two.astype(F32)).astype(BF)


def scatter_rows(own, other):
    chip = {r: added(own[r], hop(other[r], "c", 1)) for r in (2, 1, 3, 0)}
    to_right = hop(chip[2][:HALF], "y", 3)
    to_left = hop(chip[2][HALF:], "y", 1)
    left_bottom = hop(chip[1][HALF:], "y", 3)
    right_top = hop(chip[3][:HALF], "y", 1)
    left_top = hop(added(chip[1][:HALF], to_right), "y", 3)
    right_bottom = hop(added(chip[3][HALF:], to_left), "y", 1)
    return chip[0], left_top, left_bottom, right_top, right_bottom


def transposed_devices(value, back):
    pairs = [(16 * s + d, 8 * d + s) for s in range(8) for d in range(16)]
    return lax.ppermute(value, DP_SEQ, [(b, a) for a, b in pairs] if back else pairs)


def gather_dp(first, second):
    first = jnp.concatenate([first] + [hop(first, "x", r) for r in (1, 2, 3)])
    second = jnp.concatenate([second] + [hop(second, "z", r) for r in (1, 2, 3)])
    return (
        [first] + [hop(first, "z", r) for r in (1, 2, 3)],
        [second] + [hop(second, "x", r) for r in (1, 2, 3)],
    )


def scatter_dp(first, second):
    def total(parts):
        out = parts[0].astype(F32)
        for part in parts[1:]:
            out = out + part.astype(F32)
        return out

    got_first = [hop(first[r], "z", 4 - r) for r in (1, 2, 3)]
    got_second = [hop(second[r], "x", 4 - r) for r in (1, 2, 3)]
    first = total([first[0]] + got_first).astype(BF).reshape(4, REC_ROWS, 128)
    second = total([second[0]] + got_second).astype(BF).reshape(4, REC_ROWS, 128)
    return (
        total([first[0]] + [hop(first[r], "x", 4 - r) for r in (1, 2, 3)]),
        total([second[0]] + [hop(second[r], "z", 4 - r) for r in (1, 2, 3)]),
    )


def nn(a, b):
    return jnp.dot(a, b, preferred_element_type=F32)


def nt(a, b):
    return lax.dot_general(a, b, (((1,), (1,)), ((), ())), preferred_element_type=F32)


def tn(a, b):
    return lax.dot_general(a, b, (((0,), (0,)), ((), ())), preferred_element_type=F32)


def gelu_parts(v):
    sq = v * v
    t = jnp.tanh(GELU_C * v * (1.0 + GELU_K * sq))
    half = 0.5 * (1.0 + t)
    slope = half + 0.5 * v * (1.0 - t * t) * (GELU_C * (1.0 + 3.0 * GELU_K * sq))
    return v * half, slope


def neg_expm1(v):
    series = 1.0 + v * (1.0 / 7.0)
    for k in (6, 5, 4, 3, 2):
        series = 1.0 + v * (1.0 / k) * series
    return jnp.where(v > -0.35, -v * series, 1.0 - jnp.exp(v))


def softplus(v):
    e = jnp.exp(-jnp.abs(v))
    series = e * (1.0 - e * (1 / 2 - e * (1 / 3 - e * (1 / 4 - e * (1 / 5 - e * (1 / 6))))))
    return jnp.maximum(v, 0.0) + jnp.where(e < 0.05, series, jnp.log(1.0 + e))


def block_start(pos, ry, rc):
    return (lax.rem(pos[2] + ry, 4) * 2 + lax.rem(pos[3] + rc, 2)) * BLOCK


def dp_index(pos, rz, rx):
    return lax.rem(pos[0] + rz, 4) * 4 + lax.rem(pos[1] + rx, 4)


def start_in(pos, refs, scratch, sems):
    copies = []
    for k, (ref, (ry, rc, row)) in enumerate(zip(refs, PIECES)):
        at = pl.multiple_of(block_start(pos, ry, rc) + row, HALF)
        copies.append(pltpu.make_async_copy(ref, scratch.at[pl.ds(at, HALF), :], sems.at[k]))
        copies[-1].start()
    return copies


def start_out(pos, scratch, refs, sems):
    copies = []
    for k in range(8):
        at = pl.multiple_of(block_start(pos, k % 4, k // 4), BLOCK)
        copies.append(pltpu.make_async_copy(scratch.at[pl.ds(at, BLOCK), :], refs[k], sems.at[k]))
        copies[-1].start()
    return copies


def start_saves(pairs, sems, first):
    copies = []
    for k, (scratch, ref) in enumerate(pairs):
        copies.append(pltpu.make_async_copy(scratch, ref, sems.at[first + k]))
        copies[-1].start()
    return copies


def small_rows(c_ref):
    return c_ref[:, 1792:1920].astype(F32).T


def scan_chunks(step, carry):
    def four(k, carry):
        for j in range(4):
            carry = step(k * 4 + j, carry)
        return carry

    return lax.fori_loop(0, BLOCK // 4, four, carry)


def chunk_rows(t):
    return pl.ds(t, 8, stride=BLOCK)


def side(ref, lanes):
    rows = ref.shape[0] // 2
    return ref.at[lanes * rows : (lanes + 1) * rows, :]


def get_rows(ref, lo, count):
    return jnp.concatenate([side(ref, k)[lo : lo + count, :] for k in (0, 1)], axis=1)


def put_rows(ref, lo, count, value):
    for k in (0, 1):
        side(ref, k)[lo : lo + count, :] = value[:, 128 * k : 128 * k + 128]


def chain(mult_ref, ahead, add_ref, product_ref, backward):
    def step(t, carry):
        t = BLOCK - 1 - t if backward else t
        out = []
        for k in (0, 1):
            state, product = carry[2 * k : 2 * k + 2]
            mult = side(mult_ref, k)[chunk_rows(t + ahead), :]
            state = mult * state + side(add_ref, k)[chunk_rows(t), :]
            product = product * mult
            side(add_ref, k)[chunk_rows(t), :] = state
            side(product_ref, k)[chunk_rows(t), :] = product
            out += [state, product]
        return tuple(out)

    zero, one = jnp.zeros((8, 128), F32), jnp.ones((8, 128), F32)
    left, left_p, right, right_p = scan_chunks(step, (zero, one, zero, one))
    return jnp.concatenate([left, right], axis=1), jnp.concatenate([left_p, right_p], axis=1)


def rec_forward_kernel(
    pos, *refs
):
    x_refs, w_first, w_second, edge_ref = refs[:16], refs[16:20], refs[20:24], refs[24]
    outs = refs[25:33]
    (x_out, w_out, c_out, xl_out, yp_out, a_out, rg_out, op_out, hid_out, mix_out, rs_out) = refs[33:44]
    (x_s, w_s, c_s, xl_s, yp_s, a_s, rg_s, op_s, hid_s, mix_s, rs_s, push_s, cum_s, part_s, in_sems, out_sems) = refs[44:]
    loads = start_in(pos, x_refs, x_s, in_sems)
    for rz in range(4):
        for rx in range(4):
            place = dp_index(pos, rz, rx)
            rows = pl.ds(pl.multiple_of(place * 96, 32), 96)
            few = pl.ds(pl.multiple_of(place * 16, 16), 16)
            one, two = w_first[rz], w_second[rx]
            a, b = rx * REC_ROWS, rz * REC_ROWS
            w_s[rows, 0:128] = one[a : a + 96, :]
            w_s[rows, 128:256] = one[a + 96 : a + 192, :]
            w_s[rows, 256:384] = two[b : b + 96, :]
            w_s[rows, 384:512] = two[b + 96 : b + 192, :]
            for t in range(8):
                c_s[few, 128 * t : 128 * t + 128] = one[a + 192 + 16 * t : a + 208 + 16 * t, :]
            for t in range(7):
                c_s[few, 1024 + 128 * t : 1152 + 128 * t] = two[b + 192 + 16 * t : b + 208 + 16 * t, :]
    xl_s[0:8, :] = edge_ref[0:8, :]
    hid_s[0:8, :] = edge_ref[8:16, :]
    small = small_rows(c_s)
    for copy in loads:
        copy.wait()
    saves = start_saves(((x_s, x_out), (w_s, w_out), (c_s, c_out)), out_sems, 8)

    @pl.loop(0, TOKENS // STEP)
    def _(k):
        rows = pl.ds(pl.multiple_of(k * STEP, STEP), STEP)
        here = x_s[rows, :]
        wide = here.astype(F32)
        scale = lax.rsqrt(jnp.mean(wide * wide, axis=-1, keepdims=True) + EPS)
        both = nn(here, w_s[...]) * scale
        xl_s[pl.ds(pl.multiple_of(8 + k * STEP, 8), STEP), :] = both[:, :CHAN].astype(BF).astype(F32)
        yp_s[rows, :] = both[:, CHAN:]
        rs_s[rows, :] = jnp.broadcast_to(scale, (STEP, 128))

    saves += start_saves(((xl_s, xl_out), (yp_s, yp_out), (rs_s, rs_out)), out_sems, 11)
    gate_w = c_s[:, 1536:1792]
    decay_scale = -8.0 * softplus(small[7:8, :])
    for k in range(TOKENS // STEP):
        lo = k * STEP
        conv = small[4:5, :]
        for tap in range(4):
            conv = conv + small[tap : tap + 1, :] * xl_s[lo + 8 - tap : lo + 8 - tap + STEP, :]
        conv = conv.astype(BF)
        raw = [nn(conv[:, 128 * h : 128 * h + 128], gate_w[128 * h : 128 * h + 128, :]) for h in (0, 1)]
        rg = jax.nn.sigmoid(jnp.concatenate([raw[0][:, :128], raw[1][:, :128]], axis=1) + small[5:6, :])
        op = jax.nn.sigmoid(jnp.concatenate([raw[0][:, 128:], raw[1][:, 128:]], axis=1) + small[6:7, :])
        log_a = decay_scale * rg
        put_rows(a_s, lo, STEP, jnp.exp(log_a))
        put_rows(push_s, lo, STEP, jnp.sqrt(neg_expm1(2.0 * log_a)) * op * conv.astype(F32))
        rg_s[lo : lo + STEP, :] = rg
        op_s[lo : lo + STEP, :] = op
    put_rows(a_s, TOKENS, 8, jnp.zeros((8, CHAN), F32))
    saves += start_saves(((a_s, a_out), (rg_s, rg_out), (op_s, op_out)), out_sems, 14)

    state, product = chain(a_s, 0, push_s, cum_s, False)
    entering = edge_ref[15:16, :]
    for k in range(8):
        lo = k * BLOCK
        hidden = get_rows(push_s, lo, BLOCK) + get_rows(cum_s, lo, BLOCK) * entering
        entering = state[k : k + 1, :] + product[k : k + 1, :] * entering
        hid_s[8 + lo : 8 + lo + BLOCK, :] = hidden
        act, _ = gelu_parts(yp_s[lo : lo + BLOCK, :])
        mix_s[lo : lo + BLOCK, :] = (hidden * act).astype(BF)
    saves += start_saves(((hid_s, hid_out), (mix_s, mix_out)), out_sems, 17)

    @pl.loop(0, TOKENS // STEP)
    def _(k):
        rows = pl.ds(pl.multiple_of(k * STEP, STEP), STEP)
        part_s[rows, :] = nn(mix_s[rows, :], c_s[:, 0:WIDTH]).astype(BF)

    saves += start_out(pos, part_s, outs, out_sems)
    for copy in saves:
        copy.wait()


def mlp_unpack_kernel(all_ref, w_ref, d_ref, wide_s):
    for p in range(16):
        for j in range(3):
            at = p * MLP_ROWS + 96 * j
            w_ref[96 * p : 96 * p + 96, 384 * j : 384 * j + 384] = all_ref[at : at + 96, :]
        for j in range(4):
            at = p * MLP_ROWS + 288 + 48 * j
            wide_s[36 * p : 36 * p + 36, 384 * j : 384 * j + 384] = all_ref[at : at + 48, :].astype(F32)[:36]
    d_ref[0:HID, :] = wide_s[...].astype(BF)
    d_ref[HID:, :] = jnp.zeros((HID_PAD - HID, WIDTH), BF)


def mlp_kernel(pos, *refs):
    x_refs, c_refs, w_ref, d_ref = refs[:16], refs[16:32], refs[32], refs[33]
    outs = refs[34:42]
    x_out, c_out, prod_out, pre_out = refs[42:46]
    x_s, c_s, prod_s, pre_s, part_s, x_sems, c_sems, out_sems = refs[46:]
    loads = start_in(pos, x_refs, x_s, x_sems) + start_in(pos, c_refs, c_s, c_sems)
    for copy in loads:
        copy.wait()
    saves = start_saves(((x_s, x_out), (c_s, c_out)), out_sems, 8)

    @pl.loop(0, TOKENS // STEP)
    def _(k):
        rows = pl.ds(pl.multiple_of(k * STEP, STEP), STEP)
        pre = nn(x_s[rows, :], w_ref[...])
        d_product = nt(c_s[rows, :], d_ref[...])
        last = pre[:, 1024:1152]
        gate = jnp.concatenate([pre[:, :512], last], axis=1)
        up = jnp.concatenate([pre[:, 512:1024], pltpu.roll(last, 64, 1)], axis=1)
        act, slope = gelu_parts(gate)
        prod_s[rows, :] = (act * up).astype(BF)
        d_gate = d_product * up * slope
        d_up = d_product * act
        d_last = d_gate[:, 512:] + pltpu.roll(d_up[:, 512:], 64, 1)
        d_pre = jnp.concatenate([d_gate[:, :512], d_up[:, :512], d_last], axis=1).astype(BF)
        pre_s[rows, :] = d_pre
        part_s[rows, :] = nt(d_pre, w_ref[...]).astype(BF)

    saves += start_saves(((prod_s, prod_out), (pre_s, pre_out)), out_sems, 10)
    saves += start_out(pos, part_s, outs, out_sems)
    for copy in saves:
        copy.wait()


def mlp_out_kernel(pos, prod_ref, d_ref, *refs):
    outs, part_s, sems = refs[:8], refs[8], refs[9]

    @pl.loop(0, TOKENS // STEP)
    def _(k):
        rows = pl.ds(pl.multiple_of(k * STEP, STEP), STEP)
        part_s[rows, :] = nn(prod_ref[rows, :], d_ref[...]).astype(BF)

    for copy in start_out(pos, part_s, outs, sems):
        copy.wait()


def mlp_grads_kernel(x_ref, c_ref, prod_ref, pre_ref, out_ref, w_s, d_s):
    for k in range(WIDTH // STEP):
        w_s[STEP * k : STEP * k + STEP, :] = tn(x_ref[:, STEP * k : STEP * k + STEP], pre_ref[...]).astype(BF)
    for k in range(HID_PAD // 128):
        d_s[128 * k : 128 * k + 128, :] = tn(prod_ref[:, 128 * k : 128 * k + 128], c_ref[...])
    for p in range(16):
        for j in range(3):
            at = p * MLP_ROWS + 96 * j
            out_ref[at : at + 96, :] = w_s[96 * p : 96 * p + 96, 384 * j : 384 * j + 384]
        for j in range(4):
            at = p * MLP_ROWS + 288 + 48 * j
            out_ref[at : at + 48, :] = d_s[36 * p : 36 * p + 48, 384 * j : 384 * j + 384].astype(BF)


def rec_backward_kernel(pos, *refs):
    d_refs = refs[:16]
    x_ref, w_ref, c_ref, xl_ref, yp_ref, a_ref, rg_ref, op_ref, hid_ref, mix_ref, rs_ref = refs[16:27]
    outs, g_first, g_second = refs[27:35], refs[35:39], refs[39:43]
    (d_s, dh_s, cum_s, dc_s, dxy_s, part_s, acc_s, ga_s, gc_s, in_sems, out_sems) = refs[43:]
    for copy in start_in(pos, d_refs, d_s, in_sems):
        copy.wait()

    @pl.loop(0, TOKENS // STEP)
    def _(k):
        rows = pl.ds(pl.multiple_of(k * STEP, STEP), STEP)
        d_mixed = nt(d_s[rows, :], c_ref[:, 0:WIDTH])
        act, slope = gelu_parts(yp_ref[rows, :])
        hidden = hid_ref[pl.ds(pl.multiple_of(8 + k * STEP, 8), STEP), :]
        for h in (0, 1):
            side(dh_s, h)[rows, :] = (d_mixed * act)[:, 128 * h : 128 * h + 128]
        scale = rs_ref[rows, 0:1]
        dxy_s[rows, CHAN:] = (d_mixed * hidden * slope * scale).astype(BF)

    state, product = chain(a_ref, 1, dh_s, cum_s, True)
    small = small_rows(c_ref)
    gate_w = c_ref[:, 1536:1792]
    decay = small[7:8, :]
    decay_scale = -8.0 * softplus(decay)
    decay_slope = -8.0 * jax.nn.sigmoid(decay)
    acc_s[...] = jnp.zeros_like(acc_s)
    dc_s[TOKENS:, :] = jnp.zeros((8, CHAN), F32)
    later = [None] * 8
    entering = jnp.zeros((1, CHAN), F32)
    for k in reversed(range(8)):
        later[k] = entering
        entering = state[k : k + 1, :] + product[k : k + 1, :] * entering
    gate_grads = [jnp.zeros((128, CHAN), F32) for _ in (0, 1)]
    for k in range(8):
        lo = k * BLOCK
        rows = slice(lo, lo + BLOCK)
        state_grad = get_rows(dh_s, lo, BLOCK) + get_rows(cum_s, lo, BLOCK) * later[k]
        shifted = [xl_ref[lo + 8 - tap : lo + 8 - tap + BLOCK, :] for tap in range(4)]
        conv = small[4:5, :]
        for tap in range(4):
            conv = conv + small[tap : tap + 1, :] * shifted[tap]
        conv_low = conv.astype(BF)
        conv = conv_low.astype(F32)
        rg, op, a = rg_ref[rows, :], op_ref[rows, :], get_rows(a_ref, lo, BLOCK)
        root = jnp.sqrt(neg_expm1(2.0 * decay_scale * rg))
        pushed = state_grad * op
        d_log = a * (state_grad * hid_ref[lo + 7 : lo + 7 + BLOCK, :] - pushed * conv * a / root)
        d_rg = d_log * rg
        acc_s[7:8, :] += jnp.sum(d_rg, axis=0, keepdims=True) * decay_slope
        d_raw = decay_scale * d_rg * (1.0 - rg)
        d_open = pushed * root * conv * (1.0 - op)
        acc_s[5:6, :] += jnp.sum(d_raw, axis=0, keepdims=True)
        acc_s[6:7, :] += jnp.sum(d_open, axis=0, keepdims=True)
        d_raw, d_open = d_raw.astype(BF), d_open.astype(BF)
        back = []
        for h in (0, 1):
            cols = slice(128 * h, 128 * h + 128)
            d_block = jnp.concatenate([d_raw[:, cols], d_open[:, cols]], axis=1)
            gate_grads[h] = gate_grads[h] + tn(conv_low[:, cols], d_block)
            back.append(nt(d_block, gate_w[cols, :]))
        d_conv = pushed * root + jnp.concatenate(back, axis=1)
        dc_s[rows, :] = d_conv
        acc_s[4:5, :] += jnp.sum(d_conv, axis=0, keepdims=True)
        for tap in range(4):
            acc_s[tap : tap + 1, :] += jnp.sum(d_conv * shifted[tap], axis=0, keepdims=True)
    for k in range(8):
        lo = k * BLOCK
        d_x = small[0:1, :] * dc_s[lo : lo + BLOCK, :]
        for tap in range(1, 4):
            d_x = d_x + small[tap : tap + 1, :] * dc_s[lo + tap : lo + tap + BLOCK, :]
        dxy_s[lo : lo + BLOCK, 0:CHAN] = (d_x * rs_ref[lo : lo + BLOCK, 0:1]).astype(BF)

    @pl.loop(0, TOKENS // STEP)
    def _(k):
        rows = pl.ds(pl.multiple_of(k * STEP, STEP), STEP)
        part_s[rows, :] = nt(dxy_s[rows, :], w_ref[...]).astype(BF)

    saves = start_out(pos, part_s, outs, out_sems)
    for k in range(WIDTH // STEP):
        ga_s[STEP * k : STEP * k + STEP, :] = tn(x_ref[:, STEP * k : STEP * k + STEP], dxy_s[...]).astype(BF)
    gc_s[:, 0:WIDTH] = tn(mix_ref[...], d_s[...]).astype(BF)
    for h in (0, 1):
        gc_s[128 * h : 128 * h + 128, 1536:1792] = gate_grads[h].astype(BF)
    gc_s[:, 1792:1920] = acc_s[...].T.astype(BF)
    for rz in range(4):
        for rx in range(4):
            place = dp_index(pos, rz, rx)
            rows = pl.ds(pl.multiple_of(place * 96, 32), 96)
            few = pl.ds(pl.multiple_of(place * 16, 16), 16)
            one, two = g_first[rz], g_second[rx]
            a, b = rx * REC_ROWS, rz * REC_ROWS
            one[a : a + 96, :] = ga_s[rows, 0:128]
            one[a + 96 : a + 192, :] = ga_s[rows, 128:256]
            two[b : b + 96, :] = ga_s[rows, 256:384]
            two[b + 96 : b + 192, :] = ga_s[rows, 384:512]
            for t in range(8):
                one[a + 192 + 16 * t : a + 208 + 16 * t, :] = gc_s[few, 128 * t : 128 * t + 128]
            for t in range(7):
                two[b + 192 + 16 * t : b + 208 + 16 * t, :] = gc_s[few, 1024 + 128 * t : 1152 + 128 * t]
            two[b + 304 : b + 320, :] = jnp.zeros((16, 128), BF)
    for copy in saves:
        copy.wait()


def add_terms(terms, half):
    own, left_top, left_bottom, right_top, right_bottom = terms
    rest = (left_top, right_top) if half == 0 else (left_bottom, right_bottom)
    total = own[HALF * half : HALF * half + HALF, :].astype(F32)
    for term in rest:
        total = total + term[...].astype(F32)
    return total


def residual_kernel(x_ref, *refs):
    terms, (res_ref, scale_ref, top_ref, bottom_ref) = refs[:5], refs[5:]
    for half, low_ref in enumerate((top_ref, bottom_ref)):
        rows = slice(HALF * half, HALF * half + HALF)
        residual = x_ref[rows, :].astype(F32) + add_terms(terms, half)
        scale = lax.rsqrt(jnp.mean(residual * residual, axis=-1, keepdims=True) + EPS)
        res_ref[rows, :] = residual
        scale_ref[rows, :] = jnp.broadcast_to(scale, (HALF, 128))
        low_ref[...] = (residual * scale).astype(BF)


def d_residual_kernel(cot_ref, res_ref, scale_ref, *refs):
    terms, (d_ref, top_ref, bottom_ref) = refs[:5], refs[5:]
    for half, low_ref in enumerate((top_ref, bottom_ref)):
        rows = slice(HALF * half, HALF * half + HALF)
        d_normed = add_terms(terms, half)
        scale = scale_ref[rows, 0:1]
        normed = res_ref[rows, :] * scale
        along = jnp.mean(normed * d_normed, axis=-1, keepdims=True)
        d_residual = cot_ref[rows, :].astype(F32) + scale * (d_normed - normed * along)
        d_ref[rows, :] = d_residual
        low_ref[...] = d_residual.astype(BF)


def input_grad_kernel(x_ref, d_ref, *refs):
    terms, out_ref = refs[:5], refs[5]
    for half in (0, 1):
        rows = slice(HALF * half, HALF * half + HALF)
        scaled = add_terms(terms, half)
        x = x_ref[rows, :].astype(F32)
        power = 1.0 / (jnp.mean(x * x, axis=-1, keepdims=True) + EPS)
        along = jnp.mean(x * scaled, axis=-1, keepdims=True) * power
        out_ref[rows, :] = (d_ref[rows, :] + scaled - x * along).astype(BF)


def layer_out_kernel(res_ref, *refs):
    terms, out_ref = refs[:5], refs[5]
    for half in (0, 1):
        rows = slice(HALF * half, HALF * half + HALF)
        out_ref[rows, :] = (res_ref[rows, :] + add_terms(terms, half)).astype(BF)


def shape(dims, dtype):
    return jax.ShapeDtypeStruct(dims, dtype)


def call(kernel, name, args, in_specs, outs, out_specs, scratch=(), flops=0, vmem=48):
    return pl.pallas_call(
        kernel,
        name=name,
        in_specs=in_specs,
        out_specs=out_specs,
        out_shape=outs,
        scratch_shapes=scratch,
        cost_estimate=pl.CostEstimate(flops=flops, bytes_accessed=8 << 20, transcendentals=0),
        compiler_params=pltpu.CompilerParams(vmem_limit_bytes=vmem << 20),
    )(*args)


def simple(kernel, name, args, outs):
    return call(kernel, name, args, [VMEM] * len(args), outs, [VMEM] * len(outs), flops=1 << 30)


PART_OUTS = [shape((BLOCK, WIDTH), BF)] * 8
SEMS16 = pltpu.SemaphoreType.DMA((16,))


def rec_forward(pos, x_pieces, w_first, w_second, edges):
    saved = [
        ((TOKENS, WIDTH), BF),
        ((WIDTH, 2 * CHAN), BF),
        ((CHAN, C_WIDTH), BF),
        ((TOKENS + 8, CHAN), F32),
        ((TOKENS, CHAN), F32),
        ((2 * TOKENS + 16, 128), F32),
        ((TOKENS, CHAN), F32),
        ((TOKENS, CHAN), F32),
        ((TOKENS + 8, CHAN), F32),
        ((TOKENS, CHAN), BF),
        ((TOKENS, 128), F32),
    ]
    out = call(
        rec_forward_kernel,
        "rec_forward",
        (pos, *x_pieces, *w_first, *w_second, edges),
        [SMEM] + [ANY] * 16 + [VMEM] * 9,
        PART_OUTS + [shape(*s) for s in saved],
        [ANY] * 19,
        [pltpu.VMEM(*s) for s in saved]
        + [pltpu.VMEM((2 * TOKENS, 128), F32)] * 2
        + [pltpu.VMEM((TOKENS, WIDTH), BF), SEMS16, pltpu.SemaphoreType.DMA((19,))],
        flops=12 << 30,
    )
    return out[:4], out[4:8], out[8:]


def mlp_forward_backward(pos, x_pieces, c_pieces, w_up, w_down):
    saved = [
        ((TOKENS, WIDTH), BF),
        ((TOKENS, WIDTH), BF),
        ((TOKENS, HID_PAD), BF),
        ((TOKENS, GATED), BF),
    ]
    out = call(
        mlp_kernel,
        "mlp",
        (pos, *x_pieces, *c_pieces, w_up, w_down),
        [SMEM] + [ANY] * 32 + [VMEM] * 2,
        PART_OUTS + [shape(*s) for s in saved],
        [ANY] * 12,
        [pltpu.VMEM(*s) for s in saved]
        + [pltpu.VMEM((TOKENS, WIDTH), BF), SEMS16, SEMS16, pltpu.SemaphoreType.DMA((12,))],
        flops=12 << 30,
    )
    return out[:4], out[4:8], out[8:]


def rec_backward(pos, d_pieces, saved):
    rec = [shape((4 * REC_ROWS, 128), BF)] * 8
    out = call(
        rec_backward_kernel,
        "rec_backward",
        (pos, *d_pieces, *saved),
        [SMEM] + [ANY] * 16 + [VMEM] * 11,
        PART_OUTS + rec,
        [ANY] * 8 + [VMEM] * 8,
        [
            pltpu.VMEM((TOKENS, WIDTH), BF),
            pltpu.VMEM((2 * TOKENS, 128), F32),
            pltpu.VMEM((2 * TOKENS, 128), F32),
            pltpu.VMEM((TOKENS + 8, CHAN), F32),
            pltpu.VMEM((TOKENS, 2 * CHAN), BF),
            pltpu.VMEM((TOKENS, WIDTH), BF),
            pltpu.VMEM((128, CHAN), F32),
            pltpu.VMEM((WIDTH, 2 * CHAN), BF),
            pltpu.VMEM((CHAN, C_WIDTH), BF),
            SEMS16,
            pltpu.SemaphoreType.DMA((8,)),
        ],
        flops=16 << 30,
    )
    return out[:4], out[4:8], out[8:12], out[12:16]


def by_columns(scaled, width):
    return scaled.reshape(12, 8, width).transpose(1, 0, 2)


def exchanged(blocks):
    width = blocks.shape[-1]
    padded = jnp.pad(blocks, ((0, 0), (0, 4), (0, 0)))
    return lax.all_to_all(padded, SEQ, 0, 0, tiled=True)[:, :12].reshape(96, width)


def returned(rows):
    blocks = jnp.pad(rows.reshape(8, 12, -1), ((0, 0), (0, 4), (0, 0)))
    return lax.all_to_all(blocks, SEQ, 0, 0, tiled=True)[:, :12]


def row_tiles(array, lanes):
    return jnp.concatenate([array[:, k : k + lanes] for k in range(0, array.shape[1], lanes)])


def column_tiles(array, count):
    return jnp.concatenate(jnp.split(array, count), axis=1)


def per_device(
    inputs,
    cotangent,
    resets,
    start_state,
    conv_history,
    norm_gain,
    proj_x,
    proj_y,
    conv_taps,
    conv_bias,
    gate_weight,
    gate_bias,
    decay_param,
    proj_out,
    mlp_gain,
    mlp_gate,
    mlp_up,
    mlp_down,
):
    pos = jnp.stack([lax.axis_index(a) for a in DP_SEQ]).astype(jnp.int32)
    flat_in = inputs[0]
    flat_cot = cotangent[0]
    x_pieces = gather_rows(flat_in[:HALF], flat_in[HALF:])

    gain_one = norm_gain.astype(F32)[:, None]
    scaled_x = (proj_x.astype(F32) * gain_one).astype(BF)
    scaled_y = (proj_y.astype(F32) * gain_one).astype(BF)
    cols = exchanged(jnp.concatenate([by_columns(scaled_x, CHAN), by_columns(scaled_y, CHAN)], axis=2))
    fill = jnp.zeros((16, 120), BF)
    rest = jnp.concatenate(
        [proj_out, gate_weight, conv_taps, conv_bias[:, None], gate_bias, decay_param[:, None], fill], axis=1
    )
    rest = transposed_devices(rest, False)
    rec_first = jnp.concatenate([row_tiles(cols[:, :256], 128), row_tiles(rest[:, :1024], 128)])
    rec_second = jnp.concatenate(
        [row_tiles(cols[:, 256:], 128), row_tiles(rest[:, 1024:], 128), jnp.zeros((16, 128), BF)]
    )
    w_first, w_second = gather_dp(rec_first, rec_second)

    gain_two = mlp_gain.astype(F32)[:, None]
    scaled_gate = by_columns((mlp_gate.astype(F32) * gain_two).astype(BF), HID)
    scaled_up = by_columns((mlp_up.astype(F32) * gain_two).astype(BF), HID)
    mlp_cols = exchanged(
        jnp.concatenate(
            [scaled_gate[..., :512], scaled_up[..., :512], scaled_gate[..., 512:], scaled_up[..., 512:]], axis=2
        )
    )
    down = jnp.pad(transposed_devices(mlp_down, False), ((0, 12), (0, 0)))
    mlp_shard = jnp.concatenate([row_tiles(mlp_cols, MLP_LANES), row_tiles(down, MLP_LANES)])
    mlp_all = lax.all_gather(mlp_shard, DP, axis=0, tiled=True)
    w_up, w_down = call(
        mlp_unpack_kernel,
        "mlp_unpack",
        (mlp_all,),
        [VMEM],
        [shape((WIDTH, GATED), BF), shape((HID_PAD, WIDTH), BF)],
        [VMEM, VMEM],
        [pltpu.VMEM((HID, WIDTH), F32)],
        flops=1 << 30,
    )
    c_pieces = gather_rows(flat_cot[:HALF], flat_cot[HALF:])

    keep = (1 - resets).astype(F32)
    place = lax.axis_index(SEQ) * CHAN
    history = lax.dynamic_slice(conv_history[0].astype(F32), (0, place), (3, CHAN)) * keep
    initial = lax.dynamic_slice(start_state, (0, place), (1, CHAN)) * keep
    edges = jnp.concatenate([jnp.zeros((5, CHAN), F32), history, jnp.zeros((7, CHAN), F32), initial])
    own, other, saved = rec_forward(pos, x_pieces, w_first, w_second, edges)
    residual, scale_two, top, bottom = simple(
        residual_kernel,
        "residual",
        (flat_in, *scatter_rows(own, other)),
        [shape((BLOCK, WIDTH), F32), shape((BLOCK, 128), F32)] + [shape((HALF, WIDTH), BF)] * 2,
    )

    own, other, mlp_saved = mlp_forward_backward(pos, gather_rows(top, bottom), c_pieces, w_up, w_down)
    normed_all, cot_all, product, d_pre = mlp_saved
    d_residual, top, bottom = simple(
        d_residual_kernel,
        "d_residual",
        (flat_cot, residual, scale_two, *scatter_rows(own, other)),
        [shape((BLOCK, WIDTH), F32)] + [shape((HALF, WIDTH), BF)] * 2,
    )
    mlp_grads = call(
        mlp_grads_kernel,
        "mlp_grads",
        (normed_all, cot_all, product, d_pre),
        [VMEM] * 4,
        [shape((16 * MLP_ROWS, MLP_LANES), BF)],
        [VMEM],
        [pltpu.VMEM((WIDTH, GATED), BF), pltpu.VMEM((HID_PAD, WIDTH), F32)],
        flops=12 << 30,
    )[0]
    mlp_sum = lax.psum_scatter(mlp_grads, DP, scatter_dimension=0, tiled=True)
    out_parts = call(
        mlp_out_kernel,
        "mlp_out",
        (pos, product, w_down),
        [SMEM, VMEM, VMEM],
        PART_OUTS,
        [ANY] * 8,
        [pltpu.VMEM((TOKENS, WIDTH), BF), pltpu.SemaphoreType.DMA((8,))],
        flops=4 << 30,
    )

    own, other, g_first, g_second = rec_backward(pos, gather_rows(top, bottom), saved)
    input_grad = simple(
        input_grad_kernel,
        "input_grad",
        (flat_in, d_residual, *scatter_rows(own, other)),
        [shape((BLOCK, WIDTH), BF)],
    )[0]
    layer_out = simple(
        layer_out_kernel,
        "layer_out",
        (residual, *scatter_rows(out_parts[:4], out_parts[4:])),
        [shape((BLOCK, WIDTH), BF)],
    )[0]

    sum_first, sum_second = scatter_dp(g_first, g_second)
    cols = jnp.concatenate([column_tiles(sum_first[:192], 2), column_tiles(sum_second[:192], 2)], axis=1)
    rest = jnp.concatenate([column_tiles(sum_first[192:], 8), column_tiles(sum_second[192:304], 7)], axis=1)
    cols = returned(cols.astype(BF)).astype(F32)
    rest = transposed_devices(rest.astype(BF), True).astype(F32)
    grad_x = cols[..., :CHAN].transpose(1, 0, 2).reshape(12, -1)
    grad_y = cols[..., CHAN:].transpose(1, 0, 2).reshape(12, -1)
    grad_norm_gain = jnp.sum(grad_x * proj_x.astype(F32) + grad_y * proj_y.astype(F32), axis=1)

    mlp_cols = returned(column_tiles(mlp_sum[:288], 3)).astype(F32)
    grad_gate = jnp.concatenate([mlp_cols[..., :512], mlp_cols[..., 1024:1088]], axis=2)
    grad_up = jnp.concatenate([mlp_cols[..., 512:1024], mlp_cols[..., 1088:]], axis=2)
    grad_gate = grad_gate.transpose(1, 0, 2).reshape(12, -1)
    grad_up = grad_up.transpose(1, 0, 2).reshape(12, -1)
    grad_mlp_gain = jnp.sum(grad_gate * mlp_gate.astype(F32) + grad_up * mlp_up.astype(F32), axis=1)
    grad_down = transposed_devices(column_tiles(mlp_sum[288:], 4)[:36], True).astype(F32)
    return (
        layer_out[None],
        input_grad[None],
        grad_norm_gain,
        grad_x * gain_one,
        grad_y * gain_one,
        rest[:, 1792:1796],
        rest[:, 1796],
        rest[:, 1536:1792],
        rest[:, 1797:1799],
        rest[:, 1799],
        rest[:, :1536],
        grad_mlp_gain,
        grad_gate * gain_two,
        grad_up * gain_two,
        grad_down,
    )


def solution(mesh):
    finer = Mesh(mesh.devices.reshape(4, 4, 4, 2), DP_SEQ)
    rows = P(DP_SEQ, None)
    line = P(DP_SEQ)
    tokens = P(DP, SEQ, None)
    in_specs = (
        tokens,
        tokens,
        P(DP),
        P(DP, None),
        P(DP, None, None),
        line,
        rows,
        rows,
        rows,
        line,
        rows,
        rows,
        line,
        rows,
        line,
        rows,
        rows,
        rows,
    )
    out_specs = (
        tokens,
        tokens,
        line,
        rows,
        rows,
        rows,
        line,
        rows,
        rows,
        line,
        rows,
        line,
        rows,
        rows,
        rows,
    )
    return jax.shard_map(per_device, mesh=finer, in_specs=in_specs, out_specs=out_specs, check_vma=False)
```

```python
import jax
import jax.numpy as jnp
from jax import lax
from jax.experimental import pallas as pl
from jax.experimental.pallas import tpu as pltpu
from jax.sharding import Mesh
from jax.sharding import PartitionSpec as P

BF = jnp.bfloat16
F32 = jnp.float32
EPS = 1e-06
GELU_C = 0.7978845608028654
GELU_K = 0.044715

TOKENS = 1024
ROWS = 512
BLOCK = 128
WIDTH = 1536
CHAN = 256
HID = 576
HID_PAD = 640
GATED = 2 * HID
STEP = 256
C_WIDTH = 1920
SENT = 2 * CHAN + GATED
SMALL = 384
EARLY = 240
COLS = 384
LATE = 1248
DOWN_ROWS = 192
COLS_ROWS = 48
SUM_ROWS = 80
REST = 256
MLP_ROWS = 480
MLP_LANES = 384

DP = ("z", "x")
SEQ = ("y", "c")
DP_SEQ = ("z", "x", "y", "c")

ANY = pl.BlockSpec(memory_space=pl.ANY)
VMEM = pl.BlockSpec(memory_space=pltpu.VMEM)
SMEM = pl.BlockSpec(memory_space=pltpu.SMEM)

PIECES = (0, 1, 3, 2)
PLACES = [(ry, rc) for rc in (0, 1) for ry in (0, 2, 1, 3)]


def hop(value, axis, distance):
    size = lax.axis_size(axis)
    return lax.ppermute(value, axis, [(i, (i - distance) % size) for i in range(size)])


def added(one, two):
    return (one.astype(F32) + two.astype(F32)).astype(BF)


def swapped(value):
    return hop(value, "c", 1)


def gather_rows(block):
    return [block] + [hop(block, "y", r) for r in PIECES[1:]]


def scatter_rows(parts):
    return [parts[0]] + [hop(parts[r], "y", 4 - r) for r in (2, 1, 3)]


def tied(*values):
    return lax.optimization_barrier(values)


def transposed_devices(value, back):
    pairs = [(16 * s + d, 8 * d + s) for s in range(8) for d in range(16)]
    return lax.ppermute(value, DP_SEQ, [(b, a) for a, b in pairs] if back else pairs)


def exchanged(blocks):
    out = []
    for (ry, rc), block in zip(PLACES, blocks):
        route = [(2 * y + c, 2 * ((y + ry) % 4) + (c + rc) % 2) for y in range(4) for c in range(2)]
        out.append(lax.ppermute(block, SEQ, route) if (ry, rc) != (0, 0) else block)
    return out


def nn(a, b):
    return jnp.dot(a, b, preferred_element_type=F32)


def nt(a, b):
    return lax.dot_general(a, b, (((1,), (1,)), ((), ())), preferred_element_type=F32)


def tn(a, b):
    return lax.dot_general(a, b, (((0,), (0,)), ((), ())), preferred_element_type=F32)


def gelu_parts(v):
    sq = v * v
    t = jnp.tanh(GELU_C * v * (1.0 + GELU_K * sq))
    half = 0.5 * (1.0 + t)
    slope = half + 0.5 * v * (1.0 - t * t) * (GELU_C * (1.0 + 3.0 * GELU_K * sq))
    return v * half, slope


def neg_expm1(v):
    series = 1.0 + v * (1.0 / 7.0)
    for k in (6, 5, 4, 3, 2):
        series = 1.0 + v * (1.0 / k) * series
    return jnp.where(v > -0.35, -v * series, 1.0 - jnp.exp(v))


def softplus(v):
    e = jnp.exp(-jnp.abs(v))
    series = e * (1.0 - e * (1 / 2 - e * (1 / 3 - e * (1 / 4 - e * (1 / 5 - e * (1 / 6))))))
    return jnp.maximum(v, 0.0) + jnp.where(e < 0.05, series, jnp.log(1.0 + e))


def column(row_ref):
    n = row_ref.shape[1]
    square = jnp.broadcast_to(row_ref[...].astype(F32), (n, n))
    same = lax.broadcasted_iota(jnp.int32, (n, n), 0) == lax.broadcasted_iota(jnp.int32, (n, n), 1)
    return jnp.sum(jnp.where(same, square, 0.0), axis=1, keepdims=True)


def as_row(col):
    n = col.shape[0]
    square = jnp.broadcast_to(col, (n, n))
    same = lax.broadcasted_iota(jnp.int32, (n, n), 0) == lax.broadcasted_iota(jnp.int32, (n, n), 1)
    return jnp.sum(jnp.where(same, square, 0.0), axis=0, keepdims=True)


def place_of(pos, ry, rc):
    return lax.rem(pos[2] + ry, 4) * 2 + lax.rem(pos[3] + rc, 2)


def block_rows(pos, ry):
    return pl.ds(pl.multiple_of(lax.rem(pos[2] + ry, 4) * BLOCK, BLOCK), BLOCK)


def time_start(pos, y, rc):
    return (2 * y + lax.rem(pos[3] + rc, 2)) * BLOCK


def start_loads(pairs, sems, first):
    copies = []
    for k, (ref, scratch) in enumerate(pairs):
        copies.append(pltpu.make_async_copy(ref, scratch, sems.at[first + k]))
        copies[-1].start()
    return copies


def start_in(pos, refs, scratch, sems, first=0):
    return start_loads([(ref, scratch.at[block_rows(pos, ry), :]) for ref, ry in zip(refs, PIECES)], sems, first)


def start_out(pos, scratch, refs, sems, first=0):
    return start_loads([(scratch.at[block_rows(pos, r), :], refs[r]) for r in range(4)], sems, first)


def wait_all(copies):
    for copy in copies:
        copy.wait()


def small_rows(c_ref):
    return c_ref[:, CHAN:SMALL].astype(F32).T


def scan_chunks(step, carry):
    def four(k, carry):
        for j in range(4):
            carry = step(k * 4 + j, carry)
        return carry

    return lax.fori_loop(0, BLOCK // 4, four, carry)


def chunk_rows(t):
    return pl.ds(t, 8, stride=BLOCK)


def side(ref, lanes):
    rows = ref.shape[0] // 2
    return ref.at[lanes * rows : (lanes + 1) * rows, :]


def get_rows(ref, lo, count):
    return jnp.concatenate([side(ref, k)[lo : lo + count, :] for k in (0, 1)], axis=1)


def put_rows(ref, lo, count, value):
    for k in (0, 1):
        side(ref, k)[lo : lo + count, :] = value[:, 128 * k : 128 * k + 128]


def chain(mult_ref, ahead, add_ref, product_ref, backward):
    def step(t, carry):
        t = BLOCK - 1 - t if backward else t
        out = []
        for k in (0, 1):
            state, product = carry[2 * k : 2 * k + 2]
            mult = side(mult_ref, k)[chunk_rows(t + ahead), :]
            state = mult * state + side(add_ref, k)[chunk_rows(t), :]
            product = product * mult
            side(add_ref, k)[chunk_rows(t), :] = state
            side(product_ref, k)[chunk_rows(t), :] = product
            out += [state, product]
        return tuple(out)

    zero, one = jnp.zeros((8, 128), F32), jnp.ones((8, 128), F32)
    left, left_p, right, right_p = scan_chunks(step, (zero, one, zero, one))
    return jnp.concatenate([left, right], axis=1), jnp.concatenate([left_p, right_p], axis=1)


def gated_cols(gate, up, s):
    lo = HID * s
    return [gate[:, lo : lo + 512], up[:, lo : lo + 512], gate[:, lo + 512 : lo + HID], up[:, lo + 512 : lo + HID]]


def pack_cols_kernel(pos, gain_one, gain_two, x_ref, y_ref, gate_ref, up_ref, *refs):
    outs, blocks_s = refs[:8], refs[8]
    gain = column(gain_one)
    x, y = x_ref[...].astype(F32) * gain, y_ref[...].astype(F32) * gain
    gain = column(gain_two)
    gate, up = gate_ref[...].astype(F32) * gain, up_ref[...].astype(F32) * gain
    fill = jnp.zeros((4, SENT), F32)
    for s in range(8):
        cols = slice(CHAN * s, CHAN * s + CHAN)
        block = jnp.concatenate([x[:, cols], y[:, cols], *gated_cols(gate, up, s)], axis=1)
        blocks_s[s] = jnp.concatenate([block, fill])
    for k, (ry, rc) in enumerate(PLACES):
        outs[k][...] = blocks_s[place_of(pos, ry, rc)].astype(BF)


def pack_rows_kernel(out_ref, gate_w_ref, taps_ref, bias_ref, gate_bias_ref, decay_ref, rest_ref):
    rest_ref[:, 0:WIDTH] = out_ref[...]
    rest_ref[:, 1536:1792] = gate_w_ref[...]
    lane = lax.broadcasted_iota(jnp.int32, (16, 128), 1)
    small = jnp.zeros((16, 128), F32)
    for k in range(4):
        small = jnp.where(lane == k, column(taps_ref.at[k : k + 1, :]), small)
    small = jnp.where(lane == 4, column(bias_ref), small)
    for k in range(2):
        small = jnp.where(lane == 5 + k, column(gate_bias_ref.at[k : k + 1, :]), small)
    rest_ref[:, 1792:1920] = jnp.where(lane == 7, column(decay_ref), small).astype(BF)


def shard_kernel(pos, *refs):
    blocks, (rest_ref, early_ref, late_ref, blocks_s, wide_s) = refs[:8], refs[8:]
    for k, (ry, rc) in enumerate(PLACES):
        blocks_s[place_of(pos, 4 - ry, rc)] = blocks[k][...].astype(F32)
    for s in range(8):
        wide_s[12 * s : 12 * s + 12, :] = blocks_s[s, 0:12, :]
    for t in range(2):
        early_ref[96 * t : 96 * t + 96, :] = wide_s[:, 128 * t : 128 * t + 128].astype(BF)
        late_ref[96 * t : 96 * t + 96, :] = wide_s[:, CHAN + 128 * t : CHAN + 128 * t + 128].astype(BF)
    for t in range(3):
        early_ref[192 + 16 * t : 208 + 16 * t, :] = rest_ref[:, WIDTH + 128 * t : WIDTH + 128 * t + 128]
    for t in range(12):
        late_ref[192 + 16 * t : 208 + 16 * t, :] = rest_ref[:, 128 * t : 128 * t + 128]
    for t in range(9):
        late_ref[COLS + 96 * t : COLS + 96 * t + 96, :] = wide_s[:, 512 + 128 * t : 640 + 128 * t].astype(BF)


def early_unpack_kernel(all_ref, w_ref, c_ref):
    for p in range(16):
        at = EARLY * p
        for t in range(2):
            w_ref[96 * p : 96 * p + 96, 128 * t : 128 * t + 128] = all_ref[at + 96 * t : at + 96 * t + 96, :]
        for t in range(3):
            lo = at + 192 + 16 * t
            c_ref[16 * p : 16 * p + 16, 128 * t : 128 * t + 128] = all_ref[lo : lo + 16, :]


def late_unpack_kernel(all_ref, w_ref, o_ref, late_s, copy_sems):
    slots = [late_s.at[COLS * p : COLS * p + COLS, :] for p in range(16)]
    loads = start_loads([(all_ref.at[LATE * p : LATE * p + COLS, :], slots[p]) for p in range(16)], copy_sems, 0)
    for p in range(16):
        loads[p].wait()
        at = COLS * p
        for t in range(2):
            w_ref[96 * p : 96 * p + 96, 128 * t : 128 * t + 128] = late_s[at + 96 * t : at + 96 * t + 96, :]
        for t in range(12):
            lo = at + 192 + 16 * t
            o_ref[16 * p : 16 * p + 16, 128 * t : 128 * t + 128] = late_s[lo : lo + 16, :]


def cols_unpack_kernel(all_ref, w_ref):
    for p in range(16):
        for t in range(9):
            at = LATE * p + COLS + 96 * t
            w_ref[96 * p : 96 * p + 96, 128 * t : 128 * t + 128] = all_ref[at : at + 96, :]


def down_pack_kernel(down_ref, out_ref):
    down = jnp.concatenate([down_ref[...].astype(F32), jnp.zeros((12, WIDTH), F32)]).astype(BF)
    for j in range(4):
        out_ref[48 * j : 48 * j + 48, :] = down[:, 384 * j : 384 * j + 384]


def down_unpack_kernel(all_ref, d_ref, wide_s):
    for p in range(16):
        for j in range(4):
            at = p * DOWN_ROWS + 48 * j
            wide_s[36 * p : 36 * p + 36, 384 * j : 384 * j + 384] = all_ref[at : at + 48, :].astype(F32)[:36]
    d_ref[0:HID, :] = wide_s[...].astype(BF)
    d_ref[HID:, :] = jnp.zeros((HID_PAD - HID, WIDTH), BF)


def in_proj_kernel(pos, *refs):
    x_refs, w_mine, w_theirs = refs[:4], refs[4], refs[5]
    xl_mine, xl_theirs, x_s, rs_ref, copy_sems = refs[6:]
    wait_all(start_in(pos, x_refs, x_s, copy_sems))
    for k in range(ROWS // STEP):
        rows = slice(k * STEP, k * STEP + STEP)
        here = x_s[rows, :]
        wide = here.astype(F32)
        scale = lax.rsqrt(jnp.mean(wide * wide, axis=-1, keepdims=True) + EPS)
        rs_ref[rows, :] = jnp.broadcast_to(scale, (STEP, 128))
        xl_theirs[rows, :] = (nn(here, w_theirs[...]) * scale).astype(BF)
        xl_mine[rows, :] = (nn(here, w_mine[...]) * scale).astype(BF)


def y_proj_kernel(x_ref, rs_ref, w_mine, w_theirs, yp_ref):
    for k in range(ROWS // STEP):
        rows = slice(k * STEP, k * STEP + STEP)
        scale = rs_ref[rows, 0:1]
        yp_ref[rows, :CHAN] = nn(x_ref[rows, :], w_mine[...]) * scale
        yp_ref[rows, CHAN:] = nn(x_ref[rows, :], w_theirs[...]) * scale


def recurrence_kernel(pos, mine_ref, theirs_ref, c_ref, edge_ref, *refs):
    hid_mine, hid_theirs, xl_s, a_s, rg_s, op_s, hid_s, push_s, cum_s = refs
    xl_s[0:8, :] = edge_ref[0:8, :]
    hid_s[0:8, :] = edge_ref[8:16, :]
    for y in range(4):
        for rc, ref in enumerate((mine_ref, theirs_ref)):
            at = pl.multiple_of(8 + time_start(pos, y, rc), 8)
            xl_s[pl.ds(at, BLOCK), :] = ref[BLOCK * y : BLOCK * y + BLOCK, :].astype(F32)
    small = small_rows(c_ref)
    gate_w = c_ref[:, 0:CHAN]
    decay_scale = -8.0 * softplus(small[7:8, :])
    for k in range(TOKENS // STEP):
        lo = k * STEP
        conv = small[4:5, :]
        for tap in range(4):
            conv = conv + small[tap : tap + 1, :] * xl_s[lo + 8 - tap : lo + 8 - tap + STEP, :]
        conv = conv.astype(BF)
        raw = [nn(conv[:, 128 * h : 128 * h + 128], gate_w[128 * h : 128 * h + 128, :]) for h in (0, 1)]
        rg = jax.nn.sigmoid(jnp.concatenate([raw[0][:, :128], raw[1][:, :128]], axis=1) + small[5:6, :])
        op = jax.nn.sigmoid(jnp.concatenate([raw[0][:, 128:], raw[1][:, 128:]], axis=1) + small[6:7, :])
        log_a = decay_scale * rg
        put_rows(a_s, lo, STEP, jnp.exp(log_a))
        put_rows(push_s, lo, STEP, jnp.sqrt(neg_expm1(2.0 * log_a)) * op * conv.astype(F32))
        rg_s[lo : lo + STEP, :] = rg
        op_s[lo : lo + STEP, :] = op
    put_rows(a_s, TOKENS, 8, jnp.zeros((8, CHAN), F32))
    state, product = chain(a_s, 0, push_s, cum_s, False)
    entering = edge_ref[15:16, :]
    for k in range(8):
        lo = k * BLOCK
        hidden = get_rows(push_s, lo, BLOCK) + get_rows(cum_s, lo, BLOCK) * entering
        entering = state[k : k + 1, :] + product[k : k + 1, :] * entering
        hid_s[8 + lo : 8 + lo + BLOCK, :] = hidden
    for y in range(4):
        for rc, ref in enumerate((hid_mine, hid_theirs)):
            at = pl.multiple_of(8 + time_start(pos, y, rc), 8)
            ref[BLOCK * y : BLOCK * y + BLOCK, :] = hid_s[pl.ds(at, BLOCK), :].astype(BF)


def out_proj_kernel(pos, hid_mine, hid_theirs, yp_ref, o_mine, o_theirs, *refs):
    outs, mix_ref, part_s, sems = refs[:4], refs[4], refs[5], refs[6]
    for k in range(ROWS // STEP):
        rows = slice(k * STEP, k * STEP + STEP)
        act, _ = gelu_parts(yp_ref[rows, :])
        hidden = jnp.concatenate([hid_mine[rows, :], hid_theirs[rows, :]], axis=1)
        mixed = (hidden.astype(F32) * act).astype(BF)
        mix_ref[rows, :] = mixed
        part = nn(mixed[:, :CHAN], o_mine[...]) + nn(mixed[:, CHAN:], o_theirs[...])
        part_s[rows, :] = part.astype(BF)
    wait_all(start_out(pos, part_s, outs, sems))


def mlp_kernel(pos, *refs):
    x_refs, c_refs, weights = refs[:4], refs[4:8], (refs[8:10], refs[10:12])
    outs, xc_ref, saves, (part_s, copy_sems) = refs[12:16], refs[16], refs[17:19], refs[19:]
    x_s, c_ref = xc_ref.at[:ROWS, :], xc_ref.at[ROWS:, :]
    wait_all(start_in(pos, x_refs, x_s, copy_sems) + start_in(pos, c_refs, c_ref, copy_sems, 4))

    @pl.loop(0, ROWS // STEP)
    def _(k):
        rows = pl.ds(pl.multiple_of(k * STEP, STEP), STEP)
        part = None
        for (w_ref, d_ref), save_ref in zip(weights, saves):
            pre = nn(x_s[rows, :], w_ref[...])
            d_product = nt(c_ref[rows, :], d_ref[...])
            last = pre[:, 1024:1152]
            gate = jnp.concatenate([pre[:, :512], last], axis=1)
            up = jnp.concatenate([pre[:, 512:1024], pltpu.roll(last, 64, 1)], axis=1)
            act, slope = gelu_parts(gate)
            save_ref[rows, :HID_PAD] = (act * up).astype(BF)
            d_gate = d_product * up * slope
            d_up = d_product * act
            d_last = d_gate[:, 512:] + pltpu.roll(d_up[:, 512:], 64, 1)
            d_pre = jnp.concatenate([d_gate[:, :512], d_up[:, :512], d_last], axis=1).astype(BF)
            save_ref[rows, HID_PAD:] = d_pre
            term = nt(d_pre, w_ref[...])
            part = term if part is None else part + term
        part_s[rows, :] = part.astype(BF)

    wait_all(start_out(pos, part_s, outs, copy_sems))


def mlp_out_kernel(prod_mine, prod_theirs, d_mine, d_theirs, out_ref):
    for k in range(ROWS // STEP):
        rows = slice(k * STEP, k * STEP + STEP)
        part = nn(prod_mine[rows, :HID_PAD], d_mine[...]) + nn(prod_theirs[rows, :HID_PAD], d_theirs[...])
        out_ref[rows, :] = part.astype(BF)


def mlp_grads_kernel(*refs):
    xc_refs, save_refs, (out_ref, w_s, d_s) = refs[:2], refs[2:4], refs[4:]
    for k in range(WIDTH // STEP):
        cols = slice(STEP * k, STEP * k + STEP)
        grads = [tn(xc[:ROWS, cols], save[:, HID_PAD:]) for xc, save in zip(xc_refs, save_refs)]
        w_s[cols, :] = (grads[0] + grads[1]).astype(BF)
    for k in range(HID_PAD // 128):
        cols = slice(128 * k, 128 * k + 128)
        grads = [tn(save[:, cols], xc[ROWS:, :]) for xc, save in zip(xc_refs, save_refs)]
        d_s[cols, :] = grads[0] + grads[1]
    for p in range(16):
        for j in range(3):
            at = p * MLP_ROWS + 96 * j
            out_ref[at : at + 96, :] = w_s[96 * p : 96 * p + 96, 384 * j : 384 * j + 384]
        for j in range(4):
            at = p * MLP_ROWS + 288 + 48 * j
            out_ref[at : at + 48, :] = d_s[36 * p : 36 * p + 48, 384 * j : 384 * j + 384].astype(BF)


def mixed_backward_kernel(pos, *refs):
    d_refs, (o_mine, o_theirs, yp_ref, hid_mine, hid_theirs, rs_ref) = refs[:4], refs[4:10]
    mine_ref, theirs_ref, d_s, copy_sems = refs[10:]
    wait_all(start_in(pos, d_refs, d_s, copy_sems))
    sides = ((o_mine, hid_mine, mine_ref), (o_theirs, hid_theirs, theirs_ref))
    for k in range(ROWS // STEP):
        rows = slice(k * STEP, k * STEP + STEP)
        here = d_s[rows, :]
        scale = rs_ref[rows, 0:1]
        for h, (o_ref, hid_ref, out_ref) in enumerate(sides):
            d_mixed = nt(here, o_ref[...])
            act, slope = gelu_parts(yp_ref[rows, CHAN * h : CHAN * h + CHAN])
            out_ref[rows, :CHAN] = (d_mixed * act).astype(BF)
            out_ref[rows, CHAN:] = (d_mixed * hid_ref[rows, :].astype(F32) * slope * scale).astype(BF)


def out_grads_kernel(mix_ref, d_ref, mine_ref, theirs_ref):
    theirs_ref[...] = tn(mix_ref[:, CHAN:], d_ref[...]).astype(BF)
    mine_ref[...] = tn(mix_ref[:, :CHAN], d_ref[...]).astype(BF)


def chain_backward_kernel(pos, *refs):
    (mine_ref, theirs_ref, c_ref, xl_ref, a_ref, rg_ref, op_ref, hid_ref) = refs[:8]
    dx_mine, dx_theirs, gs_ref, dh_s, cum_s, dc_s, dx_s, acc_s = refs[8:]
    for y in range(4):
        for rc, ref in enumerate((mine_ref, theirs_ref)):
            block = ref[BLOCK * y : BLOCK * y + BLOCK, :CHAN].astype(F32)
            at = pl.multiple_of(time_start(pos, y, rc), BLOCK)
            for k in (0, 1):
                side(dh_s, k)[pl.ds(at, BLOCK), :] = block[:, 128 * k : 128 * k + 128]
    state, product = chain(a_ref, 1, dh_s, cum_s, True)
    small = small_rows(c_ref)
    gate_w = c_ref[:, 0:CHAN]
    decay = small[7:8, :]
    decay_scale = -8.0 * softplus(decay)
    decay_slope = -8.0 * jax.nn.sigmoid(decay)
    acc_s[...] = jnp.zeros_like(acc_s)
    dc_s[TOKENS:, :] = jnp.zeros((8, CHAN), F32)
    later = [None] * 8
    entering = jnp.zeros((1, CHAN), F32)
    for k in reversed(range(8)):
        later[k] = entering
        entering = state[k : k + 1, :] + product[k : k + 1, :] * entering
    gate_grads = [jnp.zeros((128, CHAN), F32) for _ in (0, 1)]
    for k in range(8):
        lo = k * BLOCK
        rows = slice(lo, lo + BLOCK)
        state_grad = get_rows(dh_s, lo, BLOCK) + get_rows(cum_s, lo, BLOCK) * later[k]
        shifted = [xl_ref[lo + 8 - tap : lo + 8 - tap + BLOCK, :] for tap in range(4)]
        conv = small[4:5, :]
        for tap in range(4):
            conv = conv + small[tap : tap + 1, :] * shifted[tap]
        conv_low = conv.astype(BF)
        conv = conv_low.astype(F32)
        rg, op, a = rg_ref[rows, :], op_ref[rows, :], get_rows(a_ref, lo, BLOCK)
        root = jnp.sqrt(neg_expm1(2.0 * decay_scale * rg))
        pushed = state_grad * op
        d_log = a * (state_grad * hid_ref[lo + 7 : lo + 7 + BLOCK, :] - pushed * conv * a / root)
        d_rg = d_log * rg
        acc_s[7:8, :] += jnp.sum(d_rg, axis=0, keepdims=True) * decay_slope
        d_raw = decay_scale * d_rg * (1.0 - rg)
        d_open = pushed * root * conv * (1.0 - op)
        acc_s[5:6, :] += jnp.sum(d_raw, axis=0, keepdims=True)
        acc_s[6:7, :] += jnp.sum(d_open, axis=0, keepdims=True)
        d_raw, d_open = d_raw.astype(BF), d_open.astype(BF)
        back = []
        for h in (0, 1):
            cols = slice(128 * h, 128 * h + 128)
            d_block = jnp.concatenate([d_raw[:, cols], d_open[:, cols]], axis=1)
            gate_grads[h] = gate_grads[h] + tn(conv_low[:, cols], d_block)
            back.append(nt(d_block, gate_w[cols, :]))
        d_conv = pushed * root + jnp.concatenate(back, axis=1)
        dc_s[rows, :] = d_conv
        acc_s[4:5, :] += jnp.sum(d_conv, axis=0, keepdims=True)
        for tap in range(4):
            acc_s[tap : tap + 1, :] += jnp.sum(d_conv * shifted[tap], axis=0, keepdims=True)
    for k in range(8):
        lo = k * BLOCK
        d_x = small[0:1, :] * dc_s[lo : lo + BLOCK, :]
        for tap in range(1, 4):
            d_x = d_x + small[tap : tap + 1, :] * dc_s[lo + tap : lo + tap + BLOCK, :]
        dx_s[lo : lo + BLOCK, :] = d_x
    for y in range(4):
        for rc, ref in enumerate((dx_mine, dx_theirs)):
            at = pl.multiple_of(time_start(pos, y, rc), BLOCK)
            ref[BLOCK * y : BLOCK * y + BLOCK, :] = dx_s[pl.ds(at, BLOCK), :].astype(BF)
    for h in (0, 1):
        gs_ref[128 * h : 128 * h + 128, 0:256] = gate_grads[h].astype(BF)
    gs_ref[:, 256:384] = acc_s[...].T.astype(BF)


def normed_backward_kernel(pos, dx_mine, dx_theirs, dy_mine, dy_theirs, rs_ref, *refs):
    weights, outs, part_s, copy_sems = refs[:4], refs[4:8], refs[8], refs[9]
    for k in range(ROWS // STEP):
        rows = slice(k * STEP, k * STEP + STEP)
        scale = rs_ref[rows, 0:1]
        lows = [(dx_ref[rows, :].astype(F32) * scale).astype(BF) for dx_ref in (dx_mine, dx_theirs)]
        lows += [dy_mine[rows, CHAN:], dy_theirs[rows, CHAN:]]
        part_s[rows, :] = sum(nt(low, w_ref[...]) for low, w_ref in zip(lows, weights)).astype(BF)
    wait_all(start_out(pos, part_s, outs, copy_sems))


def cols_grads_kernel(*refs):
    x_refs, dx_refs, dy_refs, rs_ref = refs[:2], refs[2:4], refs[4:6], refs[6]
    go_mine, go_theirs, gs_ref, out_ref, wide_s, rest_s = refs[7:]
    rest_s[:, 0:WIDTH] = (go_mine[...].astype(F32) + go_theirs[...].astype(F32)).astype(BF)
    rest_s[:, WIDTH:C_WIDTH] = gs_ref[...]
    rest_s[:, C_WIDTH:] = jnp.zeros((CHAN, 8 * REST - C_WIDTH), BF)
    wide = x_refs[1][...].astype(F32)
    scales = (rs_ref[:, 0:1], lax.rsqrt(jnp.mean(wide * wide, axis=-1, keepdims=True) + EPS))
    lows = [
        jnp.concatenate([(dx[...].astype(F32) * scale).astype(BF), dy[:, CHAN:]], axis=1)
        for dx, dy, scale in zip(dx_refs, dy_refs, scales)
    ]
    for k in range(WIDTH // STEP):
        rows = slice(STEP * k, STEP * k + STEP)
        wide_s[rows, :] = tn(x_refs[0][:, rows], lows[0]) + tn(x_refs[1][:, rows], lows[1])
    for i in range(128):
        block = [wide_s[12 * i : 12 * i + 12, 128 * t : 128 * t + 128] for t in range(4)]
        out_ref[i, 0:COLS_ROWS, :] = jnp.concatenate(block).astype(BF)
        few = slice(16 * (i // 8), 16 * (i // 8) + 16)
        for t in range(2):
            at = REST * (i % 8) + 128 * t
            out_ref[i, COLS_ROWS + 16 * t : COLS_ROWS + 16 * t + 16, :] = rest_s[few, at : at + 128]


def add_terms(terms):
    out = terms[0][...].astype(F32)
    for term in terms[1:]:
        out = out + term[...].astype(F32)
    return out


def residual_kernel(x_ref, *refs):
    terms, (res_ref, scale_ref, low_ref) = refs[:4], refs[4:]
    residual = x_ref[...].astype(F32) + add_terms(terms)
    scale = lax.rsqrt(jnp.mean(residual * residual, axis=-1, keepdims=True) + EPS)
    res_ref[...] = residual
    scale_ref[...] = jnp.broadcast_to(scale, (BLOCK, 128))
    low_ref[...] = (residual * scale).astype(BF)


def d_residual_kernel(cot_ref, res_ref, scale_ref, *refs):
    terms, (d_ref, low_ref) = refs[:4], refs[4:]
    d_normed = add_terms(terms)
    scale = scale_ref[:, 0:1]
    normed = res_ref[...] * scale
    along = jnp.mean(normed * d_normed, axis=-1, keepdims=True)
    d_residual = cot_ref[...].astype(F32) + scale * (d_normed - normed * along)
    d_ref[...] = d_residual
    low_ref[...] = d_residual.astype(BF)


def input_grad_kernel(x_ref, d_ref, *refs):
    terms, out_ref = refs[:4], refs[4]
    scaled = add_terms(terms)
    x = x_ref[...].astype(F32)
    power = 1.0 / (jnp.mean(x * x, axis=-1, keepdims=True) + EPS)
    along = jnp.mean(x * scaled, axis=-1, keepdims=True) * power
    out_ref[...] = (d_ref[...] + scaled - x * along).astype(BF)


def layer_out_kernel(res_ref, *refs):
    sum_ref, out_ref = refs
    out_ref[...] = (res_ref[...] + sum_ref[...].astype(F32)).astype(BF)


def dp_total(got_ref, lo, count):
    out = got_ref[0, lo : lo + count, :].astype(F32)
    for k in range(1, 16):
        out = out + got_ref[k, lo : lo + count, :].astype(F32)
    return out


def finish_cols_kernel(got_ref, gain_ref, x_ref, y_ref, gx_ref, gy_ref, gain_grad_ref, wide_s):
    for s in range(8):
        wide_s[COLS_ROWS * s : COLS_ROWS * s + COLS_ROWS, :] = dp_total(got_ref, SUM_ROWS * s, COLS_ROWS)
    gain = column(gain_ref)
    along = jnp.zeros((12, 128), F32)
    for s in range(8):
        for t in range(4):
            at = CHAN * s + 128 * (t % 2)
            lo = COLS_ROWS * s + 12 * t
            grad = wide_s[lo : lo + 12, :]
            w_ref, g_ref = (x_ref, gx_ref) if t < 2 else (y_ref, gy_ref)
            along = along + grad * w_ref[:, at : at + 128].astype(F32)
            g_ref[:, at : at + 128] = grad * gain
    gain_grad_ref[...] = as_row(jnp.sum(along, axis=1, keepdims=True))


def mlp_back_kernel(got_ref, cols_ref, down_ref, wide_s):
    for j in range(3):
        wide_s[:, 384 * j : 384 * j + 384] = got_ref[96 * j : 96 * j + 96, :].astype(F32)
    for s in range(8):
        block = jnp.concatenate([wide_s[12 * s : 12 * s + 12, :], jnp.zeros((4, GATED), F32)])
        cols_ref[s] = block.astype(BF)
    for j in range(4):
        down_ref[:, 384 * j : 384 * j + 384] = got_ref[288 + 48 * j : 336 + 48 * j, :]


def rest_back_kernel(cols_ref, got_ref, out_ref):
    out_ref[:, :, :GATED] = cols_ref[...]
    for s in range(8):
        for t in range(2):
            tile = dp_total(got_ref, SUM_ROWS * s + COLS_ROWS + 16 * t, 16)
            out_ref[s, :, GATED + 128 * t : GATED + 128 * t + 128] = tile.astype(BF)


def mlp_finish_kernel(*refs):
    got_ref, down_ref, gain_ref, gate_ref, up_ref, g_gate_ref, g_up_ref, g_down_ref, gain_grad_ref = refs
    g_down_ref[...] = down_ref[...].astype(F32)[:36]
    gain = column(gain_ref)
    along = jnp.zeros((12, 1), F32)
    for s in range(8):
        block = got_ref[s, :, :GATED].astype(F32)[:12]
        lo = HID * s
        cols = slice(lo, lo + HID)
        grad_gate = jnp.concatenate([block[:, :512], block[:, 1024:1088]], axis=1)
        grad_up = jnp.concatenate([block[:, 512:1024], block[:, 1088:]], axis=1)
        terms = grad_gate * gate_ref[:, cols].astype(F32) + grad_up * up_ref[:, cols].astype(F32)
        along = along + jnp.sum(terms, axis=1, keepdims=True)
        g_gate_ref[:, cols] = grad_gate * gain
        g_up_ref[:, cols] = grad_up * gain
    gain_grad_ref[...] = as_row(along)


def rest_join_kernel(got_ref, out_ref):
    for s in range(8):
        out_ref[:, REST * s : REST * s + REST] = got_ref[s, :, GATED:]


def finish_rest_kernel(got_ref, out_ref, gate_w_ref, taps_ref, bias_ref, gate_bias_ref, decay_ref):
    out_ref[...] = got_ref[:, 0:WIDTH].astype(F32)
    gate_w_ref[...] = got_ref[:, 1536:1792].astype(F32)
    small = got_ref[:, 1792:1920].astype(F32)
    rows = [as_row(small[:, k : k + 1]) for k in range(8)]
    for k in range(4):
        taps_ref[k : k + 1, :] = rows[k]
    bias_ref[...] = rows[4]
    for k in range(2):
        gate_bias_ref[k : k + 1, :] = rows[5 + k]
    decay_ref[...] = rows[7]


def shape(dims, dtype):
    return jax.ShapeDtypeStruct(dims, dtype)


def sems(count):
    return pltpu.SemaphoreType.DMA((count,))


def call(kernel, args, outs, scratch=(), any_args=(), any_outs=(), micros=0):
    in_specs = [SMEM if a.dtype == jnp.int32 else ANY if k in any_args else VMEM for k, a in enumerate(args)]
    return pl.pallas_call(
        kernel,
        name=kernel.__name__.removesuffix("_kernel"),
        in_specs=in_specs,
        out_specs=[ANY if k in any_outs else VMEM for k in range(len(outs))],
        out_shape=[shape(*o) for o in outs],
        scratch_shapes=scratch,
        cost_estimate=pl.CostEstimate(flops=int(micros * 10**9), bytes_accessed=0, transcendentals=0),
        compiler_params=pltpu.CompilerParams(vmem_limit_bytes=60 << 20),
    )(*args)


PART = ((BLOCK, WIDTH), BF)
PARTS = [PART] * 4
PART_S = pltpu.VMEM((ROWS, WIDTH), BF)
CHAIN_S = pltpu.VMEM((2 * TOKENS, 128), F32)


def per_device(
    inputs,
    cotangent,
    resets,
    start_state,
    conv_history,
    norm_gain,
    proj_x,
    proj_y,
    conv_taps,
    conv_bias,
    gate_weight,
    gate_bias,
    decay_param,
    proj_out,
    mlp_gain,
    mlp_gate,
    mlp_up,
    mlp_down,
):
    pos = jnp.stack([lax.axis_index(a) for a in DP_SEQ]).astype(jnp.int32)
    flat_in = inputs[0]
    flat_cot = cotangent[0]
    gain_one = norm_gain[None]
    gain_two = mlp_gain[None]

    (rest,) = call(
        pack_rows_kernel,
        (proj_out, gate_weight, conv_taps.T, conv_bias[None], gate_bias.T, decay_param[None]),
        [((16, C_WIDTH), BF)],
    )
    rest, late_x, late_down = tied(rest, proj_x, mlp_down)
    rest = transposed_devices(rest, False)
    blocks = call(
        pack_cols_kernel,
        (pos, gain_one, gain_two, late_x, proj_y, mlp_gate, mlp_up),
        [((16, SENT), BF)] * 8,
        [pltpu.VMEM((8, 16, SENT), F32)],
    )
    early, late = call(
        shard_kernel,
        (pos, *exchanged(blocks), rest),
        [((EARLY, 128), BF), ((LATE, 128), BF)],
        [pltpu.VMEM((8, 16, SENT), F32), pltpu.VMEM((96, SENT), F32)],
    )
    late = lax.all_gather(late, DP, axis=0, tiled=True)
    early, early_in, late_down = tied(early, flat_in, late_down)
    x_pieces = gather_rows(early_in)
    down = transposed_devices(late_down, False)
    early = lax.all_gather(early, DP, axis=0, tiled=True)
    early, x_pieces, down = tied(early, x_pieces, down)
    x_mine, c_mine = call(early_unpack_kernel, (early,), [((WIDTH, CHAN), BF), ((CHAN, SMALL), BF)])
    x_mine, late_cot, down = tied(x_mine, flat_cot, down)
    (down,) = call(down_pack_kernel, (down,), [((DOWN_ROWS, MLP_LANES), BF)])
    down = lax.all_gather(down, DP, axis=0, tiled=True)
    x_theirs = swapped(x_mine)
    c_near = [hop(late_cot, "y", r) for r in PIECES[1:3]]

    keep = (1 - resets).astype(F32)
    place = lax.axis_index(SEQ) * CHAN
    history = lax.dynamic_slice(conv_history[0].astype(F32), (0, place), (3, CHAN)) * keep
    initial = lax.dynamic_slice(start_state, (0, place), (1, CHAN)) * keep
    edges = jnp.concatenate([jnp.zeros((5, CHAN), F32), history, jnp.zeros((7, CHAN), F32), initial])
    xl_mine, xl_theirs, x_all, rs = call(
        in_proj_kernel,
        (pos, *x_pieces, x_mine, x_theirs),
        [((ROWS, CHAN), BF)] * 2 + [((ROWS, WIDTH), BF), ((ROWS, 128), F32)],
        [sems(4)],
        any_args=range(1, 5),
        micros=8,
    )
    xl_got, c_near, late_cot = tied(swapped(xl_theirs), c_near, late_cot)
    c_far = hop(late_cot, "y", PIECES[3])
    hid_mine, hid_theirs, xl, a, rg, op, hid = call(
        recurrence_kernel,
        (pos, xl_mine, xl_got, c_mine, edges),
        [((ROWS, CHAN), BF)] * 2
        + [
            ((TOKENS + 8, CHAN), F32),
            ((2 * TOKENS + 16, 128), F32),
            ((TOKENS, CHAN), F32),
            ((TOKENS, CHAN), F32),
            ((TOKENS + 8, CHAN), F32),
        ],
        [CHAIN_S, CHAIN_S],
        micros=8,
    )
    hid_theirs = swapped(hid_theirs)
    hid_mine, c_far, late = tied(hid_mine, c_far, late)
    c_pieces = [flat_cot, *c_near, c_far]
    y_mine, o_mine = call(
        late_unpack_kernel,
        (late,),
        [((WIDTH, CHAN), BF), ((CHAN, WIDTH), BF)],
        [pltpu.VMEM((16 * COLS, 128), BF), sems(16)],
        any_args=range(1),
    )
    y_theirs, o_theirs = swapped(y_mine), swapped(o_mine)
    (yp,) = call(y_proj_kernel, (x_all, rs, y_mine, y_theirs), [((ROWS, 2 * CHAN), F32)], micros=8)
    *parts, mix = call(
        out_proj_kernel,
        (pos, hid_mine, hid_theirs, yp, o_mine, o_theirs),
        PARTS + [((ROWS, 2 * CHAN), BF)],
        [PART_S, sems(4)],
        any_outs=range(4),
        micros=1.2,
    )
    terms = scatter_rows(parts)
    _, late = tied(parts, late)
    (w_up,) = call(cols_unpack_kernel, (late,), [((WIDTH, GATED), BF)])
    w_up, down = tied(w_up, down)
    up_theirs = swapped(w_up)
    (w_down,) = call(down_unpack_kernel, (down,), [((HID_PAD, WIDTH), BF)], [pltpu.VMEM((HID, WIDTH), F32)])
    down_theirs = swapped(w_down)
    terms, w_up, w_down = tied(terms, w_up, w_down)
    residual, scale_two, normed_two = call(
        residual_kernel, (flat_in, *terms), [((BLOCK, WIDTH), F32), ((BLOCK, 128), F32), PART], micros=30
    )

    *parts, tokens, save_mine, save_theirs = call(
        mlp_kernel,
        (pos, *gather_rows(normed_two), *c_pieces, w_up, w_down, up_theirs, down_theirs),
        PARTS + [((2 * ROWS, WIDTH), BF)] + [((ROWS, HID_PAD + GATED), BF)] * 2,
        [PART_S, sems(8)],
        any_args=range(1, 9),
        any_outs=range(4),
        micros=5,
    )
    (out_part,) = call(
        mlp_out_kernel, (save_mine, save_theirs, w_down, down_theirs), [((ROWS, WIDTH), BF)], micros=15
    )
    terms = scatter_rows(parts)
    tokens_got, save_got = swapped(tokens), swapped(save_theirs)
    save_got, out_part = tied(save_got, out_part)
    (mlp_grads,) = call(
        mlp_grads_kernel,
        (tokens, tokens_got, save_mine, save_got),
        [((16 * MLP_ROWS, MLP_LANES), BF)],
        [pltpu.VMEM((WIDTH, GATED), BF), pltpu.VMEM((HID_PAD, WIDTH), F32)],
        micros=15,
    )
    terms, mlp_grads = tied(terms, mlp_grads)
    mlp_sum = lax.psum_scatter(mlp_grads, DP, scatter_dimension=0, tiled=True)
    d_residual, d_out = call(
        d_residual_kernel, (flat_cot, residual, scale_two, *terms), [((BLOCK, WIDTH), F32), PART]
    )

    d_out, late_x_all = tied(d_out, x_all)
    d_pieces, all_theirs = tied(gather_rows(d_out), swapped(late_x_all))
    back_mine, back_theirs, d_all = call(
        mixed_backward_kernel,
        (pos, *d_pieces, o_mine, o_theirs, yp, hid_mine, hid_theirs, rs),
        [((ROWS, 2 * CHAN), BF)] * 2 + [((ROWS, WIDTH), BF)],
        [sems(4)],
        any_args=range(1, 5),
        micros=2,
    )
    back_got = swapped(back_theirs)
    dx_mine, dx_theirs, g_small = call(
        chain_backward_kernel,
        (pos, back_mine, back_got, c_mine, xl, a, rg, op, hid),
        [((ROWS, CHAN), BF)] * 2 + [((CHAN, 384), BF)],
        [
            CHAIN_S,
            CHAIN_S,
            pltpu.VMEM((TOKENS + 8, CHAN), F32),
            pltpu.VMEM((TOKENS, CHAN), F32),
            pltpu.VMEM((128, CHAN), F32),
        ],
        micros=20,
    )
    dx_got = swapped(dx_theirs)
    parts = call(
        normed_backward_kernel,
        (pos, dx_mine, dx_got, back_mine, back_theirs, rs, x_mine, x_theirs, y_mine, y_theirs),
        PARTS,
        [PART_S, sems(4)],
        any_outs=range(4),
    )
    terms = scatter_rows(parts)
    _, late_mix = tied(parts, mix)
    go_mine, go_theirs = call(out_grads_kernel, (late_mix, d_all), [((CHAN, WIDTH), BF)] * 2)
    (g_cols,) = call(
        cols_grads_kernel,
        (x_all, all_theirs, dx_mine, dx_theirs, back_mine, back_got, rs, go_mine, swapped(go_theirs), g_small),
        [((128, SUM_ROWS, 128), BF)],
        [pltpu.VMEM((WIDTH, 2 * CHAN), F32), pltpu.VMEM((CHAN, 8 * REST), BF)],
    )
    g_cols = lax.all_to_all(g_cols, DP_SEQ, 0, 0, tiled=True).reshape(16, 8 * SUM_ROWS, 128)
    out_part, _ = tied(out_part, mlp_sum)
    out_sum = lax.psum_scatter(out_part, "y", scatter_dimension=0, tiled=True)
    (layer_out,) = call(layer_out_kernel, (residual, out_sum), [PART])

    terms, mlp_sum = tied(terms, mlp_sum)
    blocks, down_back = call(
        mlp_back_kernel,
        (mlp_sum,),
        [((8, 16, GATED), BF), ((48, WIDTH), BF)],
        [pltpu.VMEM((96, GATED), F32)],
        micros=100,
    )
    (input_grad,) = call(input_grad_kernel, (flat_in, d_residual, *terms), [PART])
    (blocks,) = call(rest_back_kernel, (blocks, g_cols), [((8, 16, GATED + REST), BF)])
    blocks = lax.all_to_all(blocks, SEQ, 0, 0, tiled=True)
    (g_rest,) = call(rest_join_kernel, (blocks,), [((16, 8 * REST), BF)])
    g_rest = transposed_devices(g_rest, True)
    grad_x, grad_y, grad_norm_gain = call(
        finish_cols_kernel,
        (g_cols, gain_one, proj_x, proj_y),
        [((12, 8 * CHAN), F32)] * 2 + [((1, 12), F32)],
        [pltpu.VMEM((8 * COLS_ROWS, 128), F32)],
    )
    grad_gate, grad_up, grad_down, grad_mlp_gain = call(
        mlp_finish_kernel,
        (blocks, transposed_devices(down_back, True), gain_two, mlp_gate, mlp_up),
        [((12, 8 * HID), F32)] * 2 + [((36, WIDTH), F32), ((1, 12), F32)],
    )
    grad_out, grad_gate_w, grad_taps, grad_conv_bias, grad_gate_bias, grad_decay = call(
        finish_rest_kernel,
        (g_rest,),
        [((16, WIDTH), F32), ((16, CHAN), F32), ((4, 16), F32), ((1, 16), F32), ((2, 16), F32), ((1, 16), F32)],
    )
    return (
        layer_out[None],
        input_grad[None],
        grad_norm_gain[0],
        grad_x,
        grad_y,
        grad_taps.T,
        grad_conv_bias[0],
        grad_gate_w,
        grad_gate_bias.T,
        grad_decay[0],
        grad_out,
        grad_mlp_gain[0],
        grad_gate,
        grad_up,
        grad_down,
    )


def solution(mesh):
    finer = Mesh(mesh.devices.reshape(4, 4, 4, 2), DP_SEQ)
    rows = P(DP_SEQ, None)
    line = P(DP_SEQ)
    tokens = P(DP, SEQ, None)
    in_specs = (
        tokens,
        tokens,
        P(DP),
        P(DP, None),
        P(DP, None, None),
        line,
        rows,
        rows,
        rows,
        line,
        rows,
        rows,
        line,
        rows,
        line,
        rows,
        rows,
        rows,
    )
    out_specs = (
        tokens,
        tokens,
        line,
        rows,
        rows,
        rows,
        line,
        rows,
        rows,
        line,
        rows,
        line,
        rows,
        rows,
        rows,
    )
    return jax.shard_map(per_device, mesh=finer, in_specs=in_specs, out_specs=out_specs, check_vma=False)
```

```python
import math

import jax
import jax.numpy as jnp
from jax import lax
from jax.experimental import pallas as pl
from jax.experimental.pallas import tpu as pltpu
from jax.sharding import Mesh
from jax.sharding import PartitionSpec as P

BF = jnp.bfloat16
F32 = jnp.float32
EPS = 1e-06
GELU_C = 0.7978845608028654
GELU_K = 0.044715

TOKENS = 1024
ROWS = 512
BLOCK = 128
WIDTH = 1536
CHAN = 256
HID = 576
HID_PAD = 640
GATED = 2 * HID
STEP = 256
C_WIDTH = 1920
SENT = 2 * CHAN + GATED
SMALL = 384
EARLY = 240
COLS = 384
LATE = 1248
DOWN_ROWS = 192
COLS_ROWS = 48
SUM_ROWS = 80
REST = 256
MLP_ROWS = 480
MLP_LANES = 384

DP = ("z", "x")
SEQ = ("y", "c")
DP_SEQ = ("z", "x", "y", "c")

ANY = pl.BlockSpec(memory_space=pl.ANY)
HBM = pl.BlockSpec(memory_space=pltpu.HBM)
VMEM = pl.BlockSpec(memory_space=pltpu.VMEM)
SMEM = pl.BlockSpec(memory_space=pltpu.SMEM)

PIECES = (0, 1, 3, 2)
PLACES = [(ry, rc) for rc in (0, 1) for ry in (0, 2, 1, 3)]


def hop(value, axis, distance):
    size = lax.axis_size(axis)
    return lax.ppermute(value, axis, [(i, (i - distance) % size) for i in range(size)])


def added(one, two):
    return (one.astype(F32) + two.astype(F32)).astype(BF)


def swapped(value):
    return hop(value, "c", 1)


def gather_rows(block):
    return [block] + [hop(block, "y", r) for r in PIECES[1:]]


def scatter_rows(parts):
    return [parts[0]] + [hop(parts[r], "y", 4 - r) for r in (2, 1, 3)]


def tied(*values):
    return lax.optimization_barrier(values)


def transposed_devices(value, back):
    pairs = [(16 * s + d, 8 * d + s) for s in range(8) for d in range(16)]
    return lax.ppermute(value, DP_SEQ, [(b, a) for a, b in pairs] if back else pairs)


def exchanged(blocks):
    out = []
    for (ry, rc), block in zip(PLACES, blocks):
        route = [(2 * y + c, 2 * ((y + ry) % 4) + (c + rc) % 2) for y in range(4) for c in range(2)]
        out.append(lax.ppermute(block, SEQ, route) if (ry, rc) != (0, 0) else block)
    return out


def nn(a, b):
    return jnp.dot(a, b, preferred_element_type=F32)


def nt(a, b):
    return lax.dot_general(a, b, (((1,), (1,)), ((), ())), preferred_element_type=F32)


def tn(a, b):
    return lax.dot_general(a, b, (((0,), (0,)), ((), ())), preferred_element_type=F32)


def gelu_parts(v):
    sq = v * v
    t = jnp.tanh(GELU_C * v * (1.0 + GELU_K * sq))
    half = 0.5 * (1.0 + t)
    slope = half + 0.5 * v * (1.0 - t * t) * (GELU_C * (1.0 + 3.0 * GELU_K * sq))
    return v * half, slope


def neg_expm1(v):
    series = 1.0 + v * (1.0 / 7.0)
    for k in (6, 5, 4, 3, 2):
        series = 1.0 + v * (1.0 / k) * series
    return jnp.where(v > -0.35, -v * series, 1.0 - jnp.exp(v))


def softplus(v):
    e = jnp.exp(-jnp.abs(v))
    series = e * (1.0 - e * (1 / 2 - e * (1 / 3 - e * (1 / 4 - e * (1 / 5 - e * (1 / 6))))))
    return jnp.maximum(v, 0.0) + jnp.where(e < 0.05, series, jnp.log(1.0 + e))


def column(row_ref):
    n = row_ref.shape[1]
    square = jnp.broadcast_to(row_ref[...].astype(F32), (n, n))
    same = lax.broadcasted_iota(jnp.int32, (n, n), 0) == lax.broadcasted_iota(jnp.int32, (n, n), 1)
    return jnp.sum(jnp.where(same, square, 0.0), axis=1, keepdims=True)


def as_row(col):
    n = col.shape[0]
    square = jnp.broadcast_to(col, (n, n))
    same = lax.broadcasted_iota(jnp.int32, (n, n), 0) == lax.broadcasted_iota(jnp.int32, (n, n), 1)
    return jnp.sum(jnp.where(same, square, 0.0), axis=0, keepdims=True)


def place_of(pos, ry, rc):
    return lax.rem(pos[2] + ry, 4) * 2 + lax.rem(pos[3] + rc, 2)


def block_rows(pos, ry):
    return pl.ds(pl.multiple_of(lax.rem(pos[2] + ry, 4) * BLOCK, BLOCK), BLOCK)


def time_start(pos, y, rc):
    return (2 * y + lax.rem(pos[3] + rc, 2)) * BLOCK


def start_loads(pairs, sems, first):
    copies = []
    for k, (ref, scratch) in enumerate(pairs):
        copies.append(pltpu.make_async_copy(ref, scratch, sems.at[first + k]))
        copies[-1].start()
    return copies


def start_in(pos, refs, scratch, sems, first=0):
    return start_loads([(ref, scratch.at[block_rows(pos, ry), :]) for ref, ry in zip(refs, PIECES)], sems, first)


def start_out(pos, scratch, refs, sems, first=0):
    return start_loads([(scratch.at[block_rows(pos, r), :], refs[r]) for r in range(4)], sems, first)


def wait_all(copies):
    for copy in copies:
        copy.wait()


def small_rows(c_ref):
    return c_ref[:, CHAN:SMALL].astype(F32).T


def scan_chunks(step, carry):
    def four(k, carry):
        for j in range(4):
            carry = step(k * 4 + j, carry)
        return carry

    return lax.fori_loop(0, BLOCK // 4, four, carry)


def chunk_rows(t):
    return pl.ds(t, 8, stride=BLOCK)


def side(ref, lanes):
    rows = ref.shape[0] // 2
    return ref.at[lanes * rows : (lanes + 1) * rows, :]


def get_rows(ref, lo, count):
    return jnp.concatenate([side(ref, k)[lo : lo + count, :] for k in (0, 1)], axis=1)


def put_rows(ref, lo, count, value):
    for k in (0, 1):
        side(ref, k)[lo : lo + count, :] = value[:, 128 * k : 128 * k + 128]


def chain(mult_ref, ahead, add_ref, product_ref, backward):
    def step(t, carry):
        t = BLOCK - 1 - t if backward else t
        out = []
        for k in (0, 1):
            state, product = carry[2 * k : 2 * k + 2]
            mult = side(mult_ref, k)[chunk_rows(t + ahead), :]
            state = mult * state + side(add_ref, k)[chunk_rows(t), :]
            product = product * mult
            side(add_ref, k)[chunk_rows(t), :] = state
            side(product_ref, k)[chunk_rows(t), :] = product
            out += [state, product]
        return tuple(out)

    zero, one = jnp.zeros((8, 128), F32), jnp.ones((8, 128), F32)
    left, left_p, right, right_p = scan_chunks(step, (zero, one, zero, one))
    return jnp.concatenate([left, right], axis=1), jnp.concatenate([left_p, right_p], axis=1)


def gated_cols(gate, up, s):
    lo = HID * s
    return [gate[:, lo : lo + 512], up[:, lo : lo + 512], gate[:, lo + 512 : lo + HID], up[:, lo + 512 : lo + HID]]


def pack_cols_kernel(pos, gain_one, gain_two, x_ref, y_ref, gate_ref, up_ref, *refs):
    outs, blocks_s = refs[:8], refs[8]
    gain = column(gain_one)
    x, y = x_ref[...].astype(F32) * gain, y_ref[...].astype(F32) * gain
    gain = column(gain_two)
    gate, up = gate_ref[...].astype(F32) * gain, up_ref[...].astype(F32) * gain
    fill = jnp.zeros((4, SENT), F32)
    for s in range(8):
        cols = slice(CHAN * s, CHAN * s + CHAN)
        block = jnp.concatenate([x[:, cols], y[:, cols], *gated_cols(gate, up, s)], axis=1)
        blocks_s[s] = jnp.concatenate([block, fill])
    for k, (ry, rc) in enumerate(PLACES):
        outs[k][...] = blocks_s[place_of(pos, ry, rc)].astype(BF)


def pack_rows_kernel(out_ref, gate_w_ref, taps_ref, bias_ref, gate_bias_ref, decay_ref, rest_ref):
    rest_ref[:, 0:WIDTH] = out_ref[...]
    rest_ref[:, 1536:1792] = gate_w_ref[...]
    lane = lax.broadcasted_iota(jnp.int32, (16, 128), 1)
    small = jnp.zeros((16, 128), F32)
    for k in range(4):
        small = jnp.where(lane == k, column(taps_ref.at[k : k + 1, :]), small)
    small = jnp.where(lane == 4, column(bias_ref), small)
    for k in range(2):
        small = jnp.where(lane == 5 + k, column(gate_bias_ref.at[k : k + 1, :]), small)
    rest_ref[:, 1792:1920] = jnp.where(lane == 7, column(decay_ref), small).astype(BF)


def shard_kernel(pos, *refs):
    blocks, (rest_ref, early_ref, late_ref, blocks_s, wide_s) = refs[:8], refs[8:]
    for k, (ry, rc) in enumerate(PLACES):
        blocks_s[place_of(pos, 4 - ry, rc)] = blocks[k][...].astype(F32)
    for s in range(8):
        wide_s[12 * s : 12 * s + 12, :] = blocks_s[s, 0:12, :]
    for t in range(2):
        early_ref[96 * t : 96 * t + 96, :] = wide_s[:, 128 * t : 128 * t + 128].astype(BF)
        late_ref[96 * t : 96 * t + 96, :] = wide_s[:, CHAN + 128 * t : CHAN + 128 * t + 128].astype(BF)
    for t in range(3):
        early_ref[192 + 16 * t : 208 + 16 * t, :] = rest_ref[:, WIDTH + 128 * t : WIDTH + 128 * t + 128]
    for t in range(12):
        late_ref[192 + 16 * t : 208 + 16 * t, :] = rest_ref[:, 128 * t : 128 * t + 128]
    for t in range(9):
        late_ref[COLS + 96 * t : COLS + 96 * t + 96, :] = wide_s[:, 512 + 128 * t : 640 + 128 * t].astype(BF)


def early_unpack_kernel(all_ref, w_ref, c_ref):
    for p in range(16):
        at = EARLY * p
        for t in range(2):
            w_ref[96 * p : 96 * p + 96, 128 * t : 128 * t + 128] = all_ref[at + 96 * t : at + 96 * t + 96, :]
        for t in range(3):
            lo = at + 192 + 16 * t
            c_ref[16 * p : 16 * p + 16, 128 * t : 128 * t + 128] = all_ref[lo : lo + 16, :]


def late_unpack_kernel(all_ref, w_ref, o_ref, late_s, copy_sems):
    slots = [late_s.at[COLS * p : COLS * p + COLS, :] for p in range(16)]
    loads = start_loads([(all_ref.at[LATE * p : LATE * p + COLS, :], slots[p]) for p in range(16)], copy_sems, 0)
    for p in range(16):
        loads[p].wait()
        at = COLS * p
        for t in range(2):
            w_ref[96 * p : 96 * p + 96, 128 * t : 128 * t + 128] = late_s[at + 96 * t : at + 96 * t + 96, :]
        for t in range(12):
            lo = at + 192 + 16 * t
            o_ref[16 * p : 16 * p + 16, 128 * t : 128 * t + 128] = late_s[lo : lo + 16, :]


def cols_unpack_kernel(all_ref, w_ref, cols_s, copy_sems):
    slots = [cols_s.at[864 * p : 864 * p + 864, :] for p in range(16)]
    ends = [(all_ref.at[LATE * p + COLS : LATE * p + LATE, :], slots[p]) for p in range(16)]
    loads = start_loads(ends, copy_sems, 0)
    for p in range(16):
        loads[p].wait()
        for t in range(9):
            at = 864 * p + 96 * t
            w_ref[96 * p : 96 * p + 96, 128 * t : 128 * t + 128] = cols_s[at : at + 96, :]


def down_pack_kernel(down_ref, out_ref):
    down = jnp.concatenate([down_ref[...].astype(F32), jnp.zeros((12, WIDTH), F32)]).astype(BF)
    for j in range(4):
        out_ref[48 * j : 48 * j + 48, :] = down[:, 384 * j : 384 * j + 384]


def down_unpack_kernel(all_ref, d_ref, wide_s):
    for p in range(16):
        for j in range(4):
            at = p * DOWN_ROWS + 48 * j
            wide_s[36 * p : 36 * p + 36, 384 * j : 384 * j + 384] = all_ref[at : at + 48, :].astype(F32)[:36]
    d_ref[0:HID, :] = wide_s[...].astype(BF)
    d_ref[HID:, :] = jnp.zeros((HID_PAD - HID, WIDTH), BF)


def in_proj_kernel(pos, *refs):
    x_refs, w_mine, w_theirs = refs[:4], refs[4], refs[5]
    xl_mine, xl_theirs, x_s, rs_ref, copy_sems = refs[6:]
    wait_all(start_in(pos, x_refs, x_s, copy_sems))
    for k in range(ROWS // STEP):
        rows = slice(k * STEP, k * STEP + STEP)
        here = x_s[rows, :]
        wide = here.astype(F32)
        scale = lax.rsqrt(jnp.mean(wide * wide, axis=-1, keepdims=True) + EPS)
        rs_ref[rows, :] = jnp.broadcast_to(scale, (STEP, 128))
        xl_theirs[rows, :] = (nn(here, w_theirs[...]) * scale).astype(BF)
        xl_mine[rows, :] = (nn(here, w_mine[...]) * scale).astype(BF)


def y_proj_kernel(x_ref, rs_ref, w_mine, w_theirs, yp_ref):
    for k in range(ROWS // STEP):
        rows = slice(k * STEP, k * STEP + STEP)
        scale = rs_ref[rows, 0:1]
        yp_ref[rows, :CHAN] = nn(x_ref[rows, :], w_mine[...]) * scale
        yp_ref[rows, CHAN:] = nn(x_ref[rows, :], w_theirs[...]) * scale


def saved_parts(ref):
    return [ref.at[(TOKENS + 8) * k : (TOKENS + 8) * (k + 1), :] for k in range(4)]


def recurrence_kernel(pos, mine_ref, theirs_ref, c_ref, edge_ref, *refs):
    hid_mine, hid_theirs, saved_ref, a_s, push_s, cum_s = refs
    xl_s, rg_s, op_s, hid_s = saved_parts(saved_ref)
    xl_s[0:8, :] = edge_ref[0:8, :]
    hid_s[0:8, :] = edge_ref[8:16, :]
    for y in range(4):
        for rc, ref in enumerate((mine_ref, theirs_ref)):
            at = pl.multiple_of(8 + time_start(pos, y, rc), 8)
            xl_s[pl.ds(at, BLOCK), :] = ref[BLOCK * y : BLOCK * y + BLOCK, :].astype(F32)
    small = small_rows(c_ref)
    gate_w = c_ref[:, 0:CHAN]
    decay_scale = -8.0 * softplus(small[7:8, :])
    for k in range(TOKENS // STEP):
        lo = k * STEP
        conv = small[4:5, :]
        for tap in range(4):
            conv = conv + small[tap : tap + 1, :] * xl_s[lo + 8 - tap : lo + 8 - tap + STEP, :]
        conv = conv.astype(BF)
        raw = [nn(conv[:, 128 * h : 128 * h + 128], gate_w[128 * h : 128 * h + 128, :]) for h in (0, 1)]
        rg = jax.nn.sigmoid(jnp.concatenate([raw[0][:, :128], raw[1][:, :128]], axis=1) + small[5:6, :])
        op = jax.nn.sigmoid(jnp.concatenate([raw[0][:, 128:], raw[1][:, 128:]], axis=1) + small[6:7, :])
        log_a = decay_scale * rg
        put_rows(a_s, lo, STEP, jnp.exp(log_a))
        put_rows(push_s, lo, STEP, jnp.sqrt(neg_expm1(2.0 * log_a)) * op * conv.astype(F32))
        rg_s[lo : lo + STEP, :] = rg
        op_s[lo : lo + STEP, :] = op
    state, product = chain(a_s, 0, push_s, cum_s, False)
    entering = edge_ref[15:16, :]
    for k in range(8):
        lo = k * BLOCK
        hidden = get_rows(push_s, lo, BLOCK) + get_rows(cum_s, lo, BLOCK) * entering
        entering = state[k : k + 1, :] + product[k : k + 1, :] * entering
        hid_s[8 + lo : 8 + lo + BLOCK, :] = hidden
    for y in range(4):
        for rc, ref in enumerate((hid_mine, hid_theirs)):
            at = pl.multiple_of(8 + time_start(pos, y, rc), 8)
            ref[BLOCK * y : BLOCK * y + BLOCK, :] = hid_s[pl.ds(at, BLOCK), :].astype(BF)


def out_proj_kernel(pos, hid_mine, hid_theirs, yp_ref, o_mine, o_theirs, *refs):
    outs, mix_ref, part_s, sems = refs[:4], refs[4], refs[5], refs[6]
    for k in range(ROWS // STEP):
        rows = slice(k * STEP, k * STEP + STEP)
        act, _ = gelu_parts(yp_ref[rows, :])
        hidden = jnp.concatenate([hid_mine[rows, :], hid_theirs[rows, :]], axis=1)
        mixed = (hidden.astype(F32) * act).astype(BF)
        mix_ref[rows, :] = mixed
        part = nn(mixed[:, :CHAN], o_mine[...]) + nn(mixed[:, CHAN:], o_theirs[...])
        part_s[rows, :] = part.astype(BF)
    wait_all(start_out(pos, part_s, outs, sems))


def mlp_pre_kernel(pos, *refs):
    x_refs, c_refs, weights, (xc_ref, *pres), copy_sems = refs[:4], refs[4:8], refs[8:10], refs[10:13], refs[13]
    loads = start_in(pos, x_refs, xc_ref.at[:ROWS, :], copy_sems)
    later = start_in(pos, c_refs, xc_ref.at[ROWS:, :], copy_sems, 4)
    wait_all(loads)
    for k in range(ROWS // STEP):
        rows = slice(k * STEP, k * STEP + STEP)
        for w_ref, pre_ref in zip(weights, pres):
            pre_ref[rows, :] = nn(xc_ref[rows, :], w_ref[...])
    wait_all(later)


def mlp_kernel(pos, xc_ref, *refs):
    pres, weights, outs, saves, (part_s, copy_sems) = refs[:2], (refs[2:4], refs[4:6]), refs[6:10], refs[10:12], refs[12:]

    @pl.loop(0, ROWS // STEP)
    def _(k):
        rows = pl.ds(pl.multiple_of(k * STEP, STEP), STEP)
        cot = xc_ref[pl.ds(pl.multiple_of(ROWS + k * STEP, STEP), STEP), :]
        part = None
        for (w_ref, d_ref), pre_ref, save_ref in zip(weights, pres, saves):
            d_product = nt(cot, d_ref[...])
            last = pre_ref[rows, 1024:1152]
            gate = jnp.concatenate([pre_ref[rows, :512], last], axis=1)
            up = jnp.concatenate([pre_ref[rows, 512:1024], pltpu.roll(last, 64, 1)], axis=1)
            act, slope = gelu_parts(gate)
            save_ref[rows, :HID_PAD] = (act * up).astype(BF)
            d_gate = d_product * up * slope
            d_up = d_product * act
            d_last = d_gate[:, 512:] + pltpu.roll(d_up[:, 512:], 64, 1)
            d_pre = jnp.concatenate([d_gate[:, :512], d_up[:, :512], d_last], axis=1).astype(BF)
            save_ref[rows, HID_PAD:] = d_pre
            term = nt(d_pre, w_ref[...])
            part = term if part is None else part + term
        part_s[rows, :] = part.astype(BF)

    wait_all(start_out(pos, part_s, outs, copy_sems))


def mlp_out_kernel(pos, prod_mine, prod_theirs, d_mine, d_theirs, *refs):
    outs, part_s, copy_sems = refs[:4], refs[4], refs[5]
    for k in range(ROWS // STEP):
        rows = slice(k * STEP, k * STEP + STEP)
        part = nn(prod_mine[rows, :HID_PAD], d_mine[...]) + nn(prod_theirs[rows, :HID_PAD], d_theirs[...])
        part_s[rows, :] = part.astype(BF)
    wait_all(start_out(pos, part_s, outs, copy_sems))


def mlp_grads_kernel(*refs):
    xc_refs, save_refs, (out_ref, w_s, d_s) = refs[:2], refs[2:4], refs[4:]
    for k in range(WIDTH // STEP):
        cols = slice(STEP * k, STEP * k + STEP)
        grads = [tn(xc[:ROWS, cols], save[:, HID_PAD:]) for xc, save in zip(xc_refs, save_refs)]
        w_s[cols, :] = (grads[0] + grads[1]).astype(BF)
    for k in range(HID_PAD // 128):
        cols = slice(128 * k, 128 * k + 128)
        grads = [tn(save[:, cols], xc[ROWS:, :]) for xc, save in zip(xc_refs, save_refs)]
        d_s[cols, :] = grads[0] + grads[1]
    for p in range(16):
        for j in range(3):
            at = p * MLP_ROWS + 96 * j
            out_ref[at : at + 96, :] = w_s[96 * p : 96 * p + 96, 384 * j : 384 * j + 384]
        for j in range(4):
            at = p * MLP_ROWS + 288 + 48 * j
            out_ref[at : at + 48, :] = d_s[36 * p : 36 * p + 48, 384 * j : 384 * j + 384].astype(BF)


def mixed_backward_kernel(pos, *refs):
    d_refs, (o_mine, o_theirs, yp_ref, hid_mine, hid_theirs, rs_ref) = refs[:4], refs[4:10]
    mine_ref, theirs_ref, d_s, copy_sems = refs[10:]
    wait_all(start_in(pos, d_refs, d_s, copy_sems))
    sides = ((o_mine, hid_mine, mine_ref), (o_theirs, hid_theirs, theirs_ref))
    for k in range(ROWS // STEP):
        rows = slice(k * STEP, k * STEP + STEP)
        here = d_s[rows, :]
        scale = rs_ref[rows, 0:1]
        for h, (o_ref, hid_ref, out_ref) in enumerate(sides):
            d_mixed = nt(here, o_ref[...])
            act, slope = gelu_parts(yp_ref[rows, CHAN * h : CHAN * h + CHAN])
            out_ref[rows, :CHAN] = (d_mixed * act).astype(BF)
            out_ref[rows, CHAN:] = (d_mixed * hid_ref[rows, :].astype(F32) * slope * scale).astype(BF)


def out_grads_kernel(mix_ref, d_ref, mine_ref, theirs_ref):
    theirs_ref[...] = tn(mix_ref[:, CHAN:], d_ref[...]).astype(BF)
    mine_ref[...] = tn(mix_ref[:, :CHAN], d_ref[...]).astype(BF)


def chain_backward_kernel(pos, *refs):
    (mine_ref, theirs_ref, c_ref, saved_ref) = refs[:4]
    dx_mine, dx_theirs, gs_ref, dh_s, cum_s, dc_s, dx_s, acc_s, a_ref = refs[4:]
    xl_ref, rg_ref, op_ref, hid_ref = saved_parts(saved_ref)
    small = small_rows(c_ref)
    gate_w = c_ref[:, 0:CHAN]
    decay = small[7:8, :]
    decay_scale = -8.0 * softplus(decay)
    for k in range(TOKENS // STEP):
        put_rows(a_ref, k * STEP, STEP, jnp.exp(decay_scale * rg_ref[k * STEP : k * STEP + STEP, :]))
    put_rows(a_ref, TOKENS, 8, jnp.zeros((8, CHAN), F32))
    for y in range(4):
        for rc, ref in enumerate((mine_ref, theirs_ref)):
            block = ref[BLOCK * y : BLOCK * y + BLOCK, :CHAN].astype(F32)
            at = pl.multiple_of(time_start(pos, y, rc), BLOCK)
            for k in (0, 1):
                side(dh_s, k)[pl.ds(at, BLOCK), :] = block[:, 128 * k : 128 * k + 128]
    state, product = chain(a_ref, 1, dh_s, cum_s, True)
    decay_slope = -8.0 * jax.nn.sigmoid(decay)
    acc_s[...] = jnp.zeros_like(acc_s)
    dc_s[TOKENS:, :] = jnp.zeros((8, CHAN), F32)
    later = [None] * 8
    entering = jnp.zeros((1, CHAN), F32)
    for k in reversed(range(8)):
        later[k] = entering
        entering = state[k : k + 1, :] + product[k : k + 1, :] * entering
    gate_grads = [jnp.zeros((128, CHAN), F32) for _ in (0, 1)]
    for k in range(8):
        lo = k * BLOCK
        rows = slice(lo, lo + BLOCK)
        state_grad = get_rows(dh_s, lo, BLOCK) + get_rows(cum_s, lo, BLOCK) * later[k]
        shifted = [xl_ref[lo + 8 - tap : lo + 8 - tap + BLOCK, :] for tap in range(4)]
        conv = small[4:5, :]
        for tap in range(4):
            conv = conv + small[tap : tap + 1, :] * shifted[tap]
        conv_low = conv.astype(BF)
        conv = conv_low.astype(F32)
        rg, op, a = rg_ref[rows, :], op_ref[rows, :], get_rows(a_ref, lo, BLOCK)
        root = jnp.sqrt(neg_expm1(2.0 * decay_scale * rg))
        pushed = state_grad * op
        d_log = a * (state_grad * hid_ref[lo + 7 : lo + 7 + BLOCK, :] - pushed * conv * a / root)
        d_rg = d_log * rg
        acc_s[7:8, :] += jnp.sum(d_rg, axis=0, keepdims=True) * decay_slope
        d_raw = decay_scale * d_rg * (1.0 - rg)
        d_open = pushed * root * conv * (1.0 - op)
        acc_s[5:6, :] += jnp.sum(d_raw, axis=0, keepdims=True)
        acc_s[6:7, :] += jnp.sum(d_open, axis=0, keepdims=True)
        d_raw, d_open = d_raw.astype(BF), d_open.astype(BF)
        back = []
        for h in (0, 1):
            cols = slice(128 * h, 128 * h + 128)
            d_block = jnp.concatenate([d_raw[:, cols], d_open[:, cols]], axis=1)
            gate_grads[h] = gate_grads[h] + tn(conv_low[:, cols], d_block)
            back.append(nt(d_block, gate_w[cols, :]))
        d_conv = pushed * root + jnp.concatenate(back, axis=1)
        dc_s[rows, :] = d_conv
        acc_s[4:5, :] += jnp.sum(d_conv, axis=0, keepdims=True)
        for tap in range(4):
            acc_s[tap : tap + 1, :] += jnp.sum(d_conv * shifted[tap], axis=0, keepdims=True)
    for k in range(8):
        lo = k * BLOCK
        d_x = small[0:1, :] * dc_s[lo : lo + BLOCK, :]
        for tap in range(1, 4):
            d_x = d_x + small[tap : tap + 1, :] * dc_s[lo + tap : lo + tap + BLOCK, :]
        dx_s[lo : lo + BLOCK, :] = d_x
    for y in range(4):
        for rc, ref in enumerate((dx_mine, dx_theirs)):
            at = pl.multiple_of(time_start(pos, y, rc), BLOCK)
            ref[BLOCK * y : BLOCK * y + BLOCK, :] = dx_s[pl.ds(at, BLOCK), :].astype(BF)
    for h in (0, 1):
        gs_ref[128 * h : 128 * h + 128, 0:256] = gate_grads[h].astype(BF)
    gs_ref[:, 256:384] = acc_s[...].T.astype(BF)


def normed_backward_kernel(pos, dx_mine, dx_theirs, dy_mine, dy_theirs, rs_ref, *refs):
    weights, outs, part_s, copy_sems = refs[:4], refs[4:8], refs[8], refs[9]
    for k in range(ROWS // STEP):
        rows = slice(k * STEP, k * STEP + STEP)
        scale = rs_ref[rows, 0:1]
        lows = [(dx_ref[rows, :].astype(F32) * scale).astype(BF) for dx_ref in (dx_mine, dx_theirs)]
        lows += [dy_mine[rows, CHAN:], dy_theirs[rows, CHAN:]]
        part_s[rows, :] = sum(nt(low, w_ref[...]) for low, w_ref in zip(lows, weights)).astype(BF)
    wait_all(start_out(pos, part_s, outs, copy_sems))


def cols_grads_kernel(*refs):
    x_refs, dx_refs, dy_refs, rs_ref = refs[:2], refs[2:4], refs[4:6], refs[6]
    go_mine, go_theirs, gs_ref, out_ref, wide_s, rest_s = refs[7:]
    rest_s[:, 0:WIDTH] = (go_mine[...].astype(F32) + go_theirs[...].astype(F32)).astype(BF)
    rest_s[:, WIDTH:C_WIDTH] = gs_ref[...]
    rest_s[:, C_WIDTH:] = jnp.zeros((CHAN, 8 * REST - C_WIDTH), BF)
    wide = x_refs[1][...].astype(F32)
    scales = (rs_ref[:, 0:1], lax.rsqrt(jnp.mean(wide * wide, axis=-1, keepdims=True) + EPS))
    lows = [
        jnp.concatenate([(dx[...].astype(F32) * scale).astype(BF), dy[:, CHAN:]], axis=1)
        for dx, dy, scale in zip(dx_refs, dy_refs, scales)
    ]
    for k in range(WIDTH // STEP):
        rows = slice(STEP * k, STEP * k + STEP)
        wide_s[rows, :] = tn(x_refs[0][:, rows], lows[0]) + tn(x_refs[1][:, rows], lows[1])
    for i in range(128):
        block = [wide_s[12 * i : 12 * i + 12, 128 * t : 128 * t + 128] for t in range(4)]
        out_ref[i, 0:COLS_ROWS, :] = jnp.concatenate(block).astype(BF)
        few = slice(16 * (i // 8), 16 * (i // 8) + 16)
        for t in range(2):
            at = REST * (i % 8) + 128 * t
            out_ref[i, COLS_ROWS + 16 * t : COLS_ROWS + 16 * t + 16, :] = rest_s[few, at : at + 128]


def add_terms(terms):
    out = terms[0][...].astype(F32)
    for term in terms[1:]:
        out = out + term[...].astype(F32)
    return out


def residual_kernel(x_ref, *refs):
    terms, (res_ref, scale_ref, low_ref) = refs[:4], refs[4:]
    residual = x_ref[...].astype(F32) + add_terms(terms)
    scale = lax.rsqrt(jnp.mean(residual * residual, axis=-1, keepdims=True) + EPS)
    res_ref[...] = residual
    scale_ref[...] = jnp.broadcast_to(scale, (BLOCK, 128))
    low_ref[...] = (residual * scale).astype(BF)


def d_residual_kernel(cot_ref, res_ref, scale_ref, *refs):
    terms, (d_ref, low_ref) = refs[:4], refs[4:]
    d_normed = add_terms(terms)
    scale = scale_ref[:, 0:1]
    normed = res_ref[...] * scale
    along = jnp.mean(normed * d_normed, axis=-1, keepdims=True)
    d_residual = cot_ref[...].astype(F32) + scale * (d_normed - normed * along)
    d_ref[...] = d_residual
    low_ref[...] = d_residual.astype(BF)


def input_grad_kernel(x_ref, d_ref, *refs):
    terms, out_ref = refs[:4], refs[4]
    scaled = add_terms(terms)
    x = x_ref[...].astype(F32)
    power = 1.0 / (jnp.mean(x * x, axis=-1, keepdims=True) + EPS)
    along = jnp.mean(x * scaled, axis=-1, keepdims=True) * power
    out_ref[...] = (d_ref[...] + scaled - x * along).astype(BF)


def layer_out_kernel(res_ref, *refs):
    terms, out_ref = refs[:4], refs[4]
    out_ref[...] = (res_ref[...] + add_terms(terms)).astype(BF)


def dp_total(got_ref, lo, count):
    out = got_ref[0, lo : lo + count, :].astype(F32)
    for k in range(1, 16):
        out = out + got_ref[k, lo : lo + count, :].astype(F32)
    return out


def finish_cols_kernel(got_ref, gain_ref, x_ref, y_ref, gx_ref, gy_ref, gain_grad_ref, wide_s):
    for s in range(8):
        wide_s[COLS_ROWS * s : COLS_ROWS * s + COLS_ROWS, :] = dp_total(got_ref, SUM_ROWS * s, COLS_ROWS)
    gain = column(gain_ref)
    along = jnp.zeros((12, 128), F32)
    for s in range(8):
        for t in range(4):
            at = CHAN * s + 128 * (t % 2)
            lo = COLS_ROWS * s + 12 * t
            grad = wide_s[lo : lo + 12, :]
            w_ref, g_ref = (x_ref, gx_ref) if t < 2 else (y_ref, gy_ref)
            along = along + grad * w_ref[:, at : at + 128].astype(F32)
            g_ref[:, at : at + 128] = grad * gain
    gain_grad_ref[...] = as_row(jnp.sum(along, axis=1, keepdims=True))


def mlp_back_kernel(got_ref, cols_ref, down_ref, wide_s):
    for j in range(3):
        wide_s[:, 384 * j : 384 * j + 384] = got_ref[96 * j : 96 * j + 96, :].astype(F32)
    for s in range(8):
        block = jnp.concatenate([wide_s[12 * s : 12 * s + 12, :], jnp.zeros((4, GATED), F32)])
        cols_ref[s] = block.astype(BF)
    for j in range(4):
        down_ref[:, 384 * j : 384 * j + 384] = got_ref[288 + 48 * j : 336 + 48 * j, :]


def rest_back_kernel(cols_ref, got_ref, out_ref):
    out_ref[:, :, :GATED] = cols_ref[...]
    for s in range(8):
        for t in range(2):
            tile = dp_total(got_ref, SUM_ROWS * s + COLS_ROWS + 16 * t, 16)
            out_ref[s, :, GATED + 128 * t : GATED + 128 * t + 128] = tile.astype(BF)


def mlp_finish_kernel(*refs):
    got_ref, gain_ref, gate_ref, up_ref, g_gate_ref, g_up_ref, gain_grad_ref = refs
    gain = column(gain_ref)
    along = jnp.zeros((12, 1), F32)
    for s in range(8):
        block = got_ref[s, :, :GATED].astype(F32)[:12]
        lo = HID * s
        cols = slice(lo, lo + HID)
        grad_gate = jnp.concatenate([block[:, :512], block[:, 1024:1088]], axis=1)
        grad_up = jnp.concatenate([block[:, 512:1024], block[:, 1088:]], axis=1)
        terms = grad_gate * gate_ref[:, cols].astype(F32) + grad_up * up_ref[:, cols].astype(F32)
        along = along + jnp.sum(terms, axis=1, keepdims=True)
        g_gate_ref[:, cols] = grad_gate * gain
        g_up_ref[:, cols] = grad_up * gain
    gain_grad_ref[...] = as_row(along)


def rest_join_kernel(got_ref, down_ref, out_ref):
    for s in range(8):
        out_ref[:, REST * s : REST * s + REST] = got_ref[s, :, GATED:]
    for j in range(3):
        out_ref[:, 8 * REST + WIDTH * j : 8 * REST + WIDTH * j + WIDTH] = down_ref[16 * j : 16 * j + 16, :]


def finish_rest_kernel(got_ref, out_ref, gate_w_ref, taps_ref, bias_ref, gate_bias_ref, decay_ref, down_ref):
    for j in range(3):
        rows = min(16, 36 - 16 * j)
        tile = got_ref[:, 8 * REST + WIDTH * j : 8 * REST + WIDTH * j + WIDTH]
        down_ref[16 * j : 16 * j + rows, :] = tile.astype(F32)[:rows]
    out_ref[...] = got_ref[:, 0:WIDTH].astype(F32)
    gate_w_ref[...] = got_ref[:, 1536:1792].astype(F32)
    small = got_ref[:, 1792:1920].astype(F32)
    rows = [as_row(small[:, k : k + 1]) for k in range(8)]
    for k in range(4):
        taps_ref[k : k + 1, :] = rows[k]
    bias_ref[...] = rows[4]
    for k in range(2):
        gate_bias_ref[k : k + 1, :] = rows[5 + k]
    decay_ref[...] = rows[7]


def shape(dims, dtype):
    return jax.ShapeDtypeStruct(dims, dtype)


def sems(count):
    return pltpu.SemaphoreType.DMA((count,))


def size(dims, dtype):
    return math.prod(dims) * jnp.dtype(dtype).itemsize


def call(kernel, args, outs, scratch=(), any_args=(), any_outs=(), micros=0, more=8):
    held = sum(size(a.shape, a.dtype) for k, a in enumerate(args) if k not in any_args)
    held += sum(size(*o) for k, o in enumerate(outs) if k not in any_outs)
    held += sum(size(s.shape, s.dtype) for s in scratch if s.memory_space == pltpu.VMEM)
    in_specs = [SMEM if a.dtype == jnp.int32 else HBM if k in any_args else VMEM for k, a in enumerate(args)]
    return pl.pallas_call(
        kernel,
        name=kernel.__name__.removesuffix("_kernel"),
        in_specs=in_specs,
        out_specs=[ANY if k in any_outs else VMEM for k in range(len(outs))],
        out_shape=[shape(*o) for o in outs],
        scratch_shapes=scratch,
        cost_estimate=pl.CostEstimate(flops=int(micros * 10**9), bytes_accessed=0, transcendentals=0),
        compiler_params=pltpu.CompilerParams(vmem_limit_bytes=min(held + (more << 20), 60 << 20)),
    )(*args)


PART = ((BLOCK, WIDTH), BF)
PARTS = [PART] * 4
PART_S = pltpu.VMEM((ROWS, WIDTH), BF)
CHAIN_S = pltpu.VMEM((2 * TOKENS, 128), F32)


def per_device(
    inputs,
    cotangent,
    resets,
    start_state,
    conv_history,
    norm_gain,
    proj_x,
    proj_y,
    conv_taps,
    conv_bias,
    gate_weight,
    gate_bias,
    decay_param,
    proj_out,
    mlp_gain,
    mlp_gate,
    mlp_up,
    mlp_down,
):
    pos = jnp.stack([lax.axis_index(a) for a in DP_SEQ]).astype(jnp.int32)
    flat_in = inputs[0]
    flat_cot = cotangent[0]
    gain_one = norm_gain[None]
    gain_two = mlp_gain[None]

    (rest,) = call(
        pack_rows_kernel,
        (proj_out, gate_weight, conv_taps.T, conv_bias[None], gate_bias.T, decay_param[None]),
        [((16, C_WIDTH), BF)],
        more=60,
    )
    rest, late_x, late_down = tied(rest, proj_x, mlp_down)
    rest = transposed_devices(rest, False)
    blocks = call(
        pack_cols_kernel,
        (pos, gain_one, gain_two, late_x, proj_y, mlp_gate, mlp_up),
        [((16, SENT), BF)] * 8,
        [pltpu.VMEM((8, 16, SENT), F32)],
        more=60,
    )
    early, late = call(
        shard_kernel,
        (pos, *exchanged(blocks), rest),
        [((EARLY, 128), BF), ((LATE, 128), BF)],
        [pltpu.VMEM((8, 16, SENT), F32), pltpu.VMEM((96, SENT), F32)],
    )
    late = lax.all_gather(late, DP, axis=0, tiled=True)
    early, early_in, late_down = tied(early, flat_in, late_down)
    x_pieces = gather_rows(early_in)
    down = transposed_devices(late_down, False)
    early = lax.all_gather(early, DP, axis=0, tiled=True)
    early, x_pieces, down = tied(early, x_pieces, down)
    x_mine, c_mine = call(early_unpack_kernel, (early,), [((WIDTH, CHAN), BF), ((CHAN, SMALL), BF)])
    (down,) = call(down_pack_kernel, (down,), [((DOWN_ROWS, MLP_LANES), BF)])
    x_mine, late_cot, down = tied(x_mine, flat_cot, down)
    down = lax.all_gather(down, DP, axis=0, tiled=True)
    x_theirs = swapped(x_mine)
    c_near = [hop(late_cot, "y", r) for r in PIECES[1:3]]

    keep = (1 - resets).astype(F32)
    place = lax.axis_index(SEQ) * CHAN
    history = lax.dynamic_slice(conv_history[0].astype(F32), (0, place), (3, CHAN)) * keep
    initial = lax.dynamic_slice(start_state, (0, place), (1, CHAN)) * keep
    edges = jnp.concatenate([jnp.zeros((5, CHAN), F32), history, jnp.zeros((7, CHAN), F32), initial])
    xl_mine, xl_theirs, x_all, rs = call(
        in_proj_kernel,
        (pos, *x_pieces, x_mine, x_theirs),
        [((ROWS, CHAN), BF)] * 2 + [((ROWS, WIDTH), BF), ((ROWS, 128), F32)],
        [sems(4)],
        micros=8,
    )
    xl_got, c_near, late_cot = tied(swapped(xl_theirs), c_near, late_cot)
    c_far = hop(late_cot, "y", PIECES[3])
    hid_mine, hid_theirs, saved = call(
        recurrence_kernel,
        (pos, xl_mine, xl_got, c_mine, edges),
        [((ROWS, CHAN), BF)] * 2 + [((4 * (TOKENS + 8), CHAN), F32)],
        [CHAIN_S, CHAIN_S, CHAIN_S],
        micros=8,
    )
    hid_theirs = swapped(hid_theirs)
    hid_mine, c_far, late = tied(hid_mine, c_far, late)
    c_pieces = [flat_cot, *c_near, c_far]
    y_mine, o_mine = call(
        late_unpack_kernel,
        (late,),
        [((WIDTH, CHAN), BF), ((CHAN, WIDTH), BF)],
        [pltpu.VMEM((16 * COLS, 128), BF), sems(16)],
        any_args=range(1),
    )
    y_theirs, o_theirs = swapped(y_mine), swapped(o_mine)
    (yp,) = call(y_proj_kernel, (x_all, rs, y_mine, y_theirs), [((ROWS, 2 * CHAN), F32)], micros=8)
    *parts, mix = call(
        out_proj_kernel,
        (pos, hid_mine, hid_theirs, yp, o_mine, o_theirs),
        PARTS + [((ROWS, 2 * CHAN), BF)],
        [PART_S, sems(4)],
        any_outs=range(4),
        micros=1.2,
    )
    terms = scatter_rows(parts)
    _, late = tied(parts, late)
    (w_up,) = call(
        cols_unpack_kernel,
        (late,),
        [((WIDTH, GATED), BF)],
        [pltpu.VMEM((16 * 864, 128), BF), sems(16)],
        any_args=range(1),
    )
    up_theirs = swapped(w_up)
    terms, w_up = tied(terms, w_up)
    residual, scale_two, normed_two = call(
        residual_kernel, (flat_in, *terms), [((BLOCK, WIDTH), F32), ((BLOCK, 128), F32), PART], micros=30
    )

    _, down = tied(normed_two, down)
    (w_down,) = call(down_unpack_kernel, (down,), [((HID_PAD, WIDTH), BF)], [pltpu.VMEM((HID, WIDTH), F32)])
    down_theirs = swapped(w_down)
    tokens, pre_mine, pre_theirs = call(
        mlp_pre_kernel,
        (pos, *gather_rows(normed_two), *c_pieces, w_up, up_theirs),
        [((2 * ROWS, WIDTH), BF)] + [((ROWS, GATED), F32)] * 2,
        [sems(8)],
        micros=20,
    )
    tokens_got = swapped(tokens)
    *parts, save_mine, save_theirs = call(
        mlp_kernel,
        (pos, tokens, pre_mine, pre_theirs, w_up, w_down, up_theirs, down_theirs),
        PARTS + [((ROWS, HID_PAD + GATED), BF)] * 2,
        [PART_S, sems(4)],
        any_outs=range(4),
        micros=5,
    )
    out_parts = call(
        mlp_out_kernel,
        (pos, save_mine, save_theirs, w_down, down_theirs),
        PARTS,
        [PART_S, sems(4)],
        any_outs=range(4),
        micros=15,
    )
    terms = scatter_rows(parts)
    save_got = swapped(save_theirs)
    save_got, out_parts = tied(save_got, out_parts)
    (mlp_grads,) = call(
        mlp_grads_kernel,
        (tokens, tokens_got, save_mine, save_got),
        [((16 * MLP_ROWS, MLP_LANES), BF)],
        [pltpu.VMEM((WIDTH, GATED), BF), pltpu.VMEM((HID_PAD, WIDTH), F32)],
        micros=15,
    )
    terms, mlp_grads = tied(terms, mlp_grads)
    mlp_sum = lax.psum_scatter(mlp_grads, DP, scatter_dimension=0, tiled=True)
    d_residual, d_out = call(
        d_residual_kernel, (flat_cot, residual, scale_two, *terms), [((BLOCK, WIDTH), F32), PART]
    )

    d_out, late_x_all = tied(d_out, x_all)
    d_pieces, all_theirs = tied(gather_rows(d_out), swapped(late_x_all))
    back_mine, back_theirs, d_all = call(
        mixed_backward_kernel,
        (pos, *d_pieces, o_mine, o_theirs, yp, hid_mine, hid_theirs, rs),
        [((ROWS, 2 * CHAN), BF)] * 2 + [((ROWS, WIDTH), BF)],
        [sems(4)],
        micros=2,
    )
    back_got = swapped(back_theirs)
    dx_mine, dx_theirs, g_small = call(
        chain_backward_kernel,
        (pos, back_mine, back_got, c_mine, saved),
        [((ROWS, CHAN), BF)] * 2 + [((CHAN, 384), BF)],
        [
            CHAIN_S,
            CHAIN_S,
            pltpu.VMEM((TOKENS + 8, CHAN), F32),
            pltpu.VMEM((TOKENS, CHAN), F32),
            pltpu.VMEM((128, CHAN), F32),
            pltpu.VMEM((2 * TOKENS + 16, 128), F32),
        ],
        micros=20,
    )
    dx_got = swapped(dx_theirs)
    parts = call(
        normed_backward_kernel,
        (pos, dx_mine, dx_got, back_mine, back_theirs, rs, x_mine, x_theirs, y_mine, y_theirs),
        PARTS,
        [PART_S, sems(4)],
        any_outs=range(4),
    )
    terms = scatter_rows(parts)
    _, late_mix = tied(parts, mix)
    go_mine, go_theirs = call(out_grads_kernel, (late_mix, d_all), [((CHAN, WIDTH), BF)] * 2)
    (g_cols,) = call(
        cols_grads_kernel,
        (x_all, all_theirs, dx_mine, dx_theirs, back_mine, back_got, rs, go_mine, swapped(go_theirs), g_small),
        [((128, SUM_ROWS, 128), BF)],
        [pltpu.VMEM((WIDTH, 2 * CHAN), F32), pltpu.VMEM((CHAN, 8 * REST), BF)],
    )
    g_cols = lax.all_to_all(g_cols, DP_SEQ, 0, 0, tiled=True).reshape(16, 8 * SUM_ROWS, 128)
    terms, mlp_sum = tied(terms, mlp_sum)
    blocks, down_back = call(
        mlp_back_kernel,
        (mlp_sum,),
        [((8, 16, GATED), BF), ((48, WIDTH), BF)],
        [pltpu.VMEM((96, GATED), F32)],
        micros=100,
    )
    (input_grad,) = call(input_grad_kernel, (flat_in, d_residual, *terms), [PART])
    (blocks,) = call(rest_back_kernel, (blocks, g_cols), [((8, 16, GATED + REST), BF)])
    blocks = lax.all_to_all(blocks, SEQ, 0, 0, tiled=True)
    out_parts, _ = tied(out_parts, terms)
    out_terms = scatter_rows(out_parts)
    grad_x, grad_y, grad_norm_gain = call(
        finish_cols_kernel,
        (g_cols, gain_one, proj_x, proj_y),
        [((12, 8 * CHAN), F32)] * 2 + [((1, 12), F32)],
        [pltpu.VMEM((8 * COLS_ROWS, 128), F32)],
    )
    blocks, input_grad, grad_x = tied(blocks, input_grad, grad_x)
    (g_rest,) = call(rest_join_kernel, (blocks, down_back), [((16, 8 * REST + 3 * WIDTH), BF)])
    g_rest = transposed_devices(g_rest, True)
    grad_gate, grad_up, grad_mlp_gain = call(
        mlp_finish_kernel,
        (blocks, gain_two, mlp_gate, mlp_up),
        [((12, 8 * HID), F32)] * 2 + [((1, 12), F32)],
    )
    (layer_out,) = call(layer_out_kernel, (residual, *out_terms), [PART])
    g_rest, grad_gate, layer_out = tied(g_rest, grad_gate, layer_out)
    grad_out, grad_gate_w, grad_taps, grad_conv_bias, grad_gate_bias, grad_decay, grad_down = call(
        finish_rest_kernel,
        (g_rest,),
        [
            ((16, WIDTH), F32),
            ((16, CHAN), F32),
            ((4, 16), F32),
            ((1, 16), F32),
            ((2, 16), F32),
            ((1, 16), F32),
            ((36, WIDTH), F32),
        ],
    )
    return (
        layer_out[None],
        input_grad[None],
        grad_norm_gain[0],
        grad_x,
        grad_y,
        grad_taps.T,
        grad_conv_bias[0],
        grad_gate_w,
        grad_gate_bias.T,
        grad_decay[0],
        grad_out,
        grad_mlp_gain[0],
        grad_gate,
        grad_up,
        grad_down,
    )


def solution(mesh):
    finer = Mesh(mesh.devices.reshape(4, 4, 4, 2), DP_SEQ)
    rows = P(DP_SEQ, None)
    line = P(DP_SEQ)
    tokens = P(DP, SEQ, None)
    in_specs = (
        tokens,
        tokens,
        P(DP),
        P(DP, None),
        P(DP, None, None),
        line,
        rows,
        rows,
        rows,
        line,
        rows,
        rows,
        line,
        rows,
        line,
        rows,
        rows,
        rows,
    )
    out_specs = (
        tokens,
        tokens,
        line,
        rows,
        rows,
        rows,
        line,
        rows,
        rows,
        line,
        rows,
        line,
        rows,
        rows,
        rows,
    )
    return jax.shard_map(per_device, mesh=finer, in_specs=in_specs, out_specs=out_specs, check_vma=False)
```

```python
import math

import jax
import jax.numpy as jnp
from jax import lax
from jax.experimental import pallas as pl
from jax.experimental.pallas import tpu as pltpu
from jax.sharding import Mesh
from jax.sharding import PartitionSpec as P

BF = jnp.bfloat16
F32 = jnp.float32
EPS = 1e-06
GELU_C = 0.7978845608028654
GELU_K = 0.044715

TOKENS = 1024
ROWS = 512
BLOCK = 128
WIDTH = 1536
CHAN = 256
HID = 576
HID_PAD = 640
GATED = 2 * HID
STEP = 256
C_WIDTH = 1920
SENT = 2 * CHAN + GATED
SMALL = 384
EARLY = 240
COLS = 384
LATE = 1248
DOWN_ROWS = 192
COLS_ROWS = 48
SUM_ROWS = 80
REST = 256
MLP_ROWS = 480
MLP_LANES = 384

DP = ("z", "x")
SEQ = ("y", "c")
DP_SEQ = ("z", "x", "y", "c")

ANY = pl.BlockSpec(memory_space=pl.ANY)
HBM = pl.BlockSpec(memory_space=pltpu.HBM)
VMEM = pl.BlockSpec(memory_space=pltpu.VMEM)
SMEM = pl.BlockSpec(memory_space=pltpu.SMEM)

PIECES = (0, 1, 3, 2)
PLACES = [(ry, rc) for rc in (0, 1) for ry in (0, 2, 1, 3)]


def hop(value, axis, distance):
    size = lax.axis_size(axis)
    return lax.ppermute(value, axis, [(i, (i - distance) % size) for i in range(size)])


def added(one, two):
    return (one.astype(F32) + two.astype(F32)).astype(BF)


def swapped(value):
    return hop(value, "c", 1)


def gather_rows(block):
    return [block] + [hop(block, "y", r) for r in PIECES[1:]]


def scatter_rows(parts):
    return [parts[0]] + [hop(parts[r], "y", 4 - r) for r in (2, 1, 3)]


def tied(*values):
    return lax.optimization_barrier(values)


def transposed_devices(value, back):
    pairs = [(16 * s + d, 8 * d + s) for s in range(8) for d in range(16)]
    return lax.ppermute(value, DP_SEQ, [(b, a) for a, b in pairs] if back else pairs)


def exchanged(blocks):
    out = []
    for (ry, rc), block in zip(PLACES, blocks):
        route = [(2 * y + c, 2 * ((y + ry) % 4) + (c + rc) % 2) for y in range(4) for c in range(2)]
        out.append(lax.ppermute(block, SEQ, route) if (ry, rc) != (0, 0) else block)
    return out


def nn(a, b):
    return jnp.dot(a, b, preferred_element_type=F32)


def nt(a, b):
    return lax.dot_general(a, b, (((1,), (1,)), ((), ())), preferred_element_type=F32)


def tn(a, b):
    return lax.dot_general(a, b, (((0,), (0,)), ((), ())), preferred_element_type=F32)


def gelu_parts(v):
    sq = v * v
    t = jnp.tanh(GELU_C * v * (1.0 + GELU_K * sq))
    half = 0.5 * (1.0 + t)
    slope = half + 0.5 * v * (1.0 - t * t) * (GELU_C * (1.0 + 3.0 * GELU_K * sq))
    return v * half, slope


def neg_expm1(v):
    series = 1.0 + v * (1.0 / 7.0)
    for k in (6, 5, 4, 3, 2):
        series = 1.0 + v * (1.0 / k) * series
    return jnp.where(v > -0.35, -v * series, 1.0 - jnp.exp(v))


def softplus(v):
    e = jnp.exp(-jnp.abs(v))
    series = e * (1.0 - e * (1 / 2 - e * (1 / 3 - e * (1 / 4 - e * (1 / 5 - e * (1 / 6))))))
    return jnp.maximum(v, 0.0) + jnp.where(e < 0.05, series, jnp.log(1.0 + e))


def column(row_ref):
    n = row_ref.shape[1]
    square = jnp.broadcast_to(row_ref[...].astype(F32), (n, n))
    same = lax.broadcasted_iota(jnp.int32, (n, n), 0) == lax.broadcasted_iota(jnp.int32, (n, n), 1)
    return jnp.sum(jnp.where(same, square, 0.0), axis=1, keepdims=True)


def as_row(col):
    n = col.shape[0]
    square = jnp.broadcast_to(col, (n, n))
    same = lax.broadcasted_iota(jnp.int32, (n, n), 0) == lax.broadcasted_iota(jnp.int32, (n, n), 1)
    return jnp.sum(jnp.where(same, square, 0.0), axis=0, keepdims=True)


def place_of(pos, ry, rc):
    return lax.rem(pos[2] + ry, 4) * 2 + lax.rem(pos[3] + rc, 2)


def block_rows(pos, ry):
    return pl.ds(pl.multiple_of(lax.rem(pos[2] + ry, 4) * BLOCK, BLOCK), BLOCK)


def time_start(pos, y, rc):
    return (2 * y + lax.rem(pos[3] + rc, 2)) * BLOCK


def start_loads(pairs, sems, first):
    copies = []
    for k, (ref, scratch) in enumerate(pairs):
        copies.append(pltpu.make_async_copy(ref, scratch, sems.at[first + k]))
        copies[-1].start()
    return copies


def start_in(pos, refs, scratch, sems, first=0):
    return start_loads([(ref, scratch.at[block_rows(pos, ry), :]) for ref, ry in zip(refs, PIECES)], sems, first)


def start_out(pos, scratch, refs, sems, first=0):
    return start_loads([(scratch.at[block_rows(pos, r), :], refs[r]) for r in range(4)], sems, first)


def wait_all(copies):
    for copy in copies:
        copy.wait()


def small_rows(c_ref):
    return c_ref[:, CHAN:SMALL].astype(F32).T


def scan_chunks(step, carry):
    def four(k, carry):
        for j in range(4):
            carry = step(k * 4 + j, carry)
        return carry

    return lax.fori_loop(0, BLOCK // 4, four, carry)


def chunk_rows(t):
    return pl.ds(t, 8, stride=BLOCK)


def side(ref, lanes):
    rows = ref.shape[0] // 2
    return ref.at[lanes * rows : (lanes + 1) * rows, :]


def get_rows(ref, lo, count):
    return jnp.concatenate([side(ref, k)[lo : lo + count, :] for k in (0, 1)], axis=1)


def put_rows(ref, lo, count, value):
    for k in (0, 1):
        side(ref, k)[lo : lo + count, :] = value[:, 128 * k : 128 * k + 128]


def chain(mult_ref, ahead, add_ref, product_ref, backward):
    def step(t, carry):
        t = BLOCK - 1 - t if backward else t
        out = []
        for k in (0, 1):
            state, product = carry[2 * k : 2 * k + 2]
            mult = side(mult_ref, k)[chunk_rows(t + ahead), :]
            state = mult * state + side(add_ref, k)[chunk_rows(t), :]
            product = product * mult
            side(add_ref, k)[chunk_rows(t), :] = state
            side(product_ref, k)[chunk_rows(t), :] = product
            out += [state, product]
        return tuple(out)

    zero, one = jnp.zeros((8, 128), F32), jnp.ones((8, 128), F32)
    left, left_p, right, right_p = scan_chunks(step, (zero, one, zero, one))
    return jnp.concatenate([left, right], axis=1), jnp.concatenate([left_p, right_p], axis=1)


def gated_cols(gate, up, s):
    lo = HID * s
    return [gate[:, lo : lo + 512], up[:, lo : lo + 512], gate[:, lo + 512 : lo + HID], up[:, lo + 512 : lo + HID]]


def pack_cols_kernel(pos, gain_one, gain_two, x_ref, y_ref, gate_ref, up_ref, *refs):
    outs, blocks_s = refs[:8], refs[8]
    gain = column(gain_one)
    x, y = x_ref[...].astype(F32) * gain, y_ref[...].astype(F32) * gain
    gain = column(gain_two)
    gate, up = gate_ref[...].astype(F32) * gain, up_ref[...].astype(F32) * gain
    fill = jnp.zeros((4, SENT), F32)
    for s in range(8):
        cols = slice(CHAN * s, CHAN * s + CHAN)
        block = jnp.concatenate([x[:, cols], y[:, cols], *gated_cols(gate, up, s)], axis=1)
        blocks_s[s] = jnp.concatenate([block, fill])
    for k, (ry, rc) in enumerate(PLACES):
        outs[k][...] = blocks_s[place_of(pos, ry, rc)].astype(BF)


def pack_rows_kernel(out_ref, gate_w_ref, taps_ref, bias_ref, gate_bias_ref, decay_ref, rest_ref):
    rest_ref[:, 0:WIDTH] = out_ref[...]
    rest_ref[:, 1536:1792] = gate_w_ref[...]
    lane = lax.broadcasted_iota(jnp.int32, (16, 128), 1)
    small = jnp.zeros((16, 128), F32)
    for k in range(4):
        small = jnp.where(lane == k, column(taps_ref.at[k : k + 1, :]), small)
    small = jnp.where(lane == 4, column(bias_ref), small)
    for k in range(2):
        small = jnp.where(lane == 5 + k, column(gate_bias_ref.at[k : k + 1, :]), small)
    rest_ref[:, 1792:1920] = jnp.where(lane == 7, column(decay_ref), small).astype(BF)


def shard_kernel(pos, *refs):
    blocks, (rest_ref, early_ref, late_ref, blocks_s, wide_s) = refs[:8], refs[8:]
    for k, (ry, rc) in enumerate(PLACES):
        blocks_s[place_of(pos, 4 - ry, rc)] = blocks[k][...].astype(F32)
    for s in range(8):
        wide_s[12 * s : 12 * s + 12, :] = blocks_s[s, 0:12, :]
    for t in range(2):
        early_ref[96 * t : 96 * t + 96, :] = wide_s[:, 128 * t : 128 * t + 128].astype(BF)
        late_ref[96 * t : 96 * t + 96, :] = wide_s[:, CHAN + 128 * t : CHAN + 128 * t + 128].astype(BF)
    for t in range(3):
        early_ref[192 + 16 * t : 208 + 16 * t, :] = rest_ref[:, WIDTH + 128 * t : WIDTH + 128 * t + 128]
    for t in range(12):
        late_ref[192 + 16 * t : 208 + 16 * t, :] = rest_ref[:, 128 * t : 128 * t + 128]
    for t in range(9):
        late_ref[COLS + 96 * t : COLS + 96 * t + 96, :] = wide_s[:, 512 + 128 * t : 640 + 128 * t].astype(BF)


def early_unpack_kernel(all_ref, w_ref, c_ref):
    for p in range(16):
        at = EARLY * p
        for t in range(2):
            w_ref[96 * p : 96 * p + 96, 128 * t : 128 * t + 128] = all_ref[at + 96 * t : at + 96 * t + 96, :]
        for t in range(3):
            lo = at + 192 + 16 * t
            c_ref[16 * p : 16 * p + 16, 128 * t : 128 * t + 128] = all_ref[lo : lo + 16, :]


def late_unpack_kernel(all_ref, w_ref, o_ref, late_s, copy_sems):
    slots = [late_s.at[COLS * p : COLS * p + COLS, :] for p in range(16)]
    loads = start_loads([(all_ref.at[LATE * p : LATE * p + COLS, :], slots[p]) for p in range(16)], copy_sems, 0)
    for p in range(16):
        loads[p].wait()
        at = COLS * p
        for t in range(2):
            w_ref[96 * p : 96 * p + 96, 128 * t : 128 * t + 128] = late_s[at + 96 * t : at + 96 * t + 96, :]
        for t in range(12):
            lo = at + 192 + 16 * t
            o_ref[16 * p : 16 * p + 16, 128 * t : 128 * t + 128] = late_s[lo : lo + 16, :]


def cols_unpack_kernel(all_ref, w_ref, cols_s, copy_sems):
    slots = [cols_s.at[864 * p : 864 * p + 864, :] for p in range(16)]
    ends = [(all_ref.at[LATE * p + COLS : LATE * p + LATE, :], slots[p]) for p in range(16)]
    loads = start_loads(ends, copy_sems, 0)
    for p in range(16):
        loads[p].wait()
        for t in range(9):
            at = 864 * p + 96 * t
            w_ref[96 * p : 96 * p + 96, 128 * t : 128 * t + 128] = cols_s[at : at + 96, :]


def down_pack_kernel(down_ref, out_ref):
    down = jnp.concatenate([down_ref[...].astype(F32), jnp.zeros((12, WIDTH), F32)]).astype(BF)
    for j in range(4):
        out_ref[48 * j : 48 * j + 48, :] = down[:, 384 * j : 384 * j + 384]


def down_unpack_kernel(all_ref, d_ref, wide_s):
    for p in range(16):
        for j in range(4):
            at = p * DOWN_ROWS + 48 * j
            wide_s[36 * p : 36 * p + 36, 384 * j : 384 * j + 384] = all_ref[at : at + 48, :].astype(F32)[:36]
    d_ref[0:HID, :] = wide_s[...].astype(BF)
    d_ref[HID:, :] = jnp.zeros((HID_PAD - HID, WIDTH), BF)


def in_proj_kernel(pos, *refs):
    x_refs, w_mine, w_theirs = refs[:4], refs[4], refs[5]
    xl_mine, xl_theirs, x_s, rs_ref, copy_sems = refs[6:]
    wait_all(start_in(pos, x_refs, x_s, copy_sems))
    for k in range(ROWS // STEP):
        rows = slice(k * STEP, k * STEP + STEP)
        here = x_s[rows, :]
        wide = here.astype(F32)
        scale = lax.rsqrt(jnp.mean(wide * wide, axis=-1, keepdims=True) + EPS)
        rs_ref[rows, :] = jnp.broadcast_to(scale, (STEP, 128))
        xl_theirs[rows, :] = (nn(here, w_theirs[...]) * scale).astype(BF)
        xl_mine[rows, :] = (nn(here, w_mine[...]) * scale).astype(BF)


def y_proj_kernel(x_ref, rs_ref, w_mine, w_theirs, yp_ref):
    for k in range(ROWS // STEP):
        rows = slice(k * STEP, k * STEP + STEP)
        scale = rs_ref[rows, 0:1]
        yp_ref[rows, :CHAN] = nn(x_ref[rows, :], w_mine[...]) * scale
        yp_ref[rows, CHAN:] = nn(x_ref[rows, :], w_theirs[...]) * scale


def saved_parts(ref):
    return [ref.at[(TOKENS + 8) * k : (TOKENS + 8) * (k + 1), :] for k in range(4)]


def recurrence_kernel(pos, mine_ref, theirs_ref, c_ref, edge_ref, *refs):
    hid_mine, hid_theirs, saved_out, saved_ref, a_s, push_s, cum_s, copy_sems = refs
    xl_s, rg_s, op_s, hid_s = saved_parts(saved_ref)
    parts = list(zip((xl_s, rg_s, op_s, hid_s), saved_parts(saved_out)))
    xl_s[0:8, :] = edge_ref[0:8, :]
    hid_s[0:8, :] = edge_ref[8:16, :]
    for y in range(4):
        for rc, ref in enumerate((mine_ref, theirs_ref)):
            at = pl.multiple_of(8 + time_start(pos, y, rc), 8)
            xl_s[pl.ds(at, BLOCK), :] = ref[BLOCK * y : BLOCK * y + BLOCK, :].astype(F32)
    small = small_rows(c_ref)
    gate_w = c_ref[:, 0:CHAN]
    decay_scale = -8.0 * softplus(small[7:8, :])
    for k in range(TOKENS // STEP):
        lo = k * STEP
        conv = small[4:5, :]
        for tap in range(4):
            conv = conv + small[tap : tap + 1, :] * xl_s[lo + 8 - tap : lo + 8 - tap + STEP, :]
        conv = conv.astype(BF)
        raw = [nn(conv[:, 128 * h : 128 * h + 128], gate_w[128 * h : 128 * h + 128, :]) for h in (0, 1)]
        rg = jax.nn.sigmoid(jnp.concatenate([raw[0][:, :128], raw[1][:, :128]], axis=1) + small[5:6, :])
        op = jax.nn.sigmoid(jnp.concatenate([raw[0][:, 128:], raw[1][:, 128:]], axis=1) + small[6:7, :])
        log_a = decay_scale * rg
        put_rows(a_s, lo, STEP, jnp.exp(log_a))
        put_rows(push_s, lo, STEP, jnp.sqrt(neg_expm1(2.0 * log_a)) * op * conv.astype(F32))
        rg_s[lo : lo + STEP, :] = rg
        op_s[lo : lo + STEP, :] = op
    saves = start_loads(parts[:3], copy_sems, 0)
    state, product = chain(a_s, 0, push_s, cum_s, False)
    entering = edge_ref[15:16, :]
    for k in range(8):
        lo = k * BLOCK
        hidden = get_rows(push_s, lo, BLOCK) + get_rows(cum_s, lo, BLOCK) * entering
        entering = state[k : k + 1, :] + product[k : k + 1, :] * entering
        hid_s[8 + lo : 8 + lo + BLOCK, :] = hidden
    saves += start_loads(parts[3:], copy_sems, 3)
    for y in range(4):
        for rc, ref in enumerate((hid_mine, hid_theirs)):
            at = pl.multiple_of(8 + time_start(pos, y, rc), 8)
            ref[BLOCK * y : BLOCK * y + BLOCK, :] = hid_s[pl.ds(at, BLOCK), :].astype(BF)
    wait_all(saves)


def out_proj_kernel(pos, hid_mine, hid_theirs, yp_ref, o_mine, o_theirs, *refs):
    outs, mix_ref, part_s, sems = refs[:4], refs[4], refs[5], refs[6]
    for k in range(ROWS // STEP):
        rows = slice(k * STEP, k * STEP + STEP)
        act, _ = gelu_parts(yp_ref[rows, :])
        hidden = jnp.concatenate([hid_mine[rows, :], hid_theirs[rows, :]], axis=1)
        mixed = (hidden.astype(F32) * act).astype(BF)
        mix_ref[rows, :] = mixed
        part = nn(mixed[:, :CHAN], o_mine[...]) + nn(mixed[:, CHAN:], o_theirs[...])
        part_s[rows, :] = part.astype(BF)
    wait_all(start_out(pos, part_s, outs, sems))


def mlp_pre_kernel(pos, *refs):
    x_refs, c_refs, weights, (xc_ref, *pres), copy_sems = refs[:4], refs[4:8], refs[8:10], refs[10:13], refs[13]
    loads = start_in(pos, x_refs, xc_ref.at[:ROWS, :], copy_sems)
    later = start_in(pos, c_refs, xc_ref.at[ROWS:, :], copy_sems, 4)
    wait_all(loads)
    for k in range(ROWS // STEP):
        rows = slice(k * STEP, k * STEP + STEP)
        for w_ref, pre_ref in zip(weights, pres):
            pre_ref[rows, :] = nn(xc_ref[rows, :], w_ref[...])
    wait_all(later)


def mlp_kernel(pos, xc_ref, *refs):
    pres, weights, outs, saves, (part_s, copy_sems) = refs[:2], (refs[2:4], refs[4:6]), refs[6:10], refs[10:12], refs[12:]

    @pl.loop(0, ROWS // STEP)
    def _(k):
        rows = pl.ds(pl.multiple_of(k * STEP, STEP), STEP)
        cot = xc_ref[pl.ds(pl.multiple_of(ROWS + k * STEP, STEP), STEP), :]
        part = None
        for (w_ref, d_ref), pre_ref, save_ref in zip(weights, pres, saves):
            d_product = nt(cot, d_ref[...])
            last = pre_ref[rows, 1024:1152]
            gate = jnp.concatenate([pre_ref[rows, :512], last], axis=1)
            up = jnp.concatenate([pre_ref[rows, 512:1024], pltpu.roll(last, 64, 1)], axis=1)
            act, slope = gelu_parts(gate)
            save_ref[rows, :HID_PAD] = (act * up).astype(BF)
            d_gate = d_product * up * slope
            d_up = d_product * act
            d_last = d_gate[:, 512:] + pltpu.roll(d_up[:, 512:], 64, 1)
            d_pre = jnp.concatenate([d_gate[:, :512], d_up[:, :512], d_last], axis=1).astype(BF)
            save_ref[rows, HID_PAD:] = d_pre
            term = nt(d_pre, w_ref[...])
            part = term if part is None else part + term
        part_s[rows, :] = part.astype(BF)

    wait_all(start_out(pos, part_s, outs, copy_sems))


def mlp_out_kernel(pos, prod_mine, prod_theirs, d_mine, d_theirs, *refs):
    outs, part_s, copy_sems = refs[:4], refs[4], refs[5]
    for k in range(ROWS // STEP):
        rows = slice(k * STEP, k * STEP + STEP)
        part = nn(prod_mine[rows, :HID_PAD], d_mine[...]) + nn(prod_theirs[rows, :HID_PAD], d_theirs[...])
        part_s[rows, :] = part.astype(BF)
    wait_all(start_out(pos, part_s, outs, copy_sems))


def mlp_grads_kernel(*refs):
    xc_refs, save_refs, (out_ref, out_s, w_s, d_s, copy_sems) = refs[:2], refs[2:4], refs[4:]
    for k in range(HID_PAD // 128):
        cols = slice(128 * k, 128 * k + 128)
        grads = [tn(save[:, cols], xc[ROWS:, :]) for xc, save in zip(xc_refs, save_refs)]
        d_s[cols, :] = grads[0] + grads[1]
    saves = []
    for k in range(WIDTH // 384):
        cols = slice(384 * k, 384 * k + 384)
        grads = [tn(xc[:ROWS, cols], save[:, HID_PAD:]) for xc, save in zip(xc_refs, save_refs)]
        w_s[cols, :] = (grads[0] + grads[1]).astype(BF)
        for p in range(4 * k, 4 * k + 4):
            for j in range(3):
                at = p * MLP_ROWS + 96 * j
                out_s[at : at + 96, :] = w_s[96 * p : 96 * p + 96, 384 * j : 384 * j + 384]
            for j in range(4):
                at = p * MLP_ROWS + 288 + 48 * j
                out_s[at : at + 48, :] = d_s[36 * p : 36 * p + 48, 384 * j : 384 * j + 384].astype(BF)
        part = slice(4 * MLP_ROWS * k, 4 * MLP_ROWS * (k + 1))
        saves += start_loads(((out_s.at[part, :], out_ref.at[part, :]),), copy_sems, k)
    wait_all(saves)


def mixed_backward_kernel(pos, *refs):
    d_refs, (o_mine, o_theirs, yp_ref, hid_mine, hid_theirs, rs_ref) = refs[:4], refs[4:10]
    mine_ref, theirs_ref, d_s, copy_sems = refs[10:]
    wait_all(start_in(pos, d_refs, d_s, copy_sems))
    sides = ((o_mine, hid_mine, mine_ref), (o_theirs, hid_theirs, theirs_ref))
    for k in range(ROWS // STEP):
        rows = slice(k * STEP, k * STEP + STEP)
        here = d_s[rows, :]
        scale = rs_ref[rows, 0:1]
        for h, (o_ref, hid_ref, out_ref) in enumerate(sides):
            d_mixed = nt(here, o_ref[...])
            act, slope = gelu_parts(yp_ref[rows, CHAN * h : CHAN * h + CHAN])
            out_ref[rows, :CHAN] = (d_mixed * act).astype(BF)
            out_ref[rows, CHAN:] = (d_mixed * hid_ref[rows, :].astype(F32) * slope * scale).astype(BF)


def out_grads_kernel(mix_ref, d_ref, mine_ref, theirs_ref):
    theirs_ref[...] = tn(mix_ref[:, CHAN:], d_ref[...]).astype(BF)
    mine_ref[...] = tn(mix_ref[:, :CHAN], d_ref[...]).astype(BF)


def chain_backward_kernel(pos, *refs):
    (mine_ref, theirs_ref, c_ref, saved_ref) = refs[:4]
    dx_mine, dx_theirs, gs_ref, dh_s, cum_s, dc_s, dx_s, acc_s, a_ref, saved_s, copy_sems = refs[4:]
    xl_ref, rg_ref, op_ref, hid_ref = saved_parts(saved_s)
    order = (1, 0, 2, 3)
    loads = [(saved_parts(saved_ref)[k], saved_parts(saved_s)[k]) for k in order]
    loads = start_loads(loads, copy_sems, 0)
    small = small_rows(c_ref)
    gate_w = c_ref[:, 0:CHAN]
    decay = small[7:8, :]
    decay_scale = -8.0 * softplus(decay)
    for y in range(4):
        for rc, ref in enumerate((mine_ref, theirs_ref)):
            block = ref[BLOCK * y : BLOCK * y + BLOCK, :CHAN].astype(F32)
            at = pl.multiple_of(time_start(pos, y, rc), BLOCK)
            for k in (0, 1):
                side(dh_s, k)[pl.ds(at, BLOCK), :] = block[:, 128 * k : 128 * k + 128]
    loads[0].wait()
    for k in range(TOKENS // STEP):
        put_rows(a_ref, k * STEP, STEP, jnp.exp(decay_scale * rg_ref[k * STEP : k * STEP + STEP, :]))
    put_rows(a_ref, TOKENS, 8, jnp.zeros((8, CHAN), F32))
    state, product = chain(a_ref, 1, dh_s, cum_s, True)
    wait_all(loads[1:])
    decay_slope = -8.0 * jax.nn.sigmoid(decay)
    acc_s[...] = jnp.zeros_like(acc_s)
    dc_s[TOKENS:, :] = jnp.zeros((8, CHAN), F32)
    later = [None] * 8
    entering = jnp.zeros((1, CHAN), F32)
    for k in reversed(range(8)):
        later[k] = entering
        entering = state[k : k + 1, :] + product[k : k + 1, :] * entering
    gate_grads = [jnp.zeros((128, CHAN), F32) for _ in (0, 1)]
    for k in range(8):
        lo = k * BLOCK
        rows = slice(lo, lo + BLOCK)
        state_grad = get_rows(dh_s, lo, BLOCK) + get_rows(cum_s, lo, BLOCK) * later[k]
        shifted = [xl_ref[lo + 8 - tap : lo + 8 - tap + BLOCK, :] for tap in range(4)]
        conv = small[4:5, :]
        for tap in range(4):
            conv = conv + small[tap : tap + 1, :] * shifted[tap]
        conv_low = conv.astype(BF)
        conv = conv_low.astype(F32)
        rg, op, a = rg_ref[rows, :], op_ref[rows, :], get_rows(a_ref, lo, BLOCK)
        root = jnp.sqrt(neg_expm1(2.0 * decay_scale * rg))
        pushed = state_grad * op
        d_log = a * (state_grad * hid_ref[lo + 7 : lo + 7 + BLOCK, :] - pushed * conv * a / root)
        d_rg = d_log * rg
        acc_s[7:8, :] += jnp.sum(d_rg, axis=0, keepdims=True) * decay_slope
        d_raw = decay_scale * d_rg * (1.0 - rg)
        d_open = pushed * root * conv * (1.0 - op)
        acc_s[5:6, :] += jnp.sum(d_raw, axis=0, keepdims=True)
        acc_s[6:7, :] += jnp.sum(d_open, axis=0, keepdims=True)
        d_raw, d_open = d_raw.astype(BF), d_open.astype(BF)
        back = []
        for h in (0, 1):
            cols = slice(128 * h, 128 * h + 128)
            d_block = jnp.concatenate([d_raw[:, cols], d_open[:, cols]], axis=1)
            gate_grads[h] = gate_grads[h] + tn(conv_low[:, cols], d_block)
            back.append(nt(d_block, gate_w[cols, :]))
        d_conv = pushed * root + jnp.concatenate(back, axis=1)
        dc_s[rows, :] = d_conv
        acc_s[4:5, :] += jnp.sum(d_conv, axis=0, keepdims=True)
        for tap in range(4):
            acc_s[tap : tap + 1, :] += jnp.sum(d_conv * shifted[tap], axis=0, keepdims=True)
    for k in range(8):
        lo = k * BLOCK
        d_x = small[0:1, :] * dc_s[lo : lo + BLOCK, :]
        for tap in range(1, 4):
            d_x = d_x + small[tap : tap + 1, :] * dc_s[lo + tap : lo + tap + BLOCK, :]
        dx_s[lo : lo + BLOCK, :] = d_x
    for y in range(4):
        for rc, ref in enumerate((dx_mine, dx_theirs)):
            at = pl.multiple_of(time_start(pos, y, rc), BLOCK)
            ref[BLOCK * y : BLOCK * y + BLOCK, :] = dx_s[pl.ds(at, BLOCK), :].astype(BF)
    for h in (0, 1):
        gs_ref[128 * h : 128 * h + 128, 0:256] = gate_grads[h].astype(BF)
    gs_ref[:, 256:384] = acc_s[...].T.astype(BF)


def normed_backward_kernel(pos, dx_mine, dx_theirs, dy_mine, dy_theirs, rs_ref, *refs):
    weights, outs, part_s, copy_sems = refs[:4], refs[4:8], refs[8], refs[9]
    for k in range(ROWS // STEP):
        rows = slice(k * STEP, k * STEP + STEP)
        scale = rs_ref[rows, 0:1]
        lows = [(dx_ref[rows, :].astype(F32) * scale).astype(BF) for dx_ref in (dx_mine, dx_theirs)]
        lows += [dy_mine[rows, CHAN:], dy_theirs[rows, CHAN:]]
        part_s[rows, :] = sum(nt(low, w_ref[...]) for low, w_ref in zip(lows, weights)).astype(BF)
    wait_all(start_out(pos, part_s, outs, copy_sems))


def cols_grads_kernel(*refs):
    x_refs, dx_refs, dy_refs, rs_ref = refs[:2], refs[2:4], refs[4:6], refs[6]
    go_mine, go_theirs, gs_ref, out_ref, out_s, wide_s, rest_s, copy_sems = refs[7:]
    rest_s[:, 0:WIDTH] = (go_mine[...].astype(F32) + go_theirs[...].astype(F32)).astype(BF)
    rest_s[:, WIDTH:C_WIDTH] = gs_ref[...]
    rest_s[:, C_WIDTH:] = jnp.zeros((CHAN, 8 * REST - C_WIDTH), BF)
    wide = x_refs[1][...].astype(F32)
    scales = (rs_ref[:, 0:1], lax.rsqrt(jnp.mean(wide * wide, axis=-1, keepdims=True) + EPS))
    lows = [
        jnp.concatenate([(dx[...].astype(F32) * scale).astype(BF), dy[:, CHAN:]], axis=1)
        for dx, dy, scale in zip(dx_refs, dy_refs, scales)
    ]
    saves = []
    for k in range(WIDTH // 384):
        rows = slice(384 * k, 384 * k + 384)
        wide_s[rows, :] = tn(x_refs[0][:, rows], lows[0]) + tn(x_refs[1][:, rows], lows[1])
        for i in range(32 * k, 32 * k + 32):
            block = [wide_s[12 * i : 12 * i + 12, 128 * t : 128 * t + 128] for t in range(4)]
            out_s[i, 0:COLS_ROWS, :] = jnp.concatenate(block).astype(BF)
            few = slice(16 * (i // 8), 16 * (i // 8) + 16)
            for t in range(2):
                at = REST * (i % 8) + 128 * t
                out_s[i, COLS_ROWS + 16 * t : COLS_ROWS + 16 * t + 16, :] = rest_s[few, at : at + 128]
        part = slice(32 * k, 32 * k + 32)
        saves += start_loads(((out_s.at[part], out_ref.at[part]),), copy_sems, k)
    wait_all(saves)


def add_terms(terms):
    out = terms[0][...].astype(F32)
    for term in terms[1:]:
        out = out + term[...].astype(F32)
    return out


def residual_kernel(x_ref, *refs):
    terms, (res_out, scale_out, low_ref, res_s, scale_s, copy_sems) = refs[:4], refs[4:]
    residual = x_ref[...].astype(F32) + add_terms(terms)
    scale = lax.rsqrt(jnp.mean(residual * residual, axis=-1, keepdims=True) + EPS)
    res_s[...] = residual
    scale_s[...] = jnp.broadcast_to(scale, (BLOCK, 128))
    saves = start_loads(((res_s, res_out), (scale_s, scale_out)), copy_sems, 0)
    low_ref[...] = (residual * scale).astype(BF)
    wait_all(saves)


def d_residual_kernel(cot_ref, res_ref, scale_ref, *refs):
    terms, (d_out, low_ref, d_s, copy_sems) = refs[:4], refs[4:]
    d_normed = add_terms(terms)
    scale = scale_ref[:, 0:1]
    normed = res_ref[...] * scale
    along = jnp.mean(normed * d_normed, axis=-1, keepdims=True)
    d_residual = cot_ref[...].astype(F32) + scale * (d_normed - normed * along)
    d_s[...] = d_residual
    saves = start_loads(((d_s, d_out),), copy_sems, 0)
    low_ref[...] = d_residual.astype(BF)
    wait_all(saves)


def input_grad_kernel(x_ref, d_ref, *refs):
    terms, out_ref = refs[:4], refs[4]
    scaled = add_terms(terms)
    x = x_ref[...].astype(F32)
    power = 1.0 / (jnp.mean(x * x, axis=-1, keepdims=True) + EPS)
    along = jnp.mean(x * scaled, axis=-1, keepdims=True) * power
    out_ref[...] = (d_ref[...] + scaled - x * along).astype(BF)


def layer_out_kernel(res_ref, *refs):
    terms, out_ref = refs[:4], refs[4]
    out_ref[...] = (res_ref[...] + add_terms(terms)).astype(BF)


def dp_total(got_ref, lo, count):
    out = got_ref[0, lo : lo + count, :].astype(F32)
    for k in range(1, 16):
        out = out + got_ref[k, lo : lo + count, :].astype(F32)
    return out


def finish_cols_kernel(got_ref, gain_ref, x_ref, y_ref, gx_ref, gy_ref, gain_grad_ref, wide_s):
    for s in range(8):
        wide_s[COLS_ROWS * s : COLS_ROWS * s + COLS_ROWS, :] = dp_total(got_ref, SUM_ROWS * s, COLS_ROWS)
    gain = column(gain_ref)
    along = jnp.zeros((12, 128), F32)
    for s in range(8):
        for t in range(4):
            at = CHAN * s + 128 * (t % 2)
            lo = COLS_ROWS * s + 12 * t
            grad = wide_s[lo : lo + 12, :]
            w_ref, g_ref = (x_ref, gx_ref) if t < 2 else (y_ref, gy_ref)
            along = along + grad * w_ref[:, at : at + 128].astype(F32)
            g_ref[:, at : at + 128] = grad * gain
    gain_grad_ref[...] = as_row(jnp.sum(along, axis=1, keepdims=True))


def mlp_back_kernel(got_ref, cols_ref, down_ref, wide_s):
    for j in range(3):
        wide_s[:, 384 * j : 384 * j + 384] = got_ref[96 * j : 96 * j + 96, :].astype(F32)
    for s in range(8):
        block = jnp.concatenate([wide_s[12 * s : 12 * s + 12, :], jnp.zeros((4, GATED), F32)])
        cols_ref[s] = block.astype(BF)
    for j in range(4):
        down_ref[:, 384 * j : 384 * j + 384] = got_ref[288 + 48 * j : 336 + 48 * j, :]


def rest_back_kernel(cols_ref, got_ref, out_ref):
    out_ref[:, :, :GATED] = cols_ref[...]
    for s in range(8):
        for t in range(2):
            tile = dp_total(got_ref, SUM_ROWS * s + COLS_ROWS + 16 * t, 16)
            out_ref[s, :, GATED + 128 * t : GATED + 128 * t + 128] = tile.astype(BF)


def mlp_finish_kernel(*refs):
    got_ref, gain_ref, gate_ref, up_ref, g_gate_ref, g_up_ref, gain_grad_ref = refs
    gain = column(gain_ref)
    along = jnp.zeros((12, 1), F32)
    for s in range(8):
        block = got_ref[s, :, :GATED].astype(F32)[:12]
        lo = HID * s
        cols = slice(lo, lo + HID)
        grad_gate = jnp.concatenate([block[:, :512], block[:, 1024:1088]], axis=1)
        grad_up = jnp.concatenate([block[:, 512:1024], block[:, 1088:]], axis=1)
        terms = grad_gate * gate_ref[:, cols].astype(F32) + grad_up * up_ref[:, cols].astype(F32)
        along = along + jnp.sum(terms, axis=1, keepdims=True)
        g_gate_ref[:, cols] = grad_gate * gain
        g_up_ref[:, cols] = grad_up * gain
    gain_grad_ref[...] = as_row(along)


def rest_join_kernel(got_ref, down_ref, out_ref):
    for s in range(8):
        out_ref[:, REST * s : REST * s + REST] = got_ref[s, :, GATED:]
    for j in range(3):
        out_ref[:, 8 * REST + WIDTH * j : 8 * REST + WIDTH * j + WIDTH] = down_ref[16 * j : 16 * j + 16, :]


def finish_rest_kernel(got_ref, out_ref, gate_w_ref, taps_ref, bias_ref, gate_bias_ref, decay_ref, down_ref):
    for j in range(3):
        rows = min(16, 36 - 16 * j)
        tile = got_ref[:, 8 * REST + WIDTH * j : 8 * REST + WIDTH * j + WIDTH]
        down_ref[16 * j : 16 * j + rows, :] = tile.astype(F32)[:rows]
    out_ref[...] = got_ref[:, 0:WIDTH].astype(F32)
    gate_w_ref[...] = got_ref[:, 1536:1792].astype(F32)
    small = got_ref[:, 1792:1920].astype(F32)
    rows = [as_row(small[:, k : k + 1]) for k in range(8)]
    for k in range(4):
        taps_ref[k : k + 1, :] = rows[k]
    bias_ref[...] = rows[4]
    for k in range(2):
        gate_bias_ref[k : k + 1, :] = rows[5 + k]
    decay_ref[...] = rows[7]


def shape(dims, dtype):
    return jax.ShapeDtypeStruct(dims, dtype)


def sems(count):
    return pltpu.SemaphoreType.DMA((count,))


def size(dims, dtype):
    return math.prod(dims) * jnp.dtype(dtype).itemsize


def call(kernel, args, outs, scratch=(), any_args=(), any_outs=(), far_outs=(), micros=0, more=8):
    held = sum(size(a.shape, a.dtype) for k, a in enumerate(args) if k not in any_args)
    held += sum(size(*o) for k, o in enumerate(outs) if k not in any_outs)
    held += sum(size(s.shape, s.dtype) for s in scratch if s.memory_space == pltpu.VMEM)
    args = [pltpu.with_memory_space_constraint(a, pltpu.HBM) if k in any_args else a for k, a in enumerate(args)]
    in_specs = [SMEM if a.dtype == jnp.int32 else HBM if k in any_args else VMEM for k, a in enumerate(args)]
    return pl.pallas_call(
        kernel,
        name=kernel.__name__.removesuffix("_kernel"),
        in_specs=in_specs,
        out_specs=[ANY if k in any_outs else VMEM for k in range(len(outs))],
        out_shape=[pltpu.HBM(*o) if k in far_outs else shape(*o) for k, o in enumerate(outs)],
        scratch_shapes=scratch,
        cost_estimate=pl.CostEstimate(flops=int(micros * 10**9), bytes_accessed=0, transcendentals=0),
        compiler_params=pltpu.CompilerParams(vmem_limit_bytes=min(held + (more << 20), 60 << 20)),
    )(*args)


PART = ((BLOCK, WIDTH), BF)
PARTS = [PART] * 4
PART_S = pltpu.VMEM((ROWS, WIDTH), BF)
CHAIN_S = pltpu.VMEM((2 * TOKENS, 128), F32)


def per_device(
    inputs,
    cotangent,
    resets,
    start_state,
    conv_history,
    norm_gain,
    proj_x,
    proj_y,
    conv_taps,
    conv_bias,
    gate_weight,
    gate_bias,
    decay_param,
    proj_out,
    mlp_gain,
    mlp_gate,
    mlp_up,
    mlp_down,
):
    pos = jnp.stack([lax.axis_index(a) for a in DP_SEQ]).astype(jnp.int32)
    flat_in = inputs[0]
    flat_cot = cotangent[0]
    gain_one = norm_gain[None]
    gain_two = mlp_gain[None]

    (rest,) = call(
        pack_rows_kernel,
        (proj_out, gate_weight, conv_taps.T, conv_bias[None], gate_bias.T, decay_param[None]),
        [((16, C_WIDTH), BF)],
        more=60,
    )
    rest, late_x, late_down = tied(rest, proj_x, mlp_down)
    rest = transposed_devices(rest, False)
    blocks = call(
        pack_cols_kernel,
        (pos, gain_one, gain_two, late_x, proj_y, mlp_gate, mlp_up),
        [((16, SENT), BF)] * 8,
        [pltpu.VMEM((8, 16, SENT), F32)],
        more=60,
    )
    early, late = call(
        shard_kernel,
        (pos, *exchanged(blocks), rest),
        [((EARLY, 128), BF), ((LATE, 128), BF)],
        [pltpu.VMEM((8, 16, SENT), F32), pltpu.VMEM((96, SENT), F32)],
    )
    late = lax.all_gather(late, DP, axis=0, tiled=True)
    early, early_in, late_down = tied(early, flat_in, late_down)
    x_pieces = gather_rows(early_in)
    down = transposed_devices(late_down, False)
    early = lax.all_gather(early, DP, axis=0, tiled=True)
    early, x_pieces, down = tied(early, x_pieces, down)
    x_mine, c_mine = call(early_unpack_kernel, (early,), [((WIDTH, CHAN), BF), ((CHAN, SMALL), BF)])
    (down,) = call(down_pack_kernel, (down,), [((DOWN_ROWS, MLP_LANES), BF)])
    x_mine, late_cot, down = tied(x_mine, flat_cot, down)
    down = lax.all_gather(down, DP, axis=0, tiled=True)
    x_theirs = swapped(x_mine)
    c_near = [hop(late_cot, "y", r) for r in PIECES[1:3]]

    keep = (1 - resets).astype(F32)
    place = lax.axis_index(SEQ) * CHAN
    history = lax.dynamic_slice(conv_history[0].astype(F32), (0, place), (3, CHAN)) * keep
    initial = lax.dynamic_slice(start_state, (0, place), (1, CHAN)) * keep
    edges = jnp.concatenate([jnp.zeros((5, CHAN), F32), history, jnp.zeros((7, CHAN), F32), initial])
    xl_mine, xl_theirs, x_all, rs = call(
        in_proj_kernel,
        (pos, *x_pieces, x_mine, x_theirs),
        [((ROWS, CHAN), BF)] * 2 + [((ROWS, WIDTH), BF), ((ROWS, 128), F32)],
        [sems(4)],
        any_args=range(1, 5),
        micros=8,
    )
    xl_got, c_near, late_cot = tied(swapped(xl_theirs), c_near, late_cot)
    c_far = hop(late_cot, "y", PIECES[3])
    hid_mine, hid_theirs, saved = call(
        recurrence_kernel,
        (pos, xl_mine, xl_got, c_mine, edges),
        [((ROWS, CHAN), BF)] * 2 + [((4 * (TOKENS + 8), CHAN), F32)],
        [pltpu.VMEM((4 * (TOKENS + 8), CHAN), F32), CHAIN_S, CHAIN_S, CHAIN_S, sems(4)],
        any_outs=[2],
        far_outs=[2],
        micros=8,
    )
    hid_theirs = swapped(hid_theirs)
    hid_mine, c_far, late = tied(hid_mine, c_far, late)
    c_pieces = [flat_cot, *c_near, c_far]
    y_mine, o_mine = call(
        late_unpack_kernel,
        (late,),
        [((WIDTH, CHAN), BF), ((CHAN, WIDTH), BF)],
        [pltpu.VMEM((16 * COLS, 128), BF), sems(16)],
        any_args=range(1),
    )
    y_theirs, o_theirs = swapped(y_mine), swapped(o_mine)
    (yp,) = call(y_proj_kernel, (x_all, rs, y_mine, y_theirs), [((ROWS, 2 * CHAN), F32)], micros=8)
    *parts, mix = call(
        out_proj_kernel,
        (pos, hid_mine, hid_theirs, yp, o_mine, o_theirs),
        PARTS + [((ROWS, 2 * CHAN), BF)],
        [PART_S, sems(4)],
        any_outs=range(4),
        micros=1.2,
    )
    terms = scatter_rows(parts)
    _, late = tied(parts, late)
    (w_up,) = call(
        cols_unpack_kernel,
        (late,),
        [((WIDTH, GATED), BF)],
        [pltpu.VMEM((16 * 864, 128), BF), sems(16)],
        any_args=range(1),
    )
    up_theirs = swapped(w_up)
    terms, w_up = tied(terms, w_up)
    residual, scale_two, normed_two = call(
        residual_kernel,
        (flat_in, *terms),
        [((BLOCK, WIDTH), F32), ((BLOCK, 128), F32), PART],
        [pltpu.VMEM((BLOCK, WIDTH), F32), pltpu.VMEM((BLOCK, 128), F32), sems(2)],
        any_outs=range(2),
        far_outs=range(2),
        micros=30,
    )

    _, down = tied(normed_two, down)
    (w_down,) = call(down_unpack_kernel, (down,), [((HID_PAD, WIDTH), BF)], [pltpu.VMEM((HID, WIDTH), F32)])
    down_theirs = swapped(w_down)
    tokens, pre_mine, pre_theirs = call(
        mlp_pre_kernel,
        (pos, *gather_rows(normed_two), *c_pieces, w_up, up_theirs),
        [((2 * ROWS, WIDTH), BF)] + [((ROWS, GATED), F32)] * 2,
        [sems(8)],
        micros=20,
    )
    tokens_got = swapped(tokens)
    *parts, save_mine, save_theirs = call(
        mlp_kernel,
        (pos, tokens, pre_mine, pre_theirs, w_up, w_down, up_theirs, down_theirs),
        PARTS + [((ROWS, HID_PAD + GATED), BF)] * 2,
        [PART_S, sems(4)],
        any_outs=range(4),
        micros=5,
    )
    out_parts = call(
        mlp_out_kernel,
        (pos, save_mine, save_theirs, w_down, down_theirs),
        PARTS,
        [PART_S, sems(4)],
        any_outs=range(4),
        far_outs=range(4),
        micros=15,
    )
    terms = scatter_rows(parts)
    save_got = swapped(save_theirs)
    save_got, out_parts = tied(save_got, out_parts)
    (mlp_grads,) = call(
        mlp_grads_kernel,
        (tokens, tokens_got, save_mine, save_got),
        [((16 * MLP_ROWS, MLP_LANES), BF)],
        [
            pltpu.VMEM((16 * MLP_ROWS, MLP_LANES), BF),
            pltpu.VMEM((WIDTH, GATED), BF),
            pltpu.VMEM((HID_PAD, WIDTH), F32),
            sems(4),
        ],
        any_outs=range(1),
        far_outs=range(1),
        micros=15,
    )
    terms, mlp_grads = tied(terms, mlp_grads)
    mlp_sum = lax.psum_scatter(mlp_grads, DP, scatter_dimension=0, tiled=True)
    d_residual, d_out = call(
        d_residual_kernel,
        (flat_cot, residual, scale_two, *terms),
        [((BLOCK, WIDTH), F32), PART],
        [pltpu.VMEM((BLOCK, WIDTH), F32), sems(1)],
        any_outs=range(1),
        far_outs=range(1),
    )

    d_out, late_x_all = tied(d_out, x_all)
    d_pieces, all_theirs = tied(gather_rows(d_out), swapped(late_x_all))
    back_mine, back_theirs, d_all = call(
        mixed_backward_kernel,
        (pos, *d_pieces, o_mine, o_theirs, yp, hid_mine, hid_theirs, rs),
        [((ROWS, 2 * CHAN), BF)] * 2 + [((ROWS, WIDTH), BF)],
        [sems(4)],
        micros=2,
    )
    back_got = swapped(back_theirs)
    dx_mine, dx_theirs, g_small = call(
        chain_backward_kernel,
        (pos, back_mine, back_got, c_mine, saved),
        [((ROWS, CHAN), BF)] * 2 + [((CHAN, 384), BF)],
        [
            CHAIN_S,
            CHAIN_S,
            pltpu.VMEM((TOKENS + 8, CHAN), F32),
            pltpu.VMEM((TOKENS, CHAN), F32),
            pltpu.VMEM((128, CHAN), F32),
            pltpu.VMEM((2 * TOKENS + 16, 128), F32),
            pltpu.VMEM((4 * (TOKENS + 8), CHAN), F32),
            sems(4),
        ],
        any_args=[4],
        micros=20,
    )
    dx_got = swapped(dx_theirs)
    parts = call(
        normed_backward_kernel,
        (pos, dx_mine, dx_got, back_mine, back_theirs, rs, x_mine, x_theirs, y_mine, y_theirs),
        PARTS,
        [PART_S, sems(4)],
        any_outs=range(4),
    )
    terms = scatter_rows(parts)
    _, late_mix = tied(parts, mix)
    go_mine, go_theirs = call(out_grads_kernel, (late_mix, d_all), [((CHAN, WIDTH), BF)] * 2)
    (g_cols,) = call(
        cols_grads_kernel,
        (x_all, all_theirs, dx_mine, dx_theirs, back_mine, back_got, rs, go_mine, swapped(go_theirs), g_small),
        [((128, SUM_ROWS, 128), BF)],
        [
            pltpu.VMEM((128, SUM_ROWS, 128), BF),
            pltpu.VMEM((WIDTH, 2 * CHAN), F32),
            pltpu.VMEM((CHAN, 8 * REST), BF),
            sems(4),
        ],
        any_outs=range(1),
        far_outs=range(1),
    )
    g_cols = lax.all_to_all(g_cols, DP_SEQ, 0, 0, tiled=True).reshape(16, 8 * SUM_ROWS, 128)
    terms, mlp_sum = tied(terms, mlp_sum)
    blocks, down_back = call(
        mlp_back_kernel,
        (mlp_sum,),
        [((8, 16, GATED), BF), ((48, WIDTH), BF)],
        [pltpu.VMEM((96, GATED), F32)],
        micros=100,
    )
    (input_grad,) = call(input_grad_kernel, (flat_in, d_residual, *terms), [PART])
    (blocks,) = call(rest_back_kernel, (blocks, g_cols), [((8, 16, GATED + REST), BF)])
    blocks = lax.all_to_all(blocks, SEQ, 0, 0, tiled=True)
    out_parts, _ = tied(out_parts, terms)
    out_terms = scatter_rows(out_parts)
    grad_x, grad_y, grad_norm_gain = call(
        finish_cols_kernel,
        (g_cols, gain_one, proj_x, proj_y),
        [((12, 8 * CHAN), F32)] * 2 + [((1, 12), F32)],
        [pltpu.VMEM((8 * COLS_ROWS, 128), F32)],
    )
    blocks, input_grad, grad_x = tied(blocks, input_grad, grad_x)
    (g_rest,) = call(rest_join_kernel, (blocks, down_back), [((16, 8 * REST + 3 * WIDTH), BF)])
    g_rest = transposed_devices(g_rest, True)
    grad_gate, grad_up, grad_mlp_gain = call(
        mlp_finish_kernel,
        (blocks, gain_two, mlp_gate, mlp_up),
        [((12, 8 * HID), F32)] * 2 + [((1, 12), F32)],
    )
    (layer_out,) = call(layer_out_kernel, (residual, *out_terms), [PART])
    g_rest, grad_gate, layer_out = tied(g_rest, grad_gate, layer_out)
    grad_out, grad_gate_w, grad_taps, grad_conv_bias, grad_gate_bias, grad_decay, grad_down = call(
        finish_rest_kernel,
        (g_rest,),
        [
            ((16, WIDTH), F32),
            ((16, CHAN), F32),
            ((4, 16), F32),
            ((1, 16), F32),
            ((2, 16), F32),
            ((1, 16), F32),
            ((36, WIDTH), F32),
        ],
    )
    return (
        layer_out[None],
        input_grad[None],
        grad_norm_gain[0],
        grad_x,
        grad_y,
        grad_taps.T,
        grad_conv_bias[0],
        grad_gate_w,
        grad_gate_bias.T,
        grad_decay[0],
        grad_out,
        grad_mlp_gain[0],
        grad_gate,
        grad_up,
        grad_down,
    )


def solution(mesh):
    finer = Mesh(mesh.devices.reshape(4, 4, 4, 2), DP_SEQ)
    rows = P(DP_SEQ, None)
    line = P(DP_SEQ)
    tokens = P(DP, SEQ, None)
    in_specs = (
        tokens,
        tokens,
        P(DP),
        P(DP, None),
        P(DP, None, None),
        line,
        rows,
        rows,
        rows,
        line,
        rows,
        rows,
        line,
        rows,
        line,
        rows,
        rows,
        rows,
    )
    out_specs = (
        tokens,
        tokens,
        line,
        rows,
        rows,
        rows,
        line,
        rows,
        rows,
        line,
        rows,
        line,
        rows,
        rows,
        rows,
    )
    return jax.shard_map(per_device, mesh=finer, in_specs=in_specs, out_specs=out_specs, check_vma=False)
```

```python
import math

import jax
import jax.numpy as jnp
from jax import lax
from jax.experimental import pallas as pl
from jax.experimental.pallas import tpu as pltpu
from jax.sharding import Mesh
from jax.sharding import PartitionSpec as P

BF = jnp.bfloat16
F32 = jnp.float32
EPS = 1e-06
GELU_C = 0.7978845608028654
GELU_K = 0.044715

TOKENS = 1024
ROWS = 512
BLOCK = 128
WIDTH = 1536
CHAN = 256
HID = 576
HID_PAD = 640
GATED = 2 * HID
STEP = 256
C_WIDTH = 1920
SENT = 2 * CHAN + GATED
SMALL = 384
EARLY = 240
COLS = 384
LATE = 1248
DOWN_ROWS = 192
COLS_ROWS = 48
SUM_ROWS = 80
REST = 256
MLP_ROWS = 480
MLP_LANES = 384

DP = ("z", "x")
SEQ = ("y", "c")
DP_SEQ = ("z", "x", "y", "c")

ANY = pl.BlockSpec(memory_space=pl.ANY)
HBM = pl.BlockSpec(memory_space=pltpu.HBM)
VMEM = pl.BlockSpec(memory_space=pltpu.VMEM)
SMEM = pl.BlockSpec(memory_space=pltpu.SMEM)

PIECES = (0, 1, 3, 2)
PLACES = [(ry, rc) for rc in (0, 1) for ry in (0, 2, 1, 3)]


def hop(value, axis, distance):
    size = lax.axis_size(axis)
    return lax.ppermute(value, axis, [(i, (i - distance) % size) for i in range(size)])


def added(one, two):
    return (one.astype(F32) + two.astype(F32)).astype(BF)


def swapped(value):
    return hop(value, "c", 1)


def gather_rows(block):
    return [block] + [hop(block, "y", r) for r in PIECES[1:]]


def scatter_rows(parts):
    return [parts[0]] + [hop(parts[r], "y", 4 - r) for r in (2, 1, 3)]


def tied(*values):
    return lax.optimization_barrier(values)


def transposed_devices(value, back):
    pairs = [(16 * s + d, 8 * d + s) for s in range(8) for d in range(16)]
    return lax.ppermute(value, DP_SEQ, [(b, a) for a, b in pairs] if back else pairs)


def exchanged(blocks):
    out = []
    for (ry, rc), block in zip(PLACES, blocks):
        route = [(2 * y + c, 2 * ((y + ry) % 4) + (c + rc) % 2) for y in range(4) for c in range(2)]
        out.append(lax.ppermute(block, SEQ, route) if (ry, rc) != (0, 0) else block)
    return out


def nn(a, b):
    return jnp.dot(a, b, preferred_element_type=F32)


def nt(a, b):
    return lax.dot_general(a, b, (((1,), (1,)), ((), ())), preferred_element_type=F32)


def tn(a, b):
    return lax.dot_general(a, b, (((0,), (0,)), ((), ())), preferred_element_type=F32)


def gelu_parts(v):
    sq = v * v
    t = jnp.tanh(GELU_C * v * (1.0 + GELU_K * sq))
    half = 0.5 * (1.0 + t)
    slope = half + 0.5 * v * (1.0 - t * t) * (GELU_C * (1.0 + 3.0 * GELU_K * sq))
    return v * half, slope


def neg_expm1(v):
    series = 1.0 + v * (1.0 / 7.0)
    for k in (6, 5, 4, 3, 2):
        series = 1.0 + v * (1.0 / k) * series
    return jnp.where(v > -0.35, -v * series, 1.0 - jnp.exp(v))


def softplus(v):
    e = jnp.exp(-jnp.abs(v))
    series = e * (1.0 - e * (1 / 2 - e * (1 / 3 - e * (1 / 4 - e * (1 / 5 - e * (1 / 6))))))
    return jnp.maximum(v, 0.0) + jnp.where(e < 0.05, series, jnp.log(1.0 + e))


def column(row_ref):
    n = row_ref.shape[1]
    square = jnp.broadcast_to(row_ref[...].astype(F32), (n, n))
    same = lax.broadcasted_iota(jnp.int32, (n, n), 0) == lax.broadcasted_iota(jnp.int32, (n, n), 1)
    return jnp.sum(jnp.where(same, square, 0.0), axis=1, keepdims=True)


def as_row(col):
    n = col.shape[0]
    square = jnp.broadcast_to(col, (n, n))
    same = lax.broadcasted_iota(jnp.int32, (n, n), 0) == lax.broadcasted_iota(jnp.int32, (n, n), 1)
    return jnp.sum(jnp.where(same, square, 0.0), axis=0, keepdims=True)


def place_of(pos, ry, rc):
    return lax.rem(pos[2] + ry, 4) * 2 + lax.rem(pos[3] + rc, 2)


def block_rows(pos, ry):
    return pl.ds(pl.multiple_of(lax.rem(pos[2] + ry, 4) * BLOCK, BLOCK), BLOCK)


def time_start(pos, y, rc):
    return (2 * y + lax.rem(pos[3] + rc, 2)) * BLOCK


def start_loads(pairs, sems, first):
    copies = []
    for k, (ref, scratch) in enumerate(pairs):
        copies.append(pltpu.make_async_copy(ref, scratch, sems.at[first + k]))
        copies[-1].start()
    return copies


def start_in(pos, refs, scratch, sems, first=0):
    return start_loads([(ref, scratch.at[block_rows(pos, ry), :]) for ref, ry in zip(refs, PIECES)], sems, first)


def start_out(pos, scratch, refs, sems, first=0):
    return start_loads([(scratch.at[block_rows(pos, r), :], refs[r]) for r in range(4)], sems, first)


def wait_all(copies):
    for copy in copies:
        copy.wait()


def small_rows(c_ref):
    return c_ref[:, CHAN:SMALL].astype(F32).T


def scan_chunks(step, carry):
    def four(k, carry):
        for j in range(4):
            carry = step(k * 4 + j, carry)
        return carry

    return lax.fori_loop(0, BLOCK // 4, four, carry)


def chunk_rows(t):
    return pl.ds(t, 8, stride=BLOCK)


def side(ref, lanes):
    rows = ref.shape[0] // 2
    return ref.at[lanes * rows : (lanes + 1) * rows, :]


def get_rows(ref, lo, count):
    return jnp.concatenate([side(ref, k)[lo : lo + count, :] for k in (0, 1)], axis=1)


def put_rows(ref, lo, count, value):
    for k in (0, 1):
        side(ref, k)[lo : lo + count, :] = value[:, 128 * k : 128 * k + 128]


def chain(mult_ref, ahead, add_ref, product_ref, backward):
    def step(t, carry):
        t = BLOCK - 1 - t if backward else t
        out = []
        for k in (0, 1):
            state, product = carry[2 * k : 2 * k + 2]
            mult = side(mult_ref, k)[chunk_rows(t + ahead), :]
            state = mult * state + side(add_ref, k)[chunk_rows(t), :]
            product = product * mult
            side(add_ref, k)[chunk_rows(t), :] = state
            side(product_ref, k)[chunk_rows(t), :] = product
            out += [state, product]
        return tuple(out)

    zero, one = jnp.zeros((8, 128), F32), jnp.ones((8, 128), F32)
    left, left_p, right, right_p = scan_chunks(step, (zero, one, zero, one))
    return jnp.concatenate([left, right], axis=1), jnp.concatenate([left_p, right_p], axis=1)


def gated_cols(gate, up, s):
    lo = HID * s
    return [gate[:, lo : lo + 512], up[:, lo : lo + 512], gate[:, lo + 512 : lo + HID], up[:, lo + 512 : lo + HID]]


def pack_cols_kernel(pos, gain_one, gain_two, x_ref, y_ref, gate_ref, up_ref, *refs):
    outs, blocks_s = refs[:8], refs[8]
    gain = column(gain_one)
    x, y = x_ref[...].astype(F32) * gain, y_ref[...].astype(F32) * gain
    gain = column(gain_two)
    gate, up = gate_ref[...].astype(F32) * gain, up_ref[...].astype(F32) * gain
    fill = jnp.zeros((4, SENT), F32)
    for s in range(8):
        cols = slice(CHAN * s, CHAN * s + CHAN)
        block = jnp.concatenate([x[:, cols], y[:, cols], *gated_cols(gate, up, s)], axis=1)
        blocks_s[s] = jnp.concatenate([block, fill])
    for k, (ry, rc) in enumerate(PLACES):
        outs[k][...] = blocks_s[place_of(pos, ry, rc)].astype(BF)


def pack_rows_kernel(out_ref, gate_w_ref, taps_ref, bias_ref, gate_bias_ref, decay_ref, rest_ref):
    rest_ref[:, 0:WIDTH] = out_ref[...]
    rest_ref[:, 1536:1792] = gate_w_ref[...]
    lane = lax.broadcasted_iota(jnp.int32, (16, 128), 1)
    small = jnp.zeros((16, 128), F32)
    for k in range(4):
        small = jnp.where(lane == k, column(taps_ref.at[k : k + 1, :]), small)
    small = jnp.where(lane == 4, column(bias_ref), small)
    for k in range(2):
        small = jnp.where(lane == 5 + k, column(gate_bias_ref.at[k : k + 1, :]), small)
    rest_ref[:, 1792:1920] = jnp.where(lane == 7, column(decay_ref), small).astype(BF)


def shard_kernel(pos, *refs):
    blocks, (rest_ref, early_ref, late_ref, blocks_s, wide_s) = refs[:8], refs[8:]
    for k, (ry, rc) in enumerate(PLACES):
        blocks_s[place_of(pos, 4 - ry, rc)] = blocks[k][...].astype(F32)
    for s in range(8):
        wide_s[12 * s : 12 * s + 12, :] = blocks_s[s, 0:12, :]
    for t in range(2):
        early_ref[96 * t : 96 * t + 96, :] = wide_s[:, 128 * t : 128 * t + 128].astype(BF)
        late_ref[96 * t : 96 * t + 96, :] = wide_s[:, CHAN + 128 * t : CHAN + 128 * t + 128].astype(BF)
    for t in range(3):
        early_ref[192 + 16 * t : 208 + 16 * t, :] = rest_ref[:, WIDTH + 128 * t : WIDTH + 128 * t + 128]
    for t in range(12):
        late_ref[192 + 16 * t : 208 + 16 * t, :] = rest_ref[:, 128 * t : 128 * t + 128]
    for t in range(9):
        late_ref[COLS + 96 * t : COLS + 96 * t + 96, :] = wide_s[:, 512 + 128 * t : 640 + 128 * t].astype(BF)


def early_unpack_kernel(all_ref, w_ref, c_ref):
    for p in range(16):
        at = EARLY * p
        for t in range(2):
            w_ref[96 * p : 96 * p + 96, 128 * t : 128 * t + 128] = all_ref[at + 96 * t : at + 96 * t + 96, :]
        for t in range(3):
            lo = at + 192 + 16 * t
            c_ref[16 * p : 16 * p + 16, 128 * t : 128 * t + 128] = all_ref[lo : lo + 16, :]


def late_unpack_kernel(all_ref, w_ref, o_ref, late_s, copy_sems):
    slots = [late_s.at[COLS * p : COLS * p + COLS, :] for p in range(16)]
    loads = start_loads([(all_ref.at[LATE * p : LATE * p + COLS, :], slots[p]) for p in range(16)], copy_sems, 0)
    for p in range(16):
        loads[p].wait()
        at = COLS * p
        for t in range(2):
            w_ref[96 * p : 96 * p + 96, 128 * t : 128 * t + 128] = late_s[at + 96 * t : at + 96 * t + 96, :]
        for t in range(12):
            lo = at + 192 + 16 * t
            o_ref[16 * p : 16 * p + 16, 128 * t : 128 * t + 128] = late_s[lo : lo + 16, :]


def cols_unpack_kernel(all_ref, w_ref, cols_s, copy_sems):
    slots = [cols_s.at[864 * p : 864 * p + 864, :] for p in range(16)]
    ends = [(all_ref.at[LATE * p + COLS : LATE * p + LATE, :], slots[p]) for p in range(16)]
    loads = start_loads(ends, copy_sems, 0)
    for p in range(16):
        loads[p].wait()
        for t in range(9):
            at = 864 * p + 96 * t
            w_ref[96 * p : 96 * p + 96, 128 * t : 128 * t + 128] = cols_s[at : at + 96, :]


def down_pack_kernel(down_ref, out_ref):
    down = jnp.concatenate([down_ref[...].astype(F32), jnp.zeros((12, WIDTH), F32)]).astype(BF)
    for j in range(4):
        out_ref[48 * j : 48 * j + 48, :] = down[:, 384 * j : 384 * j + 384]


def down_unpack_kernel(all_ref, d_ref, wide_s):
    for p in range(16):
        for j in range(4):
            at = p * DOWN_ROWS + 48 * j
            wide_s[36 * p : 36 * p + 36, 384 * j : 384 * j + 384] = all_ref[at : at + 48, :].astype(F32)[:36]
    d_ref[0:HID, :] = wide_s[...].astype(BF)
    d_ref[HID:, :] = jnp.zeros((HID_PAD - HID, WIDTH), BF)


def in_proj_kernel(pos, *refs):
    x_refs, w_mine, w_theirs = refs[:4], refs[4], refs[5]
    xl_mine, xl_theirs, x_s, rs_ref, copy_sems = refs[6:]
    wait_all(start_in(pos, x_refs, x_s, copy_sems))
    for k in range(ROWS // STEP):
        rows = slice(k * STEP, k * STEP + STEP)
        here = x_s[rows, :]
        wide = here.astype(F32)
        scale = lax.rsqrt(jnp.mean(wide * wide, axis=-1, keepdims=True) + EPS)
        rs_ref[rows, :] = jnp.broadcast_to(scale, (STEP, 128))
        xl_theirs[rows, :] = (nn(here, w_theirs[...]) * scale).astype(BF)
        xl_mine[rows, :] = (nn(here, w_mine[...]) * scale).astype(BF)


def y_proj_kernel(x_ref, rs_ref, w_mine, w_theirs, yp_ref):
    for k in range(ROWS // STEP):
        rows = slice(k * STEP, k * STEP + STEP)
        scale = rs_ref[rows, 0:1]
        yp_ref[rows, :CHAN] = nn(x_ref[rows, :], w_mine[...]) * scale
        yp_ref[rows, CHAN:] = nn(x_ref[rows, :], w_theirs[...]) * scale


def saved_parts(ref):
    return [ref.at[(TOKENS + 8) * k : (TOKENS + 8) * (k + 1), :] for k in range(4)]


def recurrence_kernel(pos, mine_ref, theirs_ref, c_ref, edge_ref, *refs):
    hid_mine, hid_theirs, saved_out, saved_ref, a_s, push_s, cum_s, copy_sems = refs
    xl_s, rg_s, op_s, hid_s = saved_parts(saved_ref)
    parts = list(zip((xl_s, rg_s, op_s, hid_s), saved_parts(saved_out)))
    xl_s[0:8, :] = edge_ref[0:8, :]
    hid_s[0:8, :] = edge_ref[8:16, :]
    for y in range(4):
        for rc, ref in enumerate((mine_ref, theirs_ref)):
            at = pl.multiple_of(8 + time_start(pos, y, rc), 8)
            xl_s[pl.ds(at, BLOCK), :] = ref[BLOCK * y : BLOCK * y + BLOCK, :].astype(F32)
    small = small_rows(c_ref)
    gate_w = c_ref[:, 0:CHAN]
    decay_scale = -8.0 * softplus(small[7:8, :])
    for k in range(TOKENS // STEP):
        lo = k * STEP
        conv = small[4:5, :]
        for tap in range(4):
            conv = conv + small[tap : tap + 1, :] * xl_s[lo + 8 - tap : lo + 8 - tap + STEP, :]
        conv = conv.astype(BF)
        raw = [nn(conv[:, 128 * h : 128 * h + 128], gate_w[128 * h : 128 * h + 128, :]) for h in (0, 1)]
        rg = jax.nn.sigmoid(jnp.concatenate([raw[0][:, :128], raw[1][:, :128]], axis=1) + small[5:6, :])
        op = jax.nn.sigmoid(jnp.concatenate([raw[0][:, 128:], raw[1][:, 128:]], axis=1) + small[6:7, :])
        log_a = decay_scale * rg
        put_rows(a_s, lo, STEP, jnp.exp(log_a))
        put_rows(push_s, lo, STEP, jnp.sqrt(neg_expm1(2.0 * log_a)) * op * conv.astype(F32))
        rg_s[lo : lo + STEP, :] = rg
        op_s[lo : lo + STEP, :] = op
    saves = start_loads(parts[:3], copy_sems, 0)
    state, product = chain(a_s, 0, push_s, cum_s, False)
    entering = edge_ref[15:16, :]
    for k in range(8):
        lo = k * BLOCK
        hidden = get_rows(push_s, lo, BLOCK) + get_rows(cum_s, lo, BLOCK) * entering
        entering = state[k : k + 1, :] + product[k : k + 1, :] * entering
        hid_s[8 + lo : 8 + lo + BLOCK, :] = hidden
    saves += start_loads(parts[3:], copy_sems, 3)
    for y in range(4):
        for rc, ref in enumerate((hid_mine, hid_theirs)):
            at = pl.multiple_of(8 + time_start(pos, y, rc), 8)
            ref[BLOCK * y : BLOCK * y + BLOCK, :] = hid_s[pl.ds(at, BLOCK), :].astype(BF)
    wait_all(saves)


def out_proj_kernel(pos, hid_mine, hid_theirs, yp_ref, o_mine, o_theirs, *refs):
    outs, mix_ref, part_s, sems = refs[:4], refs[4], refs[5], refs[6]
    for k in range(ROWS // STEP):
        rows = slice(k * STEP, k * STEP + STEP)
        act, _ = gelu_parts(yp_ref[rows, :])
        hidden = jnp.concatenate([hid_mine[rows, :], hid_theirs[rows, :]], axis=1)
        mixed = (hidden.astype(F32) * act).astype(BF)
        mix_ref[rows, :] = mixed
        part = nn(mixed[:, :CHAN], o_mine[...]) + nn(mixed[:, CHAN:], o_theirs[...])
        part_s[rows, :] = part.astype(BF)
    wait_all(start_out(pos, part_s, outs, sems))


def mlp_pre_kernel(pos, *refs):
    x_refs, c_refs, w_ref, far_ref, (xc_ref, *pres), (near_ref, copy_sems) = refs[:4], refs[4:8], *refs[8:10], refs[10:13], refs[13:]
    loads = start_in(pos, x_refs, xc_ref.at[:ROWS, :], copy_sems)
    other = start_loads(((far_ref, near_ref),), copy_sems, 8)
    later = start_in(pos, c_refs, xc_ref.at[ROWS:, :], copy_sems, 4)
    wait_all(loads)
    for weights, pre_ref in zip((w_ref, near_ref), pres):
        if weights is near_ref:
            wait_all(other)
        for k in range(ROWS // STEP):
            rows = slice(k * STEP, k * STEP + STEP)
            pre_ref[rows, :] = nn(xc_ref[rows, :], weights[...])
    wait_all(later)


def mlp_kernel(pos, xc_ref, *refs):
    pres, (w_ref, d_ref, far_ref, d_theirs), outs, saves = refs[:2], refs[2:6], refs[6:10], refs[10:12]
    part_s, near_ref, copy_sems = refs[12:]
    weights = ((w_ref, d_ref), (near_ref, d_theirs))
    loads = start_loads(((far_ref, near_ref),), copy_sems, 4)

    @pl.loop(0, ROWS // STEP)
    def _(k):
        rows = pl.ds(pl.multiple_of(k * STEP, STEP), STEP)
        cot = xc_ref[pl.ds(pl.multiple_of(ROWS + k * STEP, STEP), STEP), :]
        part = None
        for (w_ref, d_ref), pre_ref, save_ref in zip(weights, pres, saves):
            d_product = nt(cot, d_ref[...])
            last = pre_ref[rows, 1024:1152]
            gate = jnp.concatenate([pre_ref[rows, :512], last], axis=1)
            up = jnp.concatenate([pre_ref[rows, 512:1024], pltpu.roll(last, 64, 1)], axis=1)
            act, slope = gelu_parts(gate)
            save_ref[rows, :HID_PAD] = (act * up).astype(BF)
            d_gate = d_product * up * slope
            d_up = d_product * act
            d_last = d_gate[:, 512:] + pltpu.roll(d_up[:, 512:], 64, 1)
            d_pre = jnp.concatenate([d_gate[:, :512], d_up[:, :512], d_last], axis=1).astype(BF)
            save_ref[rows, HID_PAD:] = d_pre
            if w_ref is near_ref:

                @pl.when(k == 0)
                def _():
                    wait_all(loads)

            term = nt(d_pre, w_ref[...])
            part = term if part is None else part + term
        part_s[rows, :] = part.astype(BF)

    wait_all(start_out(pos, part_s, outs, copy_sems))


def mlp_out_kernel(pos, prod_mine, prod_theirs, d_mine, d_theirs, *refs):
    outs, part_s, copy_sems = refs[:4], refs[4], refs[5]
    for k in range(ROWS // STEP):
        rows = slice(k * STEP, k * STEP + STEP)
        part = nn(prod_mine[rows, :HID_PAD], d_mine[...]) + nn(prod_theirs[rows, :HID_PAD], d_theirs[...])
        part_s[rows, :] = part.astype(BF)
    wait_all(start_out(pos, part_s, outs, copy_sems))


def mlp_grads_kernel(*refs):
    xc_refs, save_refs, (out_ref, out_s, w_s, d_s, copy_sems) = refs[:2], refs[2:4], refs[4:]
    for k in range(HID_PAD // 128):
        cols = slice(128 * k, 128 * k + 128)
        grads = [tn(save[:, cols], xc[ROWS:, :]) for xc, save in zip(xc_refs, save_refs)]
        d_s[cols, :] = grads[0] + grads[1]
    saves = []
    for k in range(WIDTH // 384):
        cols = slice(384 * k, 384 * k + 384)
        grads = [tn(xc[:ROWS, cols], save[:, HID_PAD:]) for xc, save in zip(xc_refs, save_refs)]
        w_s[cols, :] = (grads[0] + grads[1]).astype(BF)
        for p in range(4 * k, 4 * k + 4):
            for j in range(3):
                at = p * MLP_ROWS + 96 * j
                out_s[at : at + 96, :] = w_s[96 * p : 96 * p + 96, 384 * j : 384 * j + 384]
            for j in range(4):
                at = p * MLP_ROWS + 288 + 48 * j
                out_s[at : at + 48, :] = d_s[36 * p : 36 * p + 48, 384 * j : 384 * j + 384].astype(BF)
        part = slice(4 * MLP_ROWS * k, 4 * MLP_ROWS * (k + 1))
        saves += start_loads(((out_s.at[part, :], out_ref.at[part, :]),), copy_sems, k)
    wait_all(saves)


def mixed_backward_kernel(pos, *refs):
    d_refs, (o_mine, o_theirs, yp_ref, hid_mine, hid_theirs, rs_ref) = refs[:4], refs[4:10]
    mine_ref, theirs_ref, d_s, o_s, copy_sems = refs[10:]
    o_near = (o_s.at[:CHAN, :], o_s.at[CHAN:, :])
    loads = start_loads(list(zip((o_mine, o_theirs), o_near)), copy_sems, 4)
    wait_all(start_in(pos, d_refs, d_s, copy_sems) + loads)
    sides = ((o_near[0], hid_mine, mine_ref), (o_near[1], hid_theirs, theirs_ref))
    for k in range(ROWS // STEP):
        rows = slice(k * STEP, k * STEP + STEP)
        here = d_s[rows, :]
        scale = rs_ref[rows, 0:1]
        for h, (o_ref, hid_ref, out_ref) in enumerate(sides):
            d_mixed = nt(here, o_ref[...])
            act, slope = gelu_parts(yp_ref[rows, CHAN * h : CHAN * h + CHAN])
            out_ref[rows, :CHAN] = (d_mixed * act).astype(BF)
            out_ref[rows, CHAN:] = (d_mixed * hid_ref[rows, :].astype(F32) * slope * scale).astype(BF)


def out_grads_kernel(mix_ref, d_ref, mine_ref, theirs_ref):
    theirs_ref[...] = tn(mix_ref[:, CHAN:], d_ref[...]).astype(BF)
    mine_ref[...] = tn(mix_ref[:, :CHAN], d_ref[...]).astype(BF)


def chain_backward_kernel(pos, *refs):
    (mine_ref, theirs_ref, c_ref, saved_ref) = refs[:4]
    dx_mine, dx_theirs, gs_ref, dh_s, cum_s, dc_s, dx_s, acc_s, a_ref, saved_s, copy_sems = refs[4:]
    xl_ref, rg_ref, op_ref, hid_ref = saved_parts(saved_s)
    order = (1, 0, 2, 3)
    loads = [(saved_parts(saved_ref)[k], saved_parts(saved_s)[k]) for k in order]
    loads = start_loads(loads, copy_sems, 0)
    small = small_rows(c_ref)
    gate_w = c_ref[:, 0:CHAN]
    decay = small[7:8, :]
    decay_scale = -8.0 * softplus(decay)
    for y in range(4):
        for rc, ref in enumerate((mine_ref, theirs_ref)):
            block = ref[BLOCK * y : BLOCK * y + BLOCK, :CHAN].astype(F32)
            at = pl.multiple_of(time_start(pos, y, rc), BLOCK)
            for k in (0, 1):
                side(dh_s, k)[pl.ds(at, BLOCK), :] = block[:, 128 * k : 128 * k + 128]
    loads[0].wait()
    for k in range(TOKENS // STEP):
        put_rows(a_ref, k * STEP, STEP, jnp.exp(decay_scale * rg_ref[k * STEP : k * STEP + STEP, :]))
    put_rows(a_ref, TOKENS, 8, jnp.zeros((8, CHAN), F32))
    state, product = chain(a_ref, 1, dh_s, cum_s, True)
    wait_all(loads[1:])
    decay_slope = -8.0 * jax.nn.sigmoid(decay)
    acc_s[...] = jnp.zeros_like(acc_s)
    dc_s[TOKENS:, :] = jnp.zeros((8, CHAN), F32)
    later = [None] * 8
    entering = jnp.zeros((1, CHAN), F32)
    for k in reversed(range(8)):
        later[k] = entering
        entering = state[k : k + 1, :] + product[k : k + 1, :] * entering
    gate_grads = [jnp.zeros((128, CHAN), F32) for _ in (0, 1)]
    for k in range(8):
        lo = k * BLOCK
        rows = slice(lo, lo + BLOCK)
        state_grad = get_rows(dh_s, lo, BLOCK) + get_rows(cum_s, lo, BLOCK) * later[k]
        shifted = [xl_ref[lo + 8 - tap : lo + 8 - tap + BLOCK, :] for tap in range(4)]
        conv = small[4:5, :]
        for tap in range(4):
            conv = conv + small[tap : tap + 1, :] * shifted[tap]
        conv_low = conv.astype(BF)
        conv = conv_low.astype(F32)
        rg, op, a = rg_ref[rows, :], op_ref[rows, :], get_rows(a_ref, lo, BLOCK)
        root = jnp.sqrt(neg_expm1(2.0 * decay_scale * rg))
        pushed = state_grad * op
        d_log = a * (state_grad * hid_ref[lo + 7 : lo + 7 + BLOCK, :] - pushed * conv * a / root)
        d_rg = d_log * rg
        acc_s[7:8, :] += jnp.sum(d_rg, axis=0, keepdims=True) * decay_slope
        d_raw = decay_scale * d_rg * (1.0 - rg)
        d_open = pushed * root * conv * (1.0 - op)
        acc_s[5:6, :] += jnp.sum(d_raw, axis=0, keepdims=True)
        acc_s[6:7, :] += jnp.sum(d_open, axis=0, keepdims=True)
        d_raw, d_open = d_raw.astype(BF), d_open.astype(BF)
        back = []
        for h in (0, 1):
            cols = slice(128 * h, 128 * h + 128)
            d_block = jnp.concatenate([d_raw[:, cols], d_open[:, cols]], axis=1)
            gate_grads[h] = gate_grads[h] + tn(conv_low[:, cols], d_block)
            back.append(nt(d_block, gate_w[cols, :]))
        d_conv = pushed * root + jnp.concatenate(back, axis=1)
        dc_s[rows, :] = d_conv
        acc_s[4:5, :] += jnp.sum(d_conv, axis=0, keepdims=True)
        for tap in range(4):
            acc_s[tap : tap + 1, :] += jnp.sum(d_conv * shifted[tap], axis=0, keepdims=True)
    for k in range(8):
        lo = k * BLOCK
        d_x = small[0:1, :] * dc_s[lo : lo + BLOCK, :]
        for tap in range(1, 4):
            d_x = d_x + small[tap : tap + 1, :] * dc_s[lo + tap : lo + tap + BLOCK, :]
        dx_s[lo : lo + BLOCK, :] = d_x
    for y in range(4):
        for rc, ref in enumerate((dx_mine, dx_theirs)):
            at = pl.multiple_of(time_start(pos, y, rc), BLOCK)
            ref[BLOCK * y : BLOCK * y + BLOCK, :] = dx_s[pl.ds(at, BLOCK), :].astype(BF)
    for h in (0, 1):
        gs_ref[128 * h : 128 * h + 128, 0:256] = gate_grads[h].astype(BF)
    gs_ref[:, 256:384] = acc_s[...].T.astype(BF)


def normed_backward_kernel(pos, dx_mine, dx_theirs, dy_mine, dy_theirs, rs_ref, *refs):
    weights, outs, part_s, copy_sems = refs[:4], refs[4:8], refs[8], refs[9]
    for k in range(ROWS // STEP):
        rows = slice(k * STEP, k * STEP + STEP)
        scale = rs_ref[rows, 0:1]
        lows = [(dx_ref[rows, :].astype(F32) * scale).astype(BF) for dx_ref in (dx_mine, dx_theirs)]
        lows += [dy_mine[rows, CHAN:], dy_theirs[rows, CHAN:]]
        part_s[rows, :] = sum(nt(low, w_ref[...]) for low, w_ref in zip(lows, weights)).astype(BF)
    wait_all(start_out(pos, part_s, outs, copy_sems))


def cols_grads_kernel(*refs):
    x_refs, dx_refs, dy_refs, rs_ref = refs[:2], refs[2:4], refs[4:6], refs[6]
    go_mine, go_theirs, gs_ref, out_ref, out_s, wide_s, rest_s, copy_sems = refs[7:]
    rest_s[:, 0:WIDTH] = (go_mine[...].astype(F32) + go_theirs[...].astype(F32)).astype(BF)
    rest_s[:, WIDTH:C_WIDTH] = gs_ref[...]
    rest_s[:, C_WIDTH:] = jnp.zeros((CHAN, 8 * REST - C_WIDTH), BF)
    wide = x_refs[1][...].astype(F32)
    scales = (rs_ref[:, 0:1], lax.rsqrt(jnp.mean(wide * wide, axis=-1, keepdims=True) + EPS))
    lows = [
        jnp.concatenate([(dx[...].astype(F32) * scale).astype(BF), dy[:, CHAN:]], axis=1)
        for dx, dy, scale in zip(dx_refs, dy_refs, scales)
    ]
    saves = []
    for k in range(WIDTH // 384):
        rows = slice(384 * k, 384 * k + 384)
        wide_s[rows, :] = tn(x_refs[0][:, rows], lows[0]) + tn(x_refs[1][:, rows], lows[1])
        for i in range(32 * k, 32 * k + 32):
            block = [wide_s[12 * i : 12 * i + 12, 128 * t : 128 * t + 128] for t in range(4)]
            out_s[i, 0:COLS_ROWS, :] = jnp.concatenate(block).astype(BF)
            few = slice(16 * (i // 8), 16 * (i // 8) + 16)
            for t in range(2):
                at = REST * (i % 8) + 128 * t
                out_s[i, COLS_ROWS + 16 * t : COLS_ROWS + 16 * t + 16, :] = rest_s[few, at : at + 128]
        part = slice(32 * k, 32 * k + 32)
        saves += start_loads(((out_s.at[part], out_ref.at[part]),), copy_sems, k)
    wait_all(saves)


def add_terms(terms):
    out = terms[0][...].astype(F32)
    for term in terms[1:]:
        out = out + term[...].astype(F32)
    return out


def residual_kernel(x_ref, *refs):
    terms, (res_out, scale_out, low_ref, res_s, scale_s, copy_sems) = refs[:4], refs[4:]
    residual = x_ref[...].astype(F32) + add_terms(terms)
    scale = lax.rsqrt(jnp.mean(residual * residual, axis=-1, keepdims=True) + EPS)
    res_s[...] = residual
    scale_s[...] = jnp.broadcast_to(scale, (BLOCK, 128))
    saves = start_loads(((res_s, res_out), (scale_s, scale_out)), copy_sems, 0)
    low_ref[...] = (residual * scale).astype(BF)
    wait_all(saves)


def d_residual_kernel(cot_ref, res_ref, scale_ref, *refs):
    terms, (d_out, low_ref, d_s, cot_s, copy_sems) = refs[:4], refs[4:]
    loads = start_loads(((cot_ref, cot_s),), copy_sems, 1)
    d_normed = add_terms(terms)
    scale = scale_ref[:, 0:1]
    normed = res_ref[...] * scale
    along = jnp.mean(normed * d_normed, axis=-1, keepdims=True)
    wait_all(loads)
    d_residual = cot_s[...].astype(F32) + scale * (d_normed - normed * along)
    d_s[...] = d_residual
    saves = start_loads(((d_s, d_out),), copy_sems, 0)
    low_ref[...] = d_residual.astype(BF)
    wait_all(saves)


def input_grad_kernel(x_ref, d_ref, *refs):
    terms, out_ref = refs[:4], refs[4]
    scaled = add_terms(terms)
    x = x_ref[...].astype(F32)
    power = 1.0 / (jnp.mean(x * x, axis=-1, keepdims=True) + EPS)
    along = jnp.mean(x * scaled, axis=-1, keepdims=True) * power
    out_ref[...] = (d_ref[...] + scaled - x * along).astype(BF)


def layer_out_kernel(res_ref, *refs):
    terms, out_ref = refs[:4], refs[4]
    out_ref[...] = (res_ref[...] + add_terms(terms)).astype(BF)


def dp_total(got_ref, lo, count):
    out = got_ref[0, lo : lo + count, :].astype(F32)
    for k in range(1, 16):
        out = out + got_ref[k, lo : lo + count, :].astype(F32)
    return out


def finish_cols_kernel(got_ref, gain_ref, x_ref, y_ref, gx_ref, gy_ref, gain_grad_ref, wide_s):
    for s in range(8):
        wide_s[COLS_ROWS * s : COLS_ROWS * s + COLS_ROWS, :] = dp_total(got_ref, SUM_ROWS * s, COLS_ROWS)
    gain = column(gain_ref)
    along = jnp.zeros((12, 128), F32)
    for s in range(8):
        for t in range(4):
            at = CHAN * s + 128 * (t % 2)
            lo = COLS_ROWS * s + 12 * t
            grad = wide_s[lo : lo + 12, :]
            w_ref, g_ref = (x_ref, gx_ref) if t < 2 else (y_ref, gy_ref)
            along = along + grad * w_ref[:, at : at + 128].astype(F32)
            g_ref[:, at : at + 128] = grad * gain
    gain_grad_ref[...] = as_row(jnp.sum(along, axis=1, keepdims=True))


def mlp_back_kernel(got_ref, cols_ref, down_ref, wide_s):
    for j in range(3):
        wide_s[:, 384 * j : 384 * j + 384] = got_ref[96 * j : 96 * j + 96, :].astype(F32)
    for s in range(8):
        block = jnp.concatenate([wide_s[12 * s : 12 * s + 12, :], jnp.zeros((4, GATED), F32)])
        cols_ref[s] = block.astype(BF)
    for j in range(4):
        down_ref[:, 384 * j : 384 * j + 384] = got_ref[288 + 48 * j : 336 + 48 * j, :]


def rest_back_kernel(cols_ref, got_ref, out_ref):
    out_ref[:, :, :GATED] = cols_ref[...]
    for s in range(8):
        for t in range(2):
            tile = dp_total(got_ref, SUM_ROWS * s + COLS_ROWS + 16 * t, 16)
            out_ref[s, :, GATED + 128 * t : GATED + 128 * t + 128] = tile.astype(BF)


def mlp_finish_kernel(*refs):
    got_ref, gain_ref, gate_ref, up_ref, g_gate_ref, g_up_ref, gain_grad_ref = refs
    gain = column(gain_ref)
    along = jnp.zeros((12, 1), F32)
    for s in range(8):
        block = got_ref[s, :, :GATED].astype(F32)[:12]
        lo = HID * s
        cols = slice(lo, lo + HID)
        grad_gate = jnp.concatenate([block[:, :512], block[:, 1024:1088]], axis=1)
        grad_up = jnp.concatenate([block[:, 512:1024], block[:, 1088:]], axis=1)
        terms = grad_gate * gate_ref[:, cols].astype(F32) + grad_up * up_ref[:, cols].astype(F32)
        along = along + jnp.sum(terms, axis=1, keepdims=True)
        g_gate_ref[:, cols] = grad_gate * gain
        g_up_ref[:, cols] = grad_up * gain
    gain_grad_ref[...] = as_row(along)


def rest_join_kernel(got_ref, down_ref, out_ref):
    for s in range(8):
        out_ref[:, REST * s : REST * s + REST] = got_ref[s, :, GATED:]
    for j in range(3):
        out_ref[:, 8 * REST + WIDTH * j : 8 * REST + WIDTH * j + WIDTH] = down_ref[16 * j : 16 * j + 16, :]


def finish_rest_kernel(got_ref, out_ref, gate_w_ref, taps_ref, bias_ref, gate_bias_ref, decay_ref, down_ref):
    for j in range(3):
        rows = min(16, 36 - 16 * j)
        tile = got_ref[:, 8 * REST + WIDTH * j : 8 * REST + WIDTH * j + WIDTH]
        down_ref[16 * j : 16 * j + rows, :] = tile.astype(F32)[:rows]
    out_ref[...] = got_ref[:, 0:WIDTH].astype(F32)
    gate_w_ref[...] = got_ref[:, 1536:1792].astype(F32)
    small = got_ref[:, 1792:1920].astype(F32)
    rows = [as_row(small[:, k : k + 1]) for k in range(8)]
    for k in range(4):
        taps_ref[k : k + 1, :] = rows[k]
    bias_ref[...] = rows[4]
    for k in range(2):
        gate_bias_ref[k : k + 1, :] = rows[5 + k]
    decay_ref[...] = rows[7]


def shape(dims, dtype):
    return jax.ShapeDtypeStruct(dims, dtype)


def sems(count):
    return pltpu.SemaphoreType.DMA((count,))


def size(dims, dtype):
    return math.prod(dims) * jnp.dtype(dtype).itemsize


def call(kernel, args, outs, scratch=(), any_args=(), any_outs=(), far_outs=(), micros=0, more=8):
    held = sum(size(a.shape, a.dtype) for k, a in enumerate(args) if k not in any_args)
    held += sum(size(*o) for k, o in enumerate(outs) if k not in any_outs)
    held += sum(size(s.shape, s.dtype) for s in scratch if s.memory_space == pltpu.VMEM)
    args = [pltpu.with_memory_space_constraint(a, pltpu.HBM) if k in any_args else a for k, a in enumerate(args)]
    in_specs = [SMEM if a.dtype == jnp.int32 else HBM if k in any_args else VMEM for k, a in enumerate(args)]
    return pl.pallas_call(
        kernel,
        name=kernel.__name__.removesuffix("_kernel"),
        in_specs=in_specs,
        out_specs=[ANY if k in any_outs else VMEM for k in range(len(outs))],
        out_shape=[pltpu.HBM(*o) if k in far_outs else shape(*o) for k, o in enumerate(outs)],
        scratch_shapes=scratch,
        cost_estimate=pl.CostEstimate(flops=int(micros * 10**9), bytes_accessed=0, transcendentals=0),
        compiler_params=pltpu.CompilerParams(vmem_limit_bytes=min(held + (more << 20), 60 << 20)),
    )(*args)


PART = ((BLOCK, WIDTH), BF)
PARTS = [PART] * 4
PART_S = pltpu.VMEM((ROWS, WIDTH), BF)
CHAIN_S = pltpu.VMEM((2 * TOKENS, 128), F32)


def per_device(
    inputs,
    cotangent,
    resets,
    start_state,
    conv_history,
    norm_gain,
    proj_x,
    proj_y,
    conv_taps,
    conv_bias,
    gate_weight,
    gate_bias,
    decay_param,
    proj_out,
    mlp_gain,
    mlp_gate,
    mlp_up,
    mlp_down,
):
    pos = jnp.stack([lax.axis_index(a) for a in DP_SEQ]).astype(jnp.int32)
    flat_in = inputs[0]
    flat_cot = cotangent[0]
    gain_one = norm_gain[None]
    gain_two = mlp_gain[None]

    (rest,) = call(
        pack_rows_kernel,
        (proj_out, gate_weight, conv_taps.T, conv_bias[None], gate_bias.T, decay_param[None]),
        [((16, C_WIDTH), BF)],
        more=60,
    )
    rest, late_x, late_down = tied(rest, proj_x, mlp_down)
    rest = transposed_devices(rest, False)
    blocks = call(
        pack_cols_kernel,
        (pos, gain_one, gain_two, late_x, proj_y, mlp_gate, mlp_up),
        [((16, SENT), BF)] * 8,
        [pltpu.VMEM((8, 16, SENT), F32)],
        more=60,
    )
    early, late = call(
        shard_kernel,
        (pos, *exchanged(blocks), rest),
        [((EARLY, 128), BF), ((LATE, 128), BF)],
        [pltpu.VMEM((8, 16, SENT), F32), pltpu.VMEM((96, SENT), F32)],
    )
    late = lax.all_gather(late, DP, axis=0, tiled=True)
    early, early_in, late_down = tied(early, flat_in, late_down)
    x_pieces = gather_rows(early_in)
    down = transposed_devices(late_down, False)
    early = lax.all_gather(early, DP, axis=0, tiled=True)
    early, x_pieces, down = tied(early, x_pieces, down)
    x_mine, c_mine = call(early_unpack_kernel, (early,), [((WIDTH, CHAN), BF), ((CHAN, SMALL), BF)])
    (down,) = call(down_pack_kernel, (down,), [((DOWN_ROWS, MLP_LANES), BF)])
    x_mine, late_cot, down = tied(x_mine, flat_cot, down)
    down = lax.all_gather(down, DP, axis=0, tiled=True)
    x_theirs = swapped(x_mine)
    c_near = [hop(late_cot, "y", r) for r in PIECES[1:3]]

    keep = (1 - resets).astype(F32)
    place = lax.axis_index(SEQ) * CHAN
    history = lax.dynamic_slice(conv_history[0].astype(F32), (0, place), (3, CHAN)) * keep
    initial = lax.dynamic_slice(start_state, (0, place), (1, CHAN)) * keep
    edges = jnp.concatenate([jnp.zeros((5, CHAN), F32), history, jnp.zeros((7, CHAN), F32), initial])
    xl_mine, xl_theirs, x_all, rs = call(
        in_proj_kernel,
        (pos, *x_pieces, x_mine, x_theirs),
        [((ROWS, CHAN), BF)] * 2 + [((ROWS, WIDTH), BF), ((ROWS, 128), F32)],
        [sems(4)],
        any_args=range(1, 5),
        micros=8,
    )
    xl_got, c_near, late_cot = tied(swapped(xl_theirs), c_near, late_cot)
    c_far = hop(late_cot, "y", PIECES[3])
    hid_mine, hid_theirs, saved = call(
        recurrence_kernel,
        (pos, xl_mine, xl_got, c_mine, edges),
        [((ROWS, CHAN), BF)] * 2 + [((4 * (TOKENS + 8), CHAN), F32)],
        [pltpu.VMEM((4 * (TOKENS + 8), CHAN), F32), CHAIN_S, CHAIN_S, CHAIN_S, sems(4)],
        any_outs=[2],
        far_outs=[2],
        micros=8,
    )
    hid_theirs = swapped(hid_theirs)
    hid_mine, c_far, late = tied(hid_mine, c_far, late)
    c_pieces = [flat_cot, *c_near, c_far]
    y_mine, o_mine = call(
        late_unpack_kernel,
        (late,),
        [((WIDTH, CHAN), BF), ((CHAN, WIDTH), BF)],
        [pltpu.VMEM((16 * COLS, 128), BF), sems(16)],
        any_args=range(1),
    )
    y_theirs, o_theirs = swapped(y_mine), swapped(o_mine)
    (yp,) = call(y_proj_kernel, (x_all, rs, y_mine, y_theirs), [((ROWS, 2 * CHAN), F32)], micros=8)
    *parts, mix = call(
        out_proj_kernel,
        (pos, hid_mine, hid_theirs, yp, o_mine, o_theirs),
        PARTS + [((ROWS, 2 * CHAN), BF)],
        [PART_S, sems(4)],
        any_outs=range(4),
        micros=1.2,
    )
    terms = scatter_rows(parts)
    _, late = tied(parts, late)
    (w_up,) = call(
        cols_unpack_kernel,
        (late,),
        [((WIDTH, GATED), BF)],
        [pltpu.VMEM((16 * 864, 128), BF), sems(16)],
        any_args=range(1),
    )
    up_theirs = swapped(w_up)
    terms, w_up = tied(terms, w_up)
    residual, scale_two, normed_two = call(
        residual_kernel,
        (flat_in, *terms),
        [((BLOCK, WIDTH), F32), ((BLOCK, 128), F32), PART],
        [pltpu.VMEM((BLOCK, WIDTH), F32), pltpu.VMEM((BLOCK, 128), F32), sems(2)],
        any_outs=range(2),
        far_outs=range(2),
        micros=30,
    )

    _, down = tied(normed_two, down)
    (w_down,) = call(down_unpack_kernel, (down,), [((HID_PAD, WIDTH), BF)], [pltpu.VMEM((HID, WIDTH), F32)])
    down_theirs = swapped(w_down)
    tokens, pre_mine, pre_theirs = call(
        mlp_pre_kernel,
        (pos, *gather_rows(normed_two), *c_pieces, w_up, up_theirs),
        [((2 * ROWS, WIDTH), BF)] + [((ROWS, GATED), F32)] * 2,
        [pltpu.VMEM((WIDTH, GATED), BF), sems(9)],
        any_args=(*range(1, 9), 10),
        micros=20,
    )
    tokens_got = swapped(tokens)
    *parts, save_mine, save_theirs = call(
        mlp_kernel,
        (pos, tokens, pre_mine, pre_theirs, w_up, w_down, up_theirs, down_theirs),
        PARTS + [((ROWS, HID_PAD + GATED), BF)] * 2,
        [PART_S, pltpu.VMEM((WIDTH, GATED), BF), sems(5)],
        any_args=[6],
        any_outs=range(4),
        micros=5,
    )
    out_parts = call(
        mlp_out_kernel,
        (pos, save_mine, save_theirs, w_down, down_theirs),
        PARTS,
        [PART_S, sems(4)],
        any_outs=range(4),
        far_outs=range(4),
        micros=15,
    )
    terms = scatter_rows(parts)
    save_got = swapped(save_theirs)
    save_got, out_parts = tied(save_got, out_parts)
    (mlp_grads,) = call(
        mlp_grads_kernel,
        (tokens, tokens_got, save_mine, save_got),
        [((16 * MLP_ROWS, MLP_LANES), BF)],
        [
            pltpu.VMEM((16 * MLP_ROWS, MLP_LANES), BF),
            pltpu.VMEM((WIDTH, GATED), BF),
            pltpu.VMEM((HID_PAD, WIDTH), F32),
            sems(4),
        ],
        any_outs=range(1),
        far_outs=range(1),
        micros=15,
    )
    terms, mlp_grads = tied(terms, mlp_grads)
    mlp_sum = lax.psum_scatter(mlp_grads, DP, scatter_dimension=0, tiled=True)
    d_residual, d_out = call(
        d_residual_kernel,
        (flat_cot, residual, scale_two, *terms),
        [((BLOCK, WIDTH), F32), PART],
        [pltpu.VMEM((BLOCK, WIDTH), F32), pltpu.VMEM((BLOCK, WIDTH), BF), sems(2)],
        any_args=[0],
        any_outs=range(1),
        far_outs=range(1),
    )

    d_out, late_x_all = tied(d_out, x_all)
    d_pieces, all_theirs = tied(gather_rows(d_out), swapped(late_x_all))
    back_mine, back_theirs, d_all = call(
        mixed_backward_kernel,
        (pos, *d_pieces, o_mine, o_theirs, yp, hid_mine, hid_theirs, rs),
        [((ROWS, 2 * CHAN), BF)] * 2 + [((ROWS, WIDTH), BF)],
        [pltpu.VMEM((2 * CHAN, WIDTH), BF), sems(6)],
        any_args=(5, 6),
        micros=2,
    )
    back_got = swapped(back_theirs)
    dx_mine, dx_theirs, g_small = call(
        chain_backward_kernel,
        (pos, back_mine, back_got, c_mine, saved),
        [((ROWS, CHAN), BF)] * 2 + [((CHAN, 384), BF)],
        [
            CHAIN_S,
            CHAIN_S,
            pltpu.VMEM((TOKENS + 8, CHAN), F32),
            pltpu.VMEM((TOKENS, CHAN), F32),
            pltpu.VMEM((128, CHAN), F32),
            pltpu.VMEM((2 * TOKENS + 16, 128), F32),
            pltpu.VMEM((4 * (TOKENS + 8), CHAN), F32),
            sems(4),
        ],
        any_args=[4],
        micros=20,
    )
    dx_got = swapped(dx_theirs)
    parts = call(
        normed_backward_kernel,
        (pos, dx_mine, dx_got, back_mine, back_theirs, rs, x_mine, x_theirs, y_mine, y_theirs),
        PARTS,
        [PART_S, sems(4)],
        any_outs=range(4),
    )
    terms = scatter_rows(parts)
    _, late_mix = tied(parts, mix)
    go_mine, go_theirs = call(out_grads_kernel, (late_mix, d_all), [((CHAN, WIDTH), BF)] * 2)
    (g_cols,) = call(
        cols_grads_kernel,
        (x_all, all_theirs, dx_mine, dx_theirs, back_mine, back_got, rs, go_mine, swapped(go_theirs), g_small),
        [((128, SUM_ROWS, 128), BF)],
        [
            pltpu.VMEM((128, SUM_ROWS, 128), BF),
            pltpu.VMEM((WIDTH, 2 * CHAN), F32),
            pltpu.VMEM((CHAN, 8 * REST), BF),
            sems(4),
        ],
        any_outs=range(1),
        far_outs=range(1),
    )
    g_cols = lax.all_to_all(g_cols, DP_SEQ, 0, 0, tiled=True).reshape(16, 8 * SUM_ROWS, 128)
    terms, mlp_sum = tied(terms, mlp_sum)
    blocks, down_back = call(
        mlp_back_kernel,
        (mlp_sum,),
        [((8, 16, GATED), BF), ((48, WIDTH), BF)],
        [pltpu.VMEM((96, GATED), F32)],
        micros=100,
    )
    (input_grad,) = call(input_grad_kernel, (flat_in, d_residual, *terms), [PART])
    (blocks,) = call(rest_back_kernel, (blocks, g_cols), [((8, 16, GATED + REST), BF)])
    blocks = lax.all_to_all(blocks, SEQ, 0, 0, tiled=True)
    out_parts, _ = tied(out_parts, terms)
    out_terms = scatter_rows(out_parts)
    grad_x, grad_y, grad_norm_gain = call(
        finish_cols_kernel,
        (g_cols, gain_one, proj_x, proj_y),
        [((12, 8 * CHAN), F32)] * 2 + [((1, 12), F32)],
        [pltpu.VMEM((8 * COLS_ROWS, 128), F32)],
    )
    blocks, input_grad, grad_x = tied(blocks, input_grad, grad_x)
    (g_rest,) = call(rest_join_kernel, (blocks, down_back), [((16, 8 * REST + 3 * WIDTH), BF)])
    g_rest = transposed_devices(g_rest, True)
    grad_gate, grad_up, grad_mlp_gain = call(
        mlp_finish_kernel,
        (blocks, gain_two, mlp_gate, mlp_up),
        [((12, 8 * HID), F32)] * 2 + [((1, 12), F32)],
    )
    (layer_out,) = call(layer_out_kernel, (residual, *out_terms), [PART])
    g_rest, grad_gate, layer_out = tied(g_rest, grad_gate, layer_out)
    grad_out, grad_gate_w, grad_taps, grad_conv_bias, grad_gate_bias, grad_decay, grad_down = call(
        finish_rest_kernel,
        (g_rest,),
        [
            ((16, WIDTH), F32),
            ((16, CHAN), F32),
            ((4, 16), F32),
            ((1, 16), F32),
            ((2, 16), F32),
            ((1, 16), F32),
            ((36, WIDTH), F32),
        ],
    )
    return (
        layer_out[None],
        input_grad[None],
        grad_norm_gain[0],
        grad_x,
        grad_y,
        grad_taps.T,
        grad_conv_bias[0],
        grad_gate_w,
        grad_gate_bias.T,
        grad_decay[0],
        grad_out,
        grad_mlp_gain[0],
        grad_gate,
        grad_up,
        grad_down,
    )


def solution(mesh):
    finer = Mesh(mesh.devices.reshape(4, 4, 4, 2), DP_SEQ)
    rows = P(DP_SEQ, None)
    line = P(DP_SEQ)
    tokens = P(DP, SEQ, None)
    in_specs = (
        tokens,
        tokens,
        P(DP),
        P(DP, None),
        P(DP, None, None),
        line,
        rows,
        rows,
        rows,
        line,
        rows,
        rows,
        line,
        rows,
        line,
        rows,
        rows,
        rows,
    )
    out_specs = (
        tokens,
        tokens,
        line,
        rows,
        rows,
        rows,
        line,
        rows,
        rows,
        line,
        rows,
        line,
        rows,
        rows,
        rows,
    )
    return jax.shard_map(per_device, mesh=finer, in_specs=in_specs, out_specs=out_specs, check_vma=False)
```

```python
import math

import jax
import jax.numpy as jnp
from jax import lax
from jax.experimental import pallas as pl
from jax.experimental.pallas import tpu as pltpu
from jax.sharding import Mesh
from jax.sharding import PartitionSpec as P

BF = jnp.bfloat16
F32 = jnp.float32
EPS = 1e-06
GELU_C = 0.7978845608028654
GELU_K = 0.044715

TOKENS = 1024
ROWS = 512
BLOCK = 128
WIDTH = 1536
CHAN = 256
HID = 576
HID_PAD = 640
GATED = 2 * HID
STEP = 256
C_WIDTH = 1920
SENT = 2 * CHAN + GATED
SMALL = 384
EARLY = 240
COLS = 384
LATE = 1248
DOWN_ROWS = 192
COLS_ROWS = 48
SUM_ROWS = 80
REST = 256
MLP_ROWS = 480
MLP_LANES = 384

DP = ("z", "x")
SEQ = ("y", "c")
DP_SEQ = ("z", "x", "y", "c")

ANY = pl.BlockSpec(memory_space=pl.ANY)
HBM = pl.BlockSpec(memory_space=pltpu.HBM)
VMEM = pl.BlockSpec(memory_space=pltpu.VMEM)
SMEM = pl.BlockSpec(memory_space=pltpu.SMEM)

PIECES = (0, 1, 3, 2)
PLACES = [(ry, rc) for rc in (0, 1) for ry in (0, 2, 1, 3)]


def hop(value, axis, distance):
    size = lax.axis_size(axis)
    return lax.ppermute(value, axis, [(i, (i - distance) % size) for i in range(size)])


def added(one, two):
    return (one.astype(F32) + two.astype(F32)).astype(BF)


def swapped(value):
    return hop(value, "c", 1)


def gather_rows(block):
    return [block] + [hop(block, "y", r) for r in PIECES[1:]]


def scatter_rows(parts):
    return [parts[0]] + [hop(parts[r], "y", 4 - r) for r in (2, 1, 3)]


def tied(*values):
    return lax.optimization_barrier(values)


def transposed_devices(value, back):
    pairs = [(16 * s + d, 8 * d + s) for s in range(8) for d in range(16)]
    return lax.ppermute(value, DP_SEQ, [(b, a) for a, b in pairs] if back else pairs)


def exchanged(blocks):
    out = []
    for (ry, rc), block in zip(PLACES, blocks):
        route = [(2 * y + c, 2 * ((y + ry) % 4) + (c + rc) % 2) for y in range(4) for c in range(2)]
        out.append(lax.ppermute(block, SEQ, route) if (ry, rc) != (0, 0) else block)
    return out


def nn(a, b):
    return jnp.dot(a, b, preferred_element_type=F32)


def nt(a, b):
    return lax.dot_general(a, b, (((1,), (1,)), ((), ())), preferred_element_type=F32)


def tn(a, b):
    return lax.dot_general(a, b, (((0,), (0,)), ((), ())), preferred_element_type=F32)


def gelu_parts(v):
    sq = v * v
    t = jnp.tanh(GELU_C * v * (1.0 + GELU_K * sq))
    half = 0.5 * (1.0 + t)
    slope = half + 0.5 * v * (1.0 - t * t) * (GELU_C * (1.0 + 3.0 * GELU_K * sq))
    return v * half, slope


def neg_expm1(v):
    series = 1.0 + v * (1.0 / 7.0)
    for k in (6, 5, 4, 3, 2):
        series = 1.0 + v * (1.0 / k) * series
    return jnp.where(v > -0.35, -v * series, 1.0 - jnp.exp(v))


def softplus(v):
    e = jnp.exp(-jnp.abs(v))
    series = e * (1.0 - e * (1 / 2 - e * (1 / 3 - e * (1 / 4 - e * (1 / 5 - e * (1 / 6))))))
    return jnp.maximum(v, 0.0) + jnp.where(e < 0.05, series, jnp.log(1.0 + e))


def column(row_ref):
    n = row_ref.shape[1]
    square = jnp.broadcast_to(row_ref[...].astype(F32), (n, n))
    same = lax.broadcasted_iota(jnp.int32, (n, n), 0) == lax.broadcasted_iota(jnp.int32, (n, n), 1)
    return jnp.sum(jnp.where(same, square, 0.0), axis=1, keepdims=True)


def as_row(col):
    n = col.shape[0]
    square = jnp.broadcast_to(col, (n, n))
    same = lax.broadcasted_iota(jnp.int32, (n, n), 0) == lax.broadcasted_iota(jnp.int32, (n, n), 1)
    return jnp.sum(jnp.where(same, square, 0.0), axis=0, keepdims=True)


def place_of(pos, ry, rc):
    return lax.rem(pos[2] + ry, 4) * 2 + lax.rem(pos[3] + rc, 2)


def block_rows(pos, ry):
    return pl.ds(pl.multiple_of(lax.rem(pos[2] + ry, 4) * BLOCK, BLOCK), BLOCK)


def time_start(pos, y, rc):
    return (2 * y + lax.rem(pos[3] + rc, 2)) * BLOCK


def start_loads(pairs, sems, first):
    copies = []
    for k, (ref, scratch) in enumerate(pairs):
        copies.append(pltpu.make_async_copy(ref, scratch, sems.at[first + k]))
        copies[-1].start()
    return copies


def start_in(pos, refs, scratch, sems, first=0):
    return start_loads([(ref, scratch.at[block_rows(pos, ry), :]) for ref, ry in zip(refs, PIECES)], sems, first)


def start_out(pos, scratch, refs, sems, first=0):
    return start_loads([(scratch.at[block_rows(pos, r), :], refs[r]) for r in range(4)], sems, first)


def wait_all(copies):
    for copy in copies:
        copy.wait()


def small_rows(c_ref):
    return c_ref[:, CHAN:SMALL].astype(F32).T


def scan_chunks(step, carry):
    def four(k, carry):
        for j in range(4):
            carry = step(k * 4 + j, carry)
        return carry

    return lax.fori_loop(0, BLOCK // 4, four, carry)


def chunk_rows(t):
    return pl.ds(t, 8, stride=BLOCK)


def side(ref, lanes):
    rows = ref.shape[0] // 2
    return ref.at[lanes * rows : (lanes + 1) * rows, :]


def get_rows(ref, lo, count):
    return jnp.concatenate([side(ref, k)[lo : lo + count, :] for k in (0, 1)], axis=1)


def put_rows(ref, lo, count, value):
    for k in (0, 1):
        side(ref, k)[lo : lo + count, :] = value[:, 128 * k : 128 * k + 128]


def chain(mult_ref, ahead, add_ref, product_ref, backward):
    def step(t, carry):
        t = BLOCK - 1 - t if backward else t
        out = []
        for k in (0, 1):
            state, product = carry[2 * k : 2 * k + 2]
            mult = side(mult_ref, k)[chunk_rows(t + ahead), :]
            state = mult * state + side(add_ref, k)[chunk_rows(t), :]
            product = product * mult
            side(add_ref, k)[chunk_rows(t), :] = state
            side(product_ref, k)[chunk_rows(t), :] = product
            out += [state, product]
        return tuple(out)

    zero, one = jnp.zeros((8, 128), F32), jnp.ones((8, 128), F32)
    left, left_p, right, right_p = scan_chunks(step, (zero, one, zero, one))
    return jnp.concatenate([left, right], axis=1), jnp.concatenate([left_p, right_p], axis=1)


def gated_cols(gate, up, s):
    lo = HID * s
    return [gate[:, lo : lo + 512], up[:, lo : lo + 512], gate[:, lo + 512 : lo + HID], up[:, lo + 512 : lo + HID]]


def pack_cols_kernel(pos, gain_one, gain_two, x_ref, y_ref, gate_ref, up_ref, *refs):
    outs, blocks_s = refs[:8], refs[8]
    gain = column(gain_one)
    x, y = x_ref[...].astype(F32) * gain, y_ref[...].astype(F32) * gain
    gain = column(gain_two)
    gate, up = gate_ref[...].astype(F32) * gain, up_ref[...].astype(F32) * gain
    fill = jnp.zeros((4, SENT), F32)
    for s in range(8):
        cols = slice(CHAN * s, CHAN * s + CHAN)
        block = jnp.concatenate([x[:, cols], y[:, cols], *gated_cols(gate, up, s)], axis=1)
        blocks_s[s] = jnp.concatenate([block, fill])
    for k, (ry, rc) in enumerate(PLACES):
        outs[k][...] = blocks_s[place_of(pos, ry, rc)].astype(BF)


def pack_rows_kernel(out_ref, gate_w_ref, taps_ref, bias_ref, gate_bias_ref, decay_ref, rest_ref):
    rest_ref[:, 0:WIDTH] = out_ref[...]
    rest_ref[:, 1536:1792] = gate_w_ref[...]
    lane = lax.broadcasted_iota(jnp.int32, (16, 128), 1)
    small = jnp.zeros((16, 128), F32)
    for k in range(4):
        small = jnp.where(lane == k, column(taps_ref.at[k : k + 1, :]), small)
    small = jnp.where(lane == 4, column(bias_ref), small)
    for k in range(2):
        small = jnp.where(lane == 5 + k, column(gate_bias_ref.at[k : k + 1, :]), small)
    rest_ref[:, 1792:1920] = jnp.where(lane == 7, column(decay_ref), small).astype(BF)


def shard_kernel(pos, *refs):
    blocks, (rest_ref, early_ref, late_ref, blocks_s, wide_s) = refs[:8], refs[8:]
    for k, (ry, rc) in enumerate(PLACES):
        blocks_s[place_of(pos, 4 - ry, rc)] = blocks[k][...].astype(F32)
    for s in range(8):
        wide_s[12 * s : 12 * s + 12, :] = blocks_s[s, 0:12, :]
    for t in range(2):
        early_ref[96 * t : 96 * t + 96, :] = wide_s[:, 128 * t : 128 * t + 128].astype(BF)
        late_ref[96 * t : 96 * t + 96, :] = wide_s[:, CHAN + 128 * t : CHAN + 128 * t + 128].astype(BF)
    for t in range(3):
        early_ref[192 + 16 * t : 208 + 16 * t, :] = rest_ref[:, WIDTH + 128 * t : WIDTH + 128 * t + 128]
    for t in range(12):
        late_ref[192 + 16 * t : 208 + 16 * t, :] = rest_ref[:, 128 * t : 128 * t + 128]
    for t in range(9):
        late_ref[COLS + 96 * t : COLS + 96 * t + 96, :] = wide_s[:, 512 + 128 * t : 640 + 128 * t].astype(BF)


def early_unpack_kernel(all_ref, w_ref, c_ref):
    for p in range(16):
        at = EARLY * p
        for t in range(2):
            w_ref[96 * p : 96 * p + 96, 128 * t : 128 * t + 128] = all_ref[at + 96 * t : at + 96 * t + 96, :]
        for t in range(3):
            lo = at + 192 + 16 * t
            c_ref[16 * p : 16 * p + 16, 128 * t : 128 * t + 128] = all_ref[lo : lo + 16, :]


def late_unpack_kernel(all_ref, w_ref, o_ref, late_s, copy_sems):
    slots = [late_s.at[COLS * p : COLS * p + COLS, :] for p in range(16)]
    loads = start_loads([(all_ref.at[LATE * p : LATE * p + COLS, :], slots[p]) for p in range(16)], copy_sems, 0)
    for p in range(16):
        loads[p].wait()
        at = COLS * p
        for t in range(2):
            w_ref[96 * p : 96 * p + 96, 128 * t : 128 * t + 128] = late_s[at + 96 * t : at + 96 * t + 96, :]
        for t in range(12):
            lo = at + 192 + 16 * t
            o_ref[16 * p : 16 * p + 16, 128 * t : 128 * t + 128] = late_s[lo : lo + 16, :]


def cols_unpack_kernel(all_ref, w_ref, cols_s, copy_sems):
    slots = [cols_s.at[864 * p : 864 * p + 864, :] for p in range(16)]
    ends = [(all_ref.at[LATE * p + COLS : LATE * p + LATE, :], slots[p]) for p in range(16)]
    loads = start_loads(ends, copy_sems, 0)
    for p in range(16):
        loads[p].wait()
        for t in range(9):
            at = 864 * p + 96 * t
            w_ref[96 * p : 96 * p + 96, 128 * t : 128 * t + 128] = cols_s[at : at + 96, :]


def down_pack_kernel(down_ref, out_ref):
    down = jnp.concatenate([down_ref[...].astype(F32), jnp.zeros((12, WIDTH), F32)]).astype(BF)
    for j in range(4):
        out_ref[48 * j : 48 * j + 48, :] = down[:, 384 * j : 384 * j + 384]


def down_unpack_kernel(all_ref, d_ref, wide_s):
    for p in range(16):
        for j in range(4):
            at = p * DOWN_ROWS + 48 * j
            wide_s[36 * p : 36 * p + 36, 384 * j : 384 * j + 384] = all_ref[at : at + 48, :].astype(F32)[:36]
    d_ref[0:HID, :] = wide_s[...].astype(BF)
    d_ref[HID:, :] = jnp.zeros((HID_PAD - HID, WIDTH), BF)


def in_proj_kernel(pos, *refs):
    x_refs, w_mine, w_theirs = refs[:4], refs[4], refs[5]
    xl_mine, xl_theirs, x_s, rs_ref, copy_sems = refs[6:]
    wait_all(start_in(pos, x_refs, x_s, copy_sems))
    for k in range(ROWS // STEP):
        rows = slice(k * STEP, k * STEP + STEP)
        here = x_s[rows, :]
        wide = here.astype(F32)
        scale = lax.rsqrt(jnp.mean(wide * wide, axis=-1, keepdims=True) + EPS)
        rs_ref[rows, :] = jnp.broadcast_to(scale, (STEP, 128))
        xl_theirs[rows, :] = (nn(here, w_theirs[...]) * scale).astype(BF)
        xl_mine[rows, :] = (nn(here, w_mine[...]) * scale).astype(BF)


def y_proj_kernel(x_ref, rs_ref, w_mine, w_theirs, yp_ref):
    for k in range(ROWS // STEP):
        rows = slice(k * STEP, k * STEP + STEP)
        scale = rs_ref[rows, 0:1]
        yp_ref[rows, :CHAN] = nn(x_ref[rows, :], w_mine[...]) * scale
        yp_ref[rows, CHAN:] = nn(x_ref[rows, :], w_theirs[...]) * scale


def saved_parts(ref):
    return [ref.at[(TOKENS + 8) * k : (TOKENS + 8) * (k + 1), :] for k in range(4)]


def recurrence_kernel(pos, mine_ref, theirs_ref, c_ref, edge_ref, *refs):
    hid_mine, hid_theirs, saved_out, saved_ref, a_s, push_s, cum_s, copy_sems = refs
    xl_s, rg_s, op_s, hid_s = saved_parts(saved_ref)
    parts = list(zip((xl_s, rg_s, op_s, hid_s), saved_parts(saved_out)))
    xl_s[0:8, :] = edge_ref[0:8, :]
    hid_s[0:8, :] = edge_ref[8:16, :]
    for y in range(4):
        for rc, ref in enumerate((mine_ref, theirs_ref)):
            at = pl.multiple_of(8 + time_start(pos, y, rc), 8)
            xl_s[pl.ds(at, BLOCK), :] = ref[BLOCK * y : BLOCK * y + BLOCK, :].astype(F32)
    small = small_rows(c_ref)
    gate_w = c_ref[:, 0:CHAN]
    decay_scale = -8.0 * softplus(small[7:8, :])
    for k in range(TOKENS // STEP):
        lo = k * STEP
        conv = small[4:5, :]
        for tap in range(4):
            conv = conv + small[tap : tap + 1, :] * xl_s[lo + 8 - tap : lo + 8 - tap + STEP, :]
        conv = conv.astype(BF)
        raw = [nn(conv[:, 128 * h : 128 * h + 128], gate_w[128 * h : 128 * h + 128, :]) for h in (0, 1)]
        rg = jax.nn.sigmoid(jnp.concatenate([raw[0][:, :128], raw[1][:, :128]], axis=1) + small[5:6, :])
        op = jax.nn.sigmoid(jnp.concatenate([raw[0][:, 128:], raw[1][:, 128:]], axis=1) + small[6:7, :])
        log_a = decay_scale * rg
        put_rows(a_s, lo, STEP, jnp.exp(log_a))
        put_rows(push_s, lo, STEP, jnp.sqrt(neg_expm1(2.0 * log_a)) * op * conv.astype(F32))
        rg_s[lo : lo + STEP, :] = rg
        op_s[lo : lo + STEP, :] = op
    saves = start_loads(parts[:3], copy_sems, 0)
    state, product = chain(a_s, 0, push_s, cum_s, False)
    entering = edge_ref[15:16, :]
    for k in range(8):
        lo = k * BLOCK
        hidden = get_rows(push_s, lo, BLOCK) + get_rows(cum_s, lo, BLOCK) * entering
        entering = state[k : k + 1, :] + product[k : k + 1, :] * entering
        hid_s[8 + lo : 8 + lo + BLOCK, :] = hidden
    saves += start_loads(parts[3:], copy_sems, 3)
    for y in range(4):
        for rc, ref in enumerate((hid_mine, hid_theirs)):
            at = pl.multiple_of(8 + time_start(pos, y, rc), 8)
            ref[BLOCK * y : BLOCK * y + BLOCK, :] = hid_s[pl.ds(at, BLOCK), :].astype(BF)
    wait_all(saves)


def out_proj_kernel(pos, hid_mine, hid_theirs, yp_ref, o_mine, o_theirs, *refs):
    outs, mix_ref, part_s, sems = refs[:4], refs[4], refs[5], refs[6]
    for k in range(ROWS // STEP):
        rows = slice(k * STEP, k * STEP + STEP)
        act, _ = gelu_parts(yp_ref[rows, :])
        hidden = jnp.concatenate([hid_mine[rows, :], hid_theirs[rows, :]], axis=1)
        mixed = (hidden.astype(F32) * act).astype(BF)
        mix_ref[rows, :] = mixed
        part = nn(mixed[:, :CHAN], o_mine[...]) + nn(mixed[:, CHAN:], o_theirs[...])
        part_s[rows, :] = part.astype(BF)
    wait_all(start_out(pos, part_s, outs, sems))


def mlp_pre_kernel(pos, *refs):
    x_refs, c_refs, w_ref, far_ref, (xc_ref, *pres), (near_ref, copy_sems) = refs[:4], refs[4:8], *refs[8:10], refs[10:13], refs[13:]
    loads = start_in(pos, x_refs, xc_ref.at[:ROWS, :], copy_sems)
    other = start_loads(((far_ref, near_ref),), copy_sems, 8)
    later = start_in(pos, c_refs, xc_ref.at[ROWS:, :], copy_sems, 4)
    wait_all(loads)
    for weights, pre_ref in zip((w_ref, near_ref), pres):
        if weights is near_ref:
            wait_all(other)
        for k in range(ROWS // STEP):
            rows = slice(k * STEP, k * STEP + STEP)
            pre_ref[rows, :] = nn(xc_ref[rows, :], weights[...])
    wait_all(later)


def mlp_kernel(pos, xc_ref, *refs):
    pres, (w_ref, d_ref, far_ref, d_theirs), outs, saves = refs[:2], refs[2:6], refs[6:10], refs[10:12]
    part_s, near_ref, copy_sems = refs[12:]
    weights = ((w_ref, d_ref), (near_ref, d_theirs))
    loads = start_loads(((far_ref, near_ref),), copy_sems, 4)

    @pl.loop(0, ROWS // STEP)
    def _(k):
        rows = pl.ds(pl.multiple_of(k * STEP, STEP), STEP)
        cot = xc_ref[pl.ds(pl.multiple_of(ROWS + k * STEP, STEP), STEP), :]
        part = None
        for (w_ref, d_ref), pre_ref, save_ref in zip(weights, pres, saves):
            d_product = nt(cot, d_ref[...])
            last = pre_ref[rows, 1024:1152]
            gate = jnp.concatenate([pre_ref[rows, :512], last], axis=1)
            up = jnp.concatenate([pre_ref[rows, 512:1024], pltpu.roll(last, 64, 1)], axis=1)
            act, slope = gelu_parts(gate)
            save_ref[rows, :HID_PAD] = (act * up).astype(BF)
            d_gate = d_product * up * slope
            d_up = d_product * act
            d_last = d_gate[:, 512:] + pltpu.roll(d_up[:, 512:], 64, 1)
            d_pre = jnp.concatenate([d_gate[:, :512], d_up[:, :512], d_last], axis=1).astype(BF)
            save_ref[rows, HID_PAD:] = d_pre
            if w_ref is near_ref:

                @pl.when(k == 0)
                def _():
                    wait_all(loads)

            term = nt(d_pre, w_ref[...])
            part = term if part is None else part + term
        part_s[rows, :] = part.astype(BF)

    wait_all(start_out(pos, part_s, outs, copy_sems))


def mlp_out_kernel(pos, prod_mine, prod_theirs, d_mine, d_theirs, *refs):
    outs, part_s, copy_sems = refs[:4], refs[4], refs[5]
    for k in range(ROWS // STEP):
        rows = slice(k * STEP, k * STEP + STEP)
        part = nn(prod_mine[rows, :HID_PAD], d_mine[...]) + nn(prod_theirs[rows, :HID_PAD], d_theirs[...])
        part_s[rows, :] = part.astype(BF)
    wait_all(start_out(pos, part_s, outs, copy_sems))


def mlp_grads_kernel(*refs):
    xc_refs, save_refs, (out_ref, out_s, w_s, d_s, copy_sems) = refs[:2], refs[2:4], refs[4:]
    for k in range(HID_PAD // 128):
        cols = slice(128 * k, 128 * k + 128)
        grads = [tn(save[:, cols], xc[ROWS:, :]) for xc, save in zip(xc_refs, save_refs)]
        d_s[cols, :] = grads[0] + grads[1]
    saves = []
    for k in range(WIDTH // 384):
        cols = slice(384 * k, 384 * k + 384)
        grads = [tn(xc[:ROWS, cols], save[:, HID_PAD:]) for xc, save in zip(xc_refs, save_refs)]
        w_s[cols, :] = (grads[0] + grads[1]).astype(BF)
        for p in range(4 * k, 4 * k + 4):
            for j in range(3):
                at = p * MLP_ROWS + 96 * j
                out_s[at : at + 96, :] = w_s[96 * p : 96 * p + 96, 384 * j : 384 * j + 384]
            for j in range(4):
                at = p * MLP_ROWS + 288 + 48 * j
                out_s[at : at + 48, :] = d_s[36 * p : 36 * p + 48, 384 * j : 384 * j + 384].astype(BF)
        part = slice(4 * MLP_ROWS * k, 4 * MLP_ROWS * (k + 1))
        saves += start_loads(((out_s.at[part, :], out_ref.at[part, :]),), copy_sems, k)
    wait_all(saves)


def mixed_backward_kernel(pos, *refs):
    d_refs, (o_mine, o_theirs, yp_ref, hid_mine, hid_theirs, rs_ref) = refs[:4], refs[4:10]
    mine_ref, theirs_ref, d_s, o_s, copy_sems = refs[10:]
    o_near = (o_s.at[:CHAN, :], o_s.at[CHAN:, :])
    loads = start_loads(list(zip((o_mine, o_theirs), o_near)), copy_sems, 4)
    wait_all(start_in(pos, d_refs, d_s, copy_sems) + loads)
    sides = ((o_near[0], hid_mine, mine_ref), (o_near[1], hid_theirs, theirs_ref))
    for k in range(ROWS // STEP):
        rows = slice(k * STEP, k * STEP + STEP)
        here = d_s[rows, :]
        scale = rs_ref[rows, 0:1]
        for h, (o_ref, hid_ref, out_ref) in enumerate(sides):
            d_mixed = nt(here, o_ref[...])
            act, slope = gelu_parts(yp_ref[rows, CHAN * h : CHAN * h + CHAN])
            out_ref[rows, :CHAN] = (d_mixed * act).astype(BF)
            out_ref[rows, CHAN:] = (d_mixed * hid_ref[rows, :].astype(F32) * slope * scale).astype(BF)


def out_grads_kernel(mix_ref, d_ref, mine_ref, theirs_ref):
    theirs_ref[...] = tn(mix_ref[:, CHAN:], d_ref[...]).astype(BF)
    mine_ref[...] = tn(mix_ref[:, :CHAN], d_ref[...]).astype(BF)


def chain_backward_kernel(pos, *refs):
    (mine_ref, theirs_ref, c_ref, saved_ref) = refs[:4]
    dx_mine, dx_theirs, gs_ref, dh_s, cum_s, dc_s, dx_s, acc_s, a_ref, saved_s, copy_sems = refs[4:]
    xl_ref, rg_ref, op_ref, hid_ref = saved_parts(saved_s)
    order = (1, 0, 2, 3)
    loads = [(saved_parts(saved_ref)[k], saved_parts(saved_s)[k]) for k in order]
    loads = start_loads(loads, copy_sems, 0)
    small = small_rows(c_ref)
    gate_w = c_ref[:, 0:CHAN]
    decay = small[7:8, :]
    decay_scale = -8.0 * softplus(decay)
    for y in range(4):
        for rc, ref in enumerate((mine_ref, theirs_ref)):
            block = ref[BLOCK * y : BLOCK * y + BLOCK, :CHAN].astype(F32)
            at = pl.multiple_of(time_start(pos, y, rc), BLOCK)
            for k in (0, 1):
                side(dh_s, k)[pl.ds(at, BLOCK), :] = block[:, 128 * k : 128 * k + 128]
    loads[0].wait()
    for k in range(TOKENS // STEP):
        put_rows(a_ref, k * STEP, STEP, jnp.exp(decay_scale * rg_ref[k * STEP : k * STEP + STEP, :]))
    put_rows(a_ref, TOKENS, 8, jnp.zeros((8, CHAN), F32))
    state, product = chain(a_ref, 1, dh_s, cum_s, True)
    wait_all(loads[1:])
    decay_slope = -8.0 * jax.nn.sigmoid(decay)
    acc_s[...] = jnp.zeros_like(acc_s)
    dc_s[TOKENS:, :] = jnp.zeros((8, CHAN), F32)
    later = [None] * 8
    entering = jnp.zeros((1, CHAN), F32)
    for k in reversed(range(8)):
        later[k] = entering
        entering = state[k : k + 1, :] + product[k : k + 1, :] * entering
    gate_grads = [jnp.zeros((128, CHAN), F32) for _ in (0, 1)]
    for k in range(8):
        lo = k * BLOCK
        rows = slice(lo, lo + BLOCK)
        state_grad = get_rows(dh_s, lo, BLOCK) + get_rows(cum_s, lo, BLOCK) * later[k]
        shifted = [xl_ref[lo + 8 - tap : lo + 8 - tap + BLOCK, :] for tap in range(4)]
        conv = small[4:5, :]
        for tap in range(4):
            conv = conv + small[tap : tap + 1, :] * shifted[tap]
        conv_low = conv.astype(BF)
        conv = conv_low.astype(F32)
        rg, op, a = rg_ref[rows, :], op_ref[rows, :], get_rows(a_ref, lo, BLOCK)
        root = jnp.sqrt(neg_expm1(2.0 * decay_scale * rg))
        pushed = state_grad * op
        d_log = a * (state_grad * hid_ref[lo + 7 : lo + 7 + BLOCK, :] - pushed * conv * a / root)
        d_rg = d_log * rg
        acc_s[7:8, :] += jnp.sum(d_rg, axis=0, keepdims=True) * decay_slope
        d_raw = decay_scale * d_rg * (1.0 - rg)
        d_open = pushed * root * conv * (1.0 - op)
        acc_s[5:6, :] += jnp.sum(d_raw, axis=0, keepdims=True)
        acc_s[6:7, :] += jnp.sum(d_open, axis=0, keepdims=True)
        d_raw, d_open = d_raw.astype(BF), d_open.astype(BF)
        back = []
        for h in (0, 1):
            cols = slice(128 * h, 128 * h + 128)
            d_block = jnp.concatenate([d_raw[:, cols], d_open[:, cols]], axis=1)
            gate_grads[h] = gate_grads[h] + tn(conv_low[:, cols], d_block)
            back.append(nt(d_block, gate_w[cols, :]))
        d_conv = pushed * root + jnp.concatenate(back, axis=1)
        dc_s[rows, :] = d_conv
        acc_s[4:5, :] += jnp.sum(d_conv, axis=0, keepdims=True)
        for tap in range(4):
            acc_s[tap : tap + 1, :] += jnp.sum(d_conv * shifted[tap], axis=0, keepdims=True)
    for k in range(8):
        lo = k * BLOCK
        d_x = small[0:1, :] * dc_s[lo : lo + BLOCK, :]
        for tap in range(1, 4):
            d_x = d_x + small[tap : tap + 1, :] * dc_s[lo + tap : lo + tap + BLOCK, :]
        dx_s[lo : lo + BLOCK, :] = d_x
    for y in range(4):
        for rc, ref in enumerate((dx_mine, dx_theirs)):
            at = pl.multiple_of(time_start(pos, y, rc), BLOCK)
            ref[BLOCK * y : BLOCK * y + BLOCK, :] = dx_s[pl.ds(at, BLOCK), :].astype(BF)
    for h in (0, 1):
        gs_ref[128 * h : 128 * h + 128, 0:256] = gate_grads[h].astype(BF)
    gs_ref[:, 256:384] = acc_s[...].T.astype(BF)


def normed_backward_kernel(pos, dx_mine, dx_theirs, dy_mine, dy_theirs, rs_ref, *refs):
    weights, outs, part_s, copy_sems = refs[:4], refs[4:8], refs[8], refs[9]
    for k in range(ROWS // STEP):
        rows = slice(k * STEP, k * STEP + STEP)
        scale = rs_ref[rows, 0:1]
        lows = [(dx_ref[rows, :].astype(F32) * scale).astype(BF) for dx_ref in (dx_mine, dx_theirs)]
        lows += [dy_mine[rows, CHAN:], dy_theirs[rows, CHAN:]]
        part_s[rows, :] = sum(nt(low, w_ref[...]) for low, w_ref in zip(lows, weights)).astype(BF)
    wait_all(start_out(pos, part_s, outs, copy_sems))


def cols_grads_kernel(*refs):
    x_refs, dx_refs, dy_refs, rs_ref = refs[:2], refs[2:4], refs[4:6], refs[6]
    go_mine, go_theirs, gs_ref, out_ref, out_s, wide_s, rest_s, copy_sems = refs[7:]
    rest_s[:, 0:WIDTH] = (go_mine[...].astype(F32) + go_theirs[...].astype(F32)).astype(BF)
    rest_s[:, WIDTH:C_WIDTH] = gs_ref[...]
    rest_s[:, C_WIDTH:] = jnp.zeros((CHAN, 8 * REST - C_WIDTH), BF)
    wide = x_refs[1][...].astype(F32)
    scales = (rs_ref[:, 0:1], lax.rsqrt(jnp.mean(wide * wide, axis=-1, keepdims=True) + EPS))
    lows = [
        jnp.concatenate([(dx[...].astype(F32) * scale).astype(BF), dy[:, CHAN:]], axis=1)
        for dx, dy, scale in zip(dx_refs, dy_refs, scales)
    ]
    saves = []
    for k in range(WIDTH // 384):
        rows = slice(384 * k, 384 * k + 384)
        wide_s[rows, :] = tn(x_refs[0][:, rows], lows[0]) + tn(x_refs[1][:, rows], lows[1])
        for i in range(32 * k, 32 * k + 32):
            block = [wide_s[12 * i : 12 * i + 12, 128 * t : 128 * t + 128] for t in range(4)]
            out_s[i, 0:COLS_ROWS, :] = jnp.concatenate(block).astype(BF)
            few = slice(16 * (i // 8), 16 * (i // 8) + 16)
            for t in range(2):
                at = REST * (i % 8) + 128 * t
                out_s[i, COLS_ROWS + 16 * t : COLS_ROWS + 16 * t + 16, :] = rest_s[few, at : at + 128]
        part = slice(32 * k, 32 * k + 32)
        saves += start_loads(((out_s.at[part], out_ref.at[part]),), copy_sems, k)
    wait_all(saves)


def add_terms(terms):
    out = terms[0][...].astype(F32)
    for term in terms[1:]:
        out = out + term[...].astype(F32)
    return out


def residual_kernel(x_ref, *refs):
    terms, (res_out, scale_out, low_ref, res_s, scale_s, copy_sems) = refs[:4], refs[4:]
    residual = x_ref[...].astype(F32) + add_terms(terms)
    scale = lax.rsqrt(jnp.mean(residual * residual, axis=-1, keepdims=True) + EPS)
    res_s[...] = residual
    scale_s[...] = jnp.broadcast_to(scale, (BLOCK, 128))
    saves = start_loads(((res_s, res_out), (scale_s, scale_out)), copy_sems, 0)
    low_ref[...] = (residual * scale).astype(BF)
    wait_all(saves)


def d_residual_kernel(cot_ref, res_ref, scale_ref, *refs):
    terms, (d_out, low_ref, d_s, cot_s, copy_sems) = refs[:4], refs[4:]
    loads = start_loads(((cot_ref, cot_s),), copy_sems, 1)
    d_normed = add_terms(terms)
    scale = scale_ref[:, 0:1]
    normed = res_ref[...] * scale
    along = jnp.mean(normed * d_normed, axis=-1, keepdims=True)
    wait_all(loads)
    d_residual = cot_s[...].astype(F32) + scale * (d_normed - normed * along)
    d_s[...] = d_residual
    saves = start_loads(((d_s, d_out),), copy_sems, 0)
    low_ref[...] = d_residual.astype(BF)
    wait_all(saves)


def input_grad_kernel(x_ref, d_ref, *refs):
    terms, (out_ref, near_s, d_s, copy_sems) = refs[:4], refs[4:]
    slots = [near_s.at[BLOCK * k : BLOCK * k + BLOCK, :] for k in range(5)]
    loads = start_loads([*zip((*terms, x_ref), slots), (d_ref, d_s)], copy_sems, 0)
    wait_all(loads)
    scaled = add_terms(slots[:4])
    x = slots[4][...].astype(F32)
    power = 1.0 / (jnp.mean(x * x, axis=-1, keepdims=True) + EPS)
    along = jnp.mean(x * scaled, axis=-1, keepdims=True) * power
    out_ref[...] = (d_s[...] + scaled - x * along).astype(BF)


def layer_out_kernel(res_ref, *refs):
    terms, out_ref = refs[:4], refs[4]
    out_ref[...] = (res_ref[...] + add_terms(terms)).astype(BF)


def dp_total(got_ref, lo, count):
    out = got_ref[0, lo : lo + count, :].astype(F32)
    for k in range(1, 16):
        out = out + got_ref[k, lo : lo + count, :].astype(F32)
    return out


def finish_cols_kernel(got_ref, gain_ref, x_ref, y_ref, gx_ref, gy_ref, gain_grad_ref, wide_s):
    for s in range(8):
        wide_s[COLS_ROWS * s : COLS_ROWS * s + COLS_ROWS, :] = dp_total(got_ref, SUM_ROWS * s, COLS_ROWS)
    gain = column(gain_ref)
    along = jnp.zeros((12, 128), F32)
    for s in range(8):
        for t in range(4):
            at = CHAN * s + 128 * (t % 2)
            lo = COLS_ROWS * s + 12 * t
            grad = wide_s[lo : lo + 12, :]
            w_ref, g_ref = (x_ref, gx_ref) if t < 2 else (y_ref, gy_ref)
            along = along + grad * w_ref[:, at : at + 128].astype(F32)
            g_ref[:, at : at + 128] = grad * gain
    gain_grad_ref[...] = as_row(jnp.sum(along, axis=1, keepdims=True))


def mlp_back_kernel(got_ref, cols_ref, down_ref, wide_s):
    for j in range(3):
        wide_s[:, 384 * j : 384 * j + 384] = got_ref[96 * j : 96 * j + 96, :].astype(F32)
    for s in range(8):
        block = jnp.concatenate([wide_s[12 * s : 12 * s + 12, :], jnp.zeros((4, GATED), F32)])
        cols_ref[s] = block.astype(BF)
    for j in range(4):
        down_ref[:, 384 * j : 384 * j + 384] = got_ref[288 + 48 * j : 336 + 48 * j, :]


def rest_back_kernel(cols_ref, got_ref, out_ref):
    out_ref[:, :, :GATED] = cols_ref[...]
    for s in range(8):
        for t in range(2):
            tile = dp_total(got_ref, SUM_ROWS * s + COLS_ROWS + 16 * t, 16)
            out_ref[s, :, GATED + 128 * t : GATED + 128 * t + 128] = tile.astype(BF)


def mlp_finish_kernel(*refs):
    got_ref, gain_ref, gate_ref, up_ref, g_gate_ref, g_up_ref, gain_grad_ref = refs
    gain = column(gain_ref)
    along = jnp.zeros((12, 1), F32)
    for s in range(8):
        block = got_ref[s, :, :GATED].astype(F32)[:12]
        lo = HID * s
        cols = slice(lo, lo + HID)
        grad_gate = jnp.concatenate([block[:, :512], block[:, 1024:1088]], axis=1)
        grad_up = jnp.concatenate([block[:, 512:1024], block[:, 1088:]], axis=1)
        terms = grad_gate * gate_ref[:, cols].astype(F32) + grad_up * up_ref[:, cols].astype(F32)
        along = along + jnp.sum(terms, axis=1, keepdims=True)
        g_gate_ref[:, cols] = grad_gate * gain
        g_up_ref[:, cols] = grad_up * gain
    gain_grad_ref[...] = as_row(along)


def rest_join_kernel(got_ref, down_ref, out_ref):
    for s in range(8):
        out_ref[:, REST * s : REST * s + REST] = got_ref[s, :, GATED:]
    for j in range(3):
        out_ref[:, 8 * REST + WIDTH * j : 8 * REST + WIDTH * j + WIDTH] = down_ref[16 * j : 16 * j + 16, :]


def finish_rest_kernel(got_ref, out_ref, gate_w_ref, taps_ref, bias_ref, gate_bias_ref, decay_ref, down_ref):
    for j in range(3):
        rows = min(16, 36 - 16 * j)
        tile = got_ref[:, 8 * REST + WIDTH * j : 8 * REST + WIDTH * j + WIDTH]
        down_ref[16 * j : 16 * j + rows, :] = tile.astype(F32)[:rows]
    out_ref[...] = got_ref[:, 0:WIDTH].astype(F32)
    gate_w_ref[...] = got_ref[:, 1536:1792].astype(F32)
    small = got_ref[:, 1792:1920].astype(F32)
    rows = [as_row(small[:, k : k + 1]) for k in range(8)]
    for k in range(4):
        taps_ref[k : k + 1, :] = rows[k]
    bias_ref[...] = rows[4]
    for k in range(2):
        gate_bias_ref[k : k + 1, :] = rows[5 + k]
    decay_ref[...] = rows[7]


def shape(dims, dtype):
    return jax.ShapeDtypeStruct(dims, dtype)


def sems(count):
    return pltpu.SemaphoreType.DMA((count,))


def size(dims, dtype):
    return math.prod(dims) * jnp.dtype(dtype).itemsize


def call(kernel, args, outs, scratch=(), any_args=(), any_outs=(), far_outs=(), micros=0, more=8):
    held = sum(size(a.shape, a.dtype) for k, a in enumerate(args) if k not in any_args)
    held += sum(size(*o) for k, o in enumerate(outs) if k not in any_outs)
    held += sum(size(s.shape, s.dtype) for s in scratch if s.memory_space == pltpu.VMEM)
    args = [pltpu.with_memory_space_constraint(a, pltpu.HBM) if k in any_args else a for k, a in enumerate(args)]
    in_specs = [SMEM if a.dtype == jnp.int32 else HBM if k in any_args else VMEM for k, a in enumerate(args)]
    return pl.pallas_call(
        kernel,
        name=kernel.__name__.removesuffix("_kernel"),
        in_specs=in_specs,
        out_specs=[ANY if k in any_outs else VMEM for k in range(len(outs))],
        out_shape=[pltpu.HBM(*o) if k in far_outs else shape(*o) for k, o in enumerate(outs)],
        scratch_shapes=scratch,
        cost_estimate=pl.CostEstimate(flops=int(micros * 10**9), bytes_accessed=0, transcendentals=0),
        compiler_params=pltpu.CompilerParams(vmem_limit_bytes=min(held + (more << 20), 60 << 20)),
    )(*args)


PART = ((BLOCK, WIDTH), BF)
PARTS = [PART] * 4
PART_S = pltpu.VMEM((ROWS, WIDTH), BF)
CHAIN_S = pltpu.VMEM((2 * TOKENS, 128), F32)


def per_device(
    inputs,
    cotangent,
    resets,
    start_state,
    conv_history,
    norm_gain,
    proj_x,
    proj_y,
    conv_taps,
    conv_bias,
    gate_weight,
    gate_bias,
    decay_param,
    proj_out,
    mlp_gain,
    mlp_gate,
    mlp_up,
    mlp_down,
):
    pos = jnp.stack([lax.axis_index(a) for a in DP_SEQ]).astype(jnp.int32)
    flat_in = inputs[0]
    flat_cot = cotangent[0]
    gain_one = norm_gain[None]
    gain_two = mlp_gain[None]

    (rest,) = call(
        pack_rows_kernel,
        (proj_out, gate_weight, conv_taps.T, conv_bias[None], gate_bias.T, decay_param[None]),
        [((16, C_WIDTH), BF)],
        more=60,
    )
    rest, late_x, late_down = tied(rest, proj_x, mlp_down)
    rest = transposed_devices(rest, False)
    blocks = call(
        pack_cols_kernel,
        (pos, gain_one, gain_two, late_x, proj_y, mlp_gate, mlp_up),
        [((16, SENT), BF)] * 8,
        [pltpu.VMEM((8, 16, SENT), F32)],
        more=60,
    )
    early, late = call(
        shard_kernel,
        (pos, *exchanged(blocks), rest),
        [((EARLY, 128), BF), ((LATE, 128), BF)],
        [pltpu.VMEM((8, 16, SENT), F32), pltpu.VMEM((96, SENT), F32)],
    )
    late = lax.all_gather(late, DP, axis=0, tiled=True)
    early, early_in, late_down = tied(early, flat_in, late_down)
    x_pieces = gather_rows(early_in)
    down = transposed_devices(late_down, False)
    early = lax.all_gather(early, DP, axis=0, tiled=True)
    early, x_pieces, down = tied(early, x_pieces, down)
    x_mine, c_mine = call(early_unpack_kernel, (early,), [((WIDTH, CHAN), BF), ((CHAN, SMALL), BF)])
    (down,) = call(down_pack_kernel, (down,), [((DOWN_ROWS, MLP_LANES), BF)])
    x_mine, late_cot, down = tied(x_mine, flat_cot, down)
    down = lax.all_gather(down, DP, axis=0, tiled=True)
    x_theirs = swapped(x_mine)
    c_near = [hop(late_cot, "y", r) for r in PIECES[1:3]]

    keep = (1 - resets).astype(F32)
    place = lax.axis_index(SEQ) * CHAN
    history = lax.dynamic_slice(conv_history[0].astype(F32), (0, place), (3, CHAN)) * keep
    initial = lax.dynamic_slice(start_state, (0, place), (1, CHAN)) * keep
    edges = jnp.concatenate([jnp.zeros((5, CHAN), F32), history, jnp.zeros((7, CHAN), F32), initial])
    xl_mine, xl_theirs, x_all, rs = call(
        in_proj_kernel,
        (pos, *x_pieces, x_mine, x_theirs),
        [((ROWS, CHAN), BF)] * 2 + [((ROWS, WIDTH), BF), ((ROWS, 128), F32)],
        [sems(4)],
        any_args=range(1, 5),
        micros=8,
    )
    xl_got, c_near, late_cot = tied(swapped(xl_theirs), c_near, late_cot)
    c_far = hop(late_cot, "y", PIECES[3])
    hid_mine, hid_theirs, saved = call(
        recurrence_kernel,
        (pos, xl_mine, xl_got, c_mine, edges),
        [((ROWS, CHAN), BF)] * 2 + [((4 * (TOKENS + 8), CHAN), F32)],
        [pltpu.VMEM((4 * (TOKENS + 8), CHAN), F32), CHAIN_S, CHAIN_S, CHAIN_S, sems(4)],
        any_outs=[2],
        far_outs=[2],
        micros=8,
    )
    hid_theirs = swapped(hid_theirs)
    hid_mine, c_far, late = tied(hid_mine, c_far, late)
    c_pieces = [flat_cot, *c_near, c_far]
    y_mine, o_mine = call(
        late_unpack_kernel,
        (late,),
        [((WIDTH, CHAN), BF), ((CHAN, WIDTH), BF)],
        [pltpu.VMEM((16 * COLS, 128), BF), sems(16)],
        any_args=range(1),
    )
    y_theirs, o_theirs = swapped(y_mine), swapped(o_mine)
    (yp,) = call(y_proj_kernel, (x_all, rs, y_mine, y_theirs), [((ROWS, 2 * CHAN), F32)], micros=8)
    *parts, mix = call(
        out_proj_kernel,
        (pos, hid_mine, hid_theirs, yp, o_mine, o_theirs),
        PARTS + [((ROWS, 2 * CHAN), BF)],
        [PART_S, sems(4)],
        any_outs=range(4),
        micros=1.2,
    )
    terms = scatter_rows(parts)
    _, late = tied(parts, late)
    (w_up,) = call(
        cols_unpack_kernel,
        (late,),
        [((WIDTH, GATED), BF)],
        [pltpu.VMEM((16 * 864, 128), BF), sems(16)],
        any_args=range(1),
    )
    up_theirs = swapped(w_up)
    terms, w_up = tied(terms, w_up)
    residual, scale_two, normed_two = call(
        residual_kernel,
        (flat_in, *terms),
        [((BLOCK, WIDTH), F32), ((BLOCK, 128), F32), PART],
        [pltpu.VMEM((BLOCK, WIDTH), F32), pltpu.VMEM((BLOCK, 128), F32), sems(2)],
        any_outs=range(2),
        far_outs=range(2),
        micros=30,
    )

    _, down = tied(normed_two, down)
    (w_down,) = call(down_unpack_kernel, (down,), [((HID_PAD, WIDTH), BF)], [pltpu.VMEM((HID, WIDTH), F32)])
    down_theirs = swapped(w_down)
    tokens, pre_mine, pre_theirs = call(
        mlp_pre_kernel,
        (pos, *gather_rows(normed_two), *c_pieces, w_up, up_theirs),
        [((2 * ROWS, WIDTH), BF)] + [((ROWS, GATED), F32)] * 2,
        [pltpu.VMEM((WIDTH, GATED), BF), sems(9)],
        any_args=(*range(1, 9), 10),
        micros=20,
    )
    tokens_got = swapped(tokens)
    *parts, save_mine, save_theirs = call(
        mlp_kernel,
        (pos, tokens, pre_mine, pre_theirs, w_up, w_down, up_theirs, down_theirs),
        PARTS + [((ROWS, HID_PAD + GATED), BF)] * 2,
        [PART_S, pltpu.VMEM((WIDTH, GATED), BF), sems(5)],
        any_args=[6],
        any_outs=range(4),
        micros=5,
    )
    out_parts = call(
        mlp_out_kernel,
        (pos, save_mine, save_theirs, w_down, down_theirs),
        PARTS,
        [PART_S, sems(4)],
        any_outs=range(4),
        far_outs=range(4),
        micros=15,
    )
    terms = scatter_rows(parts)
    save_got = swapped(save_theirs)
    save_got, out_parts = tied(save_got, out_parts)
    (mlp_grads,) = call(
        mlp_grads_kernel,
        (tokens, tokens_got, save_mine, save_got),
        [((16 * MLP_ROWS, MLP_LANES), BF)],
        [
            pltpu.VMEM((16 * MLP_ROWS, MLP_LANES), BF),
            pltpu.VMEM((WIDTH, GATED), BF),
            pltpu.VMEM((HID_PAD, WIDTH), F32),
            sems(4),
        ],
        any_outs=range(1),
        far_outs=range(1),
        micros=15,
    )
    terms, mlp_grads = tied(terms, mlp_grads)
    mlp_sum = lax.psum_scatter(mlp_grads, DP, scatter_dimension=0, tiled=True)
    d_residual, d_out = call(
        d_residual_kernel,
        (flat_cot, residual, scale_two, *terms),
        [((BLOCK, WIDTH), F32), PART],
        [pltpu.VMEM((BLOCK, WIDTH), F32), pltpu.VMEM((BLOCK, WIDTH), BF), sems(2)],
        any_args=[0],
        any_outs=range(1),
        far_outs=range(1),
    )

    d_out, late_x_all = tied(d_out, x_all)
    d_pieces, all_theirs = tied(gather_rows(d_out), swapped(late_x_all))
    back_mine, back_theirs, d_all = call(
        mixed_backward_kernel,
        (pos, *d_pieces, o_mine, o_theirs, yp, hid_mine, hid_theirs, rs),
        [((ROWS, 2 * CHAN), BF)] * 2 + [((ROWS, WIDTH), BF)],
        [pltpu.VMEM((2 * CHAN, WIDTH), BF), sems(6)],
        any_args=(5, 6),
        micros=2,
    )
    back_got = swapped(back_theirs)
    dx_mine, dx_theirs, g_small = call(
        chain_backward_kernel,
        (pos, back_mine, back_got, c_mine, saved),
        [((ROWS, CHAN), BF)] * 2 + [((CHAN, 384), BF)],
        [
            CHAIN_S,
            CHAIN_S,
            pltpu.VMEM((TOKENS + 8, CHAN), F32),
            pltpu.VMEM((TOKENS, CHAN), F32),
            pltpu.VMEM((128, CHAN), F32),
            pltpu.VMEM((2 * TOKENS + 16, 128), F32),
            pltpu.VMEM((4 * (TOKENS + 8), CHAN), F32),
            sems(4),
        ],
        any_args=[4],
        micros=20,
    )
    dx_got = swapped(dx_theirs)
    parts = call(
        normed_backward_kernel,
        (pos, dx_mine, dx_got, back_mine, back_theirs, rs, x_mine, x_theirs, y_mine, y_theirs),
        PARTS,
        [PART_S, sems(4)],
        any_outs=range(4),
    )
    terms = scatter_rows(parts)
    _, late_mix = tied(parts, mix)
    go_mine, go_theirs = call(out_grads_kernel, (late_mix, d_all), [((CHAN, WIDTH), BF)] * 2)
    (g_cols,) = call(
        cols_grads_kernel,
        (x_all, all_theirs, dx_mine, dx_theirs, back_mine, back_got, rs, go_mine, swapped(go_theirs), g_small),
        [((128, SUM_ROWS, 128), BF)],
        [
            pltpu.VMEM((128, SUM_ROWS, 128), BF),
            pltpu.VMEM((WIDTH, 2 * CHAN), F32),
            pltpu.VMEM((CHAN, 8 * REST), BF),
            sems(4),
        ],
        any_outs=range(1),
        far_outs=range(1),
    )
    g_cols = lax.all_to_all(g_cols, DP_SEQ, 0, 0, tiled=True).reshape(16, 8 * SUM_ROWS, 128)
    terms, mlp_sum = tied(terms, mlp_sum)
    blocks, down_back = call(
        mlp_back_kernel,
        (mlp_sum,),
        [((8, 16, GATED), BF), ((48, WIDTH), BF)],
        [pltpu.VMEM((96, GATED), F32)],
        micros=100,
    )
    (input_grad,) = call(
        input_grad_kernel,
        (flat_in, d_residual, *terms),
        [PART],
        [pltpu.VMEM((5 * BLOCK, WIDTH), BF), pltpu.VMEM((BLOCK, WIDTH), F32), sems(6)],
        any_args=range(6),
    )
    (blocks,) = call(rest_back_kernel, (blocks, g_cols), [((8, 16, GATED + REST), BF)])
    blocks = lax.all_to_all(blocks, SEQ, 0, 0, tiled=True)
    out_parts, _ = tied(out_parts, terms)
    out_terms = scatter_rows(out_parts)
    grad_x, grad_y, grad_norm_gain = call(
        finish_cols_kernel,
        (g_cols, gain_one, proj_x, proj_y),
        [((12, 8 * CHAN), F32)] * 2 + [((1, 12), F32)],
        [pltpu.VMEM((8 * COLS_ROWS, 128), F32)],
    )
    blocks, input_grad = tied(blocks, input_grad)
    (g_rest,) = call(rest_join_kernel, (blocks, down_back), [((16, 8 * REST + 3 * WIDTH), BF)])
    g_rest = transposed_devices(g_rest, True)
    grad_gate, grad_up, grad_mlp_gain = call(
        mlp_finish_kernel,
        (blocks, gain_two, mlp_gate, mlp_up),
        [((12, 8 * HID), F32)] * 2 + [((1, 12), F32)],
    )
    (layer_out,) = call(layer_out_kernel, (residual, *out_terms), [PART])
    g_rest, grad_x, grad_gate, layer_out = tied(g_rest, grad_x, grad_gate, layer_out)
    grad_out, grad_gate_w, grad_taps, grad_conv_bias, grad_gate_bias, grad_decay, grad_down = call(
        finish_rest_kernel,
        (g_rest,),
        [
            ((16, WIDTH), F32),
            ((16, CHAN), F32),
            ((4, 16), F32),
            ((1, 16), F32),
            ((2, 16), F32),
            ((1, 16), F32),
            ((36, WIDTH), F32),
        ],
    )
    return (
        layer_out[None],
        input_grad[None],
        grad_norm_gain[0],
        grad_x,
        grad_y,
        grad_taps.T,
        grad_conv_bias[0],
        grad_gate_w,
        grad_gate_bias.T,
        grad_decay[0],
        grad_out,
        grad_mlp_gain[0],
        grad_gate,
        grad_up,
        grad_down,
    )


def solution(mesh):
    finer = Mesh(mesh.devices.reshape(4, 4, 4, 2), DP_SEQ)
    rows = P(DP_SEQ, None)
    line = P(DP_SEQ)
    tokens = P(DP, SEQ, None)
    in_specs = (
        tokens,
        tokens,
        P(DP),
        P(DP, None),
        P(DP, None, None),
        line,
        rows,
        rows,
        rows,
        line,
        rows,
        rows,
        line,
        rows,
        line,
        rows,
        rows,
        rows,
    )
    out_specs = (
        tokens,
        tokens,
        line,
        rows,
        rows,
        rows,
        line,
        rows,
        rows,
        line,
        rows,
        line,
        rows,
        rows,
        rows,
    )
    return jax.shard_map(per_device, mesh=finer, in_specs=in_specs, out_specs=out_specs, check_vma=False)
```
